128 devices in a mesh: dp: 64 (over z_lo, x, y, core), fsdp: 2 (over z_hi).
Axes of the slice: x: 4, y: 4, z: 4 (z_hi: 2, z_lo: 2; z = z_hi * 2 + z_lo), core: 2. Of those that a mesh axis runs over, the one named last changes fastest.
Arguments:
- tokens: bfloat16 [65536, 1024], P(('dp', 'fsdp')), may hold values from -6 to 6
- norm_gains: bfloat16 [2, 1024], P(None, ('dp', 'fsdp')), may hold values from 0.25 to 1.75
- norm_shifts: bfloat16 [2, 1024], P(None, ('dp', 'fsdp')), may hold values from -1.1953125 to 1.1953125
- query_value_offsets_bias: bfloat16 [2, 1024], P(None, ('dp', 'fsdp')), may hold values from -1.1953125 to 1.1953125
- output_biases: bfloat16 [2, 1024], P(None, ('dp', 'fsdp')), may hold values from -1.1953125 to 1.1953125
- expand_bias: bfloat16 [4096], P(('dp', 'fsdp')), may hold values from -1.1953125 to 1.1953125
- joint_weight: bfloat16 [1024, 3072], P(('dp', 'fsdp')), may hold values from -0.1875 to 0.1875
- output_weight: bfloat16 [1024, 1024], P(('dp', 'fsdp')), may hold values from -0.75 to 0.75
- expand_weight: bfloat16 [1024, 4096], P(('dp', 'fsdp')), may hold values from -0.1875 to 0.1875
- shrink_weight: bfloat16 [4096, 1024], P(('dp', 'fsdp')), may hold values from -0.09375 to 0.09375
- query_down: bfloat16 [1024, 4], replicated, may hold values from -0.1875 to 0.1875
- query_raise_factor: bfloat16 [4, 1024], replicated, may hold values from -0.29882812 to 0.29882812
- value_down: bfloat16 [1024, 4], replicated, may hold values from -0.1875 to 0.1875
- value_raise_factor: bfloat16 [4, 1024], replicated, may hold values from -0.29882812 to 0.29882812
- cotangent: bfloat16 [65536, 1024], P(('dp', 'fsdp')), may hold values from -6 to 6
Outputs:
- block_output: bfloat16 [65536, 1024], P(('dp', 'fsdp'))
- input_grad: float32 [65536, 1024], P(('dp', 'fsdp'))
- grad_query_down: float32 [1024, 4], replicated
- query_raise_gradient: float32 [4, 1024], replicated
- grad_value_down: float32 [1024, 4], replicated
- value_raise_gradient: float32 [4, 1024], replicated
The draws below stay inside these ranges and needn't reach their ends.
All inputs are finite; a program needn't handle non-finite values.
Results may differ from the reference program's by a relative error of at most 0.015.
Values may be sent and summed in bfloat16 or wider, within the bound.
No kernel may reach another device: no remote copies, remote signals or barrier semaphores. Data moves between devices by JAX's collectives and lax.ppermute only.
A program may use at most 192 MiB of HBM per device.

```python
import math
import jax
import jax.numpy as jnp
from jax import lax

MODEL_DIM = 1024
H = 16
HD = 64
FF = 4096
RANK = 4
TOK_DEV = 512
DOCS = 64
TOKENS = 65536


def shard_levels(key, shape, split, low, top_value):
    gain, own = 1.0, jax.random.fold_in(key, 6)
    for dim, parts in split:
        steps = jnp.exp(jax.random.uniform(jax.random.fold_in(own, dim), (parts,), jnp.float32, low / len(split), top_value / len(split)))
        gain = gain * jnp.repeat(steps, shape[dim] // parts).reshape([-1 if axis == dim else 1 for axis in range(len(shape))])
    return gain


def gaussian(key, extent, spread, limit, cuts=(), kind=jnp.bfloat16):
    loudness = shard_levels(key, extent, cuts, -0.22, 0.18) if cuts else 1.0
    values = jax.random.normal(key, extent, jnp.float32) * spread * loudness
    return jnp.minimum(jnp.maximum(values, -limit), limit).astype(kind)


def setup_inputs(seed: int = 0) -> dict:
    seeds = jax.random.split(jax.random.key(seed), 16)
    tokens = gaussian(seeds[0], (TOKENS, MODEL_DIM), 1.0, 6.0, ((0, 128),))
    norm_gains = jnp.clip(1.0 + 0.15 * jax.random.normal(seeds[1], (2, MODEL_DIM), jnp.float32), 0.25, 1.75).astype(jnp.bfloat16)
    norm_shifts = gaussian(seeds[2], (2, MODEL_DIM), 0.3, 1.1953125, ((1, 128),))
    query_value_offsets_bias = gaussian(seeds[3], (2, MODEL_DIM), 0.3, 1.1953125, ((1, 128),))
    output_biases = gaussian(seeds[4], (2, MODEL_DIM), 0.3, 1.1953125, ((1, 128),))
    expand_bias = gaussian(seeds[5], (FF,), 0.3, 1.1953125, ((0, 128),))
    joint_weight = gaussian(seeds[6], (MODEL_DIM, 3 * MODEL_DIM), MODEL_DIM ** -0.5, 0.1875, ((0, 128),))
    output_weight = gaussian(seeds[7], (MODEL_DIM, MODEL_DIM), (MODEL_DIM // 16) ** -0.5, 0.75, ((0, 128),))
    expand_weight = gaussian(seeds[8], (MODEL_DIM, FF), MODEL_DIM ** -0.5, 0.1875, ((0, 128),))
    shrink_weight = gaussian(seeds[9], (FF, MODEL_DIM), FF ** -0.5, 0.09375, ((0, 128),))
    query_down = gaussian(seeds[10], (MODEL_DIM, RANK), MODEL_DIM ** -0.5, 0.1875)
    query_raise_factor = gaussian(seeds[11], (RANK, MODEL_DIM), 0.05, 0.29882812)
    value_down = gaussian(seeds[12], (MODEL_DIM, RANK), MODEL_DIM ** -0.5, 0.1875)
    value_raise_factor = gaussian(seeds[13], (RANK, MODEL_DIM), 0.05, 0.29882812)
    cotangent = gaussian(seeds[14], (TOKENS, MODEL_DIM), 1.0, 6.0, ((0, 128),))
    return {"tokens": tokens, "norm_gains": norm_gains, "norm_shifts": norm_shifts, "query_value_offsets_bias": query_value_offsets_bias, "output_biases": output_biases, "expand_bias": expand_bias, "joint_weight": joint_weight, "output_weight": output_weight, "expand_weight": expand_weight, "shrink_weight": shrink_weight, "query_down": query_down, "query_raise_factor": query_raise_factor, "value_down": value_down, "value_raise_factor": value_raise_factor, "cotangent": cotangent}


@jax.custom_vjp
def reduced_rank(v):
    return lax.optimization_barrier(v.astype(jnp.bfloat16)).astype(jnp.float32)

@jax.custom_vjp
def reduced_rank_backward(v):
    return v

def low_keep(v):
    return (reduced_rank(v), None)

def low_pass(kept, grad):
    return (grad,)

def back_keep(v):
    return (v, None)

def back_low(kept, grad):
    return (reduced_rank(grad),)
reduced_rank.defvjp(low_keep, low_pass)
reduced_rank_backward.defvjp(back_keep, back_low)
EPS = 1e-05
ADAPTER_SCALE = 8.0
HIGHEST = lax.Precision.HIGHEST

def gelu_tanh(values):
    return 0.5 * values * (1.0 + jnp.tanh(0.7978845608028654 * (values + 0.044715 * values * values * values)))

def layer_norm(tok_rows, gain_row, shift_row):
    centered = tok_rows - lax.optimization_barrier(jnp.mean(tok_rows, axis=-1, keepdims=True))
    inverse = lax.rsqrt(lax.optimization_barrier(jnp.mean(centered * centered, axis=-1, keepdims=True)) + EPS)
    return centered * inverse * gain_row + shift_row

def matrix_multiply(left, right):
    return jnp.dot(left, right, precision=HIGHEST)

def block_forward(frozen, adapters, tok_rows):
    norm_gains, norm_shifts, query_value_offsets_bias, output_biases, expand_bias, joint_weight, output_weight, expand_weight, shrink_weight = frozen
    query_down, query_raise_factor, value_down, value_raise_factor = adapters
    length = tok_rows.shape[0]
    normed_one = reduced_rank(layer_norm(tok_rows, norm_gains[0], norm_shifts[0]))
    combined_projection = matrix_multiply(normed_one, joint_weight)
    query_reduced = reduced_rank(reduced_rank_backward(matrix_multiply(normed_one, query_down)))
    value_reduced = reduced_rank(reduced_rank_backward(matrix_multiply(normed_one, value_down)))
    query_matrix_rows = reduced_rank(reduced_rank_backward(combined_projection[:, :MODEL_DIM] + query_value_offsets_bias[0] + ADAPTER_SCALE * matrix_multiply(query_reduced, query_raise_factor)))
    key_rows = reduced_rank(reduced_rank_backward(combined_projection[:, MODEL_DIM:2 * MODEL_DIM]))
    value_matrix_rows = reduced_rank(reduced_rank_backward(combined_projection[:, 2 * MODEL_DIM:] + query_value_offsets_bias[1] + ADAPTER_SCALE * matrix_multiply(value_reduced, value_raise_factor)))
    scores = jnp.einsum('qhd,khd->hqk', query_matrix_rows.reshape(length, H, HD), key_rows.reshape(length, H, HD), precision=HIGHEST) * (1.0 / math.sqrt(HD))
    causal = jnp.arange(length)[:, None] >= jnp.arange(length)[None, :]
    scores = reduced_rank_backward(jnp.where(causal[None], scores, -1e+30))
    soft_weights = reduced_rank(jax.nn.softmax(scores, axis=-1))
    mixed_heads = jnp.einsum('hqk,khd->qhd', soft_weights, value_matrix_rows.reshape(length, H, HD), precision=HIGHEST)
    mixed_heads = reduced_rank(reduced_rank_backward(mixed_heads.reshape(length, MODEL_DIM)))
    attended = reduced_rank_backward(matrix_multiply(mixed_heads, output_weight) + output_biases[0])
    residual = tok_rows + attended
    normed_two = reduced_rank(layer_norm(residual, norm_gains[1], norm_shifts[1]))
    gate_pre = reduced_rank_backward(matrix_multiply(normed_two, expand_weight) + expand_bias)
    hidden = reduced_rank(gelu_tanh(gate_pre))
    return residual + matrix_multiply(hidden, shrink_weight) + output_biases[1]

def reference(tokens, norm_gains, norm_shifts, query_value_offsets_bias, output_biases, expand_bias, joint_weight, output_weight, expand_weight, shrink_weight, query_down, query_raise_factor, value_down, value_raise_factor, cotangent):
    frozen = tuple((array.astype(jnp.float32) for array in (norm_gains, norm_shifts, query_value_offsets_bias, output_biases, expand_bias, joint_weight, output_weight, expand_weight, shrink_weight)))
    adapters = tuple((array.astype(jnp.float32) for array in (query_down, query_raise_factor, value_down, value_raise_factor)))
    doc_rows = tokens.astype(jnp.float32).reshape(DOCS, 2 * TOK_DEV, MODEL_DIM)
    doc_cots = cotangent.astype(jnp.float32).reshape(DOCS, 2 * TOK_DEV, MODEL_DIM)

    def one_doc(totals, doc_pair):
        tok_rows, cot_rows = doc_pair

        def forward_doc(inputs, adapt_set):
            return block_forward(frozen, adapt_set, inputs)
        result, pull_back = jax.vjp(forward_doc, tok_rows, adapters)
        grad_rows, grad_adapt = pull_back(cot_rows)
        totals = tuple((running + addend for running, addend in zip(totals, grad_adapt)))
        return (totals, (result, grad_rows))
    starts = tuple((jnp.zeros(array.shape, jnp.float32) for array in adapters))
    totals, (outputs, row_grads) = lax.scan(one_doc, starts, (doc_rows, doc_cots))
    return (outputs.reshape(TOKENS, MODEL_DIM).astype(jnp.bfloat16), row_grads.reshape(TOKENS, MODEL_DIM), totals[0] / DOCS, totals[1] / DOCS, totals[2] / DOCS, totals[3] / DOCS)
```

```python
import math

import jax
import jax.numpy as jnp
from jax import lax
from jax.experimental import pallas as pl
from jax.experimental.pallas import tpu as pltpu
from jax.sharding import Mesh, PartitionSpec as P

AXES = ("zl", "x", "y", "c", "zh")
PAIR = ("c", "zh")
ZRING = ("zl", "zh")
Z_PLACE = (0, 2, 1, 3)
SWAP = [(0, 0), (1, 2), (2, 1), (3, 3)]
CROSS = [(0, 2), (1, 0), (2, 3), (3, 1)]
FLIP = [(0, 1), (1, 0)]
FROM_NEXT = [(i, (i - 1) % 4) for i in range(4)]
FROM_PREV = [(i, (i + 1) % 4) for i in range(4)]
FROM_OPPOSITE = [(i, (i + 2) % 4) for i in range(4)]

EPS = 1e-05
ADAPTER_SCALE = 8.0
D = 1024
HALF = 512
HID = 2048
CHUNK = 512
BQ = 256
VMEM_LIMIT = 58 * 2**20
BF = jnp.bfloat16
F32 = jnp.float32

ANY = pl.BlockSpec(memory_space=pl.ANY)
VMEM = pl.BlockSpec(memory_space=pltpu.VMEM)


def permute(value, axis, pairs):
    if axis == ZRING:
        pairs = [(Z_PLACE[i], Z_PLACE[j]) for i, j in pairs]
    return lax.ppermute(value, axis, pairs)


def from_sibling(value):
    return lax.ppermute(value, "c", FLIP)


def ring(value, axis):
    return (
        value,
        permute(value, axis, FROM_NEXT),
        permute(value, axis, FROM_OPPOSITE),
        permute(value, axis, FROM_PREV),
    )


def ring_halves(value, axis):
    after = permute(value, axis, FROM_NEXT)
    before = permute(value, axis, FROM_PREV)
    n = value.shape[0] // 2
    first = permute(before[:n], axis, FROM_PREV)
    second = permute(after[n:], axis, FROM_NEXT)
    return (value, after, before, first, second)


def everywhere_sum(value):
    value = value + from_sibling(value)
    for axis in ("x", "y", ZRING):
        own, after, opposite, before = ring(value, axis)
        value = (own + opposite) + (after + before)
    return value


def places():
    z = lax.axis_index("zh") * 2 + lax.axis_index("zl")
    return {"x": lax.axis_index("x"), "y": lax.axis_index("y"), "z": z}


def place_of(axis, step):
    spot = lax.rem(places()[axis] + step, 4)
    if axis == "z":
        return lax.rem(spot, 2), lax.div(spot, 2)
    return (spot,)


def cost(flops, nbytes, transcendentals=0):
    return pl.CostEstimate(
        flops=int(flops), bytes_accessed=int(nbytes), transcendentals=int(transcendentals)
    )


def assemble(jobs):
    pieces = []
    for job in jobs:
        for p in job[0]:
            if not any(p is q for q in pieces):
                pieces.append(p)
    n = len(pieces)
    where = [[next(i for i, q in enumerate(pieces) if q is p) for p in job[0]] for job in jobs]

    def kernel(*refs):
        for at, job in enumerate(jobs):
            for step in range(4):
                job[2](refs[n + at], step, refs[where[at][step]])

    total = sum(math.prod(job[1]) for job in jobs)
    return pl.pallas_call(
        kernel,
        out_shape=[jax.ShapeDtypeStruct(job[1], BF) for job in jobs],
        in_specs=[VMEM] * n,
        out_specs=[VMEM] * len(jobs),
        cost_estimate=cost(0, 4 * total),
    )(*pieces)


def pack_kernel(joint, wo, w1, w2, vec, first_a, first_b, rest_a, rest_b, shuffled):
    zh = lax.axis_index("zh")
    rows = jnp.concatenate(
        [w1[:, s * 512 : (s + 1) * 512].astype(F32) for s in range(8)], axis=0
    ).astype(BF)
    lane = lax.broadcasted_iota(jnp.int32, (512, 512), 0)
    out = lax.broadcasted_iota(jnp.int32, (512, 512), 1)
    match = (lane >> 5) == ((out & 127) >> 3)
    match = match & (((lane & 31) >> 3) == (out >> 7)) & ((lane & 7) == (out & 7))
    mixed = jnp.dot(rows, jnp.where(match, 1.0, 0.0).astype(BF), preferred_element_type=F32)
    for s in range(8):
        for part in range(4):
            shuffled[part, :, s * 128 : (s + 1) * 128] = mixed[
                s * 8 : (s + 1) * 8, part * 128 : (part + 1) * 128
            ]
    for half, first, rest in ((zh, first_a, rest_a), (1 - zh, first_b, rest_b)):
        cols = [joint[:, pl.ds(pl.multiple_of(n * D + half * HALF, 128), HALF)] for n in range(3)]
        first[:, 0:512] = cols[0]
        first[:, 512:768] = cols[1][:, 0:256]
        first[:, 768:896] = vec[...]
        first[:, 896:1152] = cols[1][:, 256:512]
        first[:, 1152:1664] = cols[2]
        for g in range(2):
            rest[:, g * D : (g + 1) * D] = shuffled[2 * half + g].astype(BF)
            rest[:, HID + g * D : HID + (g + 1) * D] = w2[2 * half + g]
        rest[:, 2 * HID :] = wo[...]


def pack(joint, wo, w1, w2, vec):
    first = jax.ShapeDtypeStruct((8, 1664), BF)
    rest = jax.ShapeDtypeStruct((8, 5120), BF)
    return pl.pallas_call(
        pack_kernel,
        out_shape=[first, first, rest, rest],
        in_specs=[VMEM] * 5,
        out_specs=[VMEM] * 4,
        scratch_shapes=[pltpu.VMEM((4, 8, D), F32)],
        cost_estimate=cost(2 * 64 * 512 * 512, 600_000),
    )(joint, wo, w1, w2.reshape(4, 8, D), vec)


def chip_rows(for_a, for_b):
    a = lax.ppermute(for_a, PAIR, SWAP)
    b = lax.ppermute(for_b, PAIR, CROSS)
    low = lax.axis_index("c") == 0
    return jnp.concatenate([jnp.where(low, a, b), jnp.where(low, b, a)], axis=0)


def put_z_first(first, last):
    def put(out, step, piece):
        zl, zh = place_of("z", step)
        out[zl, zh] = piece[:, first:last]

    return put


def put_second(axis):
    def put(out, step, piece):
        (spot,) = place_of(axis, step)
        for zl in range(2):
            out[zl, spot] = piece[zl]

    return put


def put_first(axis):
    def put(out, step, piece):
        (spot,) = place_of(axis, step)
        out[spot] = piece[...]

    return put


def put_z_second(out, step, piece):
    zl, zh = place_of("z", step)
    for x in range(4):
        out[zl, x, zh] = piece[x]


def gather_joint(first_a, first_b):
    rows = chip_rows(first_a, first_b)
    pieces = ring(rows, ZRING)
    a, b = assemble(
        [
            (pieces, (2, 2, 16, 896), put_z_first(0, 896)),
            (pieces, (2, 2, 16, 768), put_z_first(896, 1664)),
        ]
    )
    a, b = a.reshape(2, 32, 896), b.reshape(2, 32, 768)
    a, b = assemble(
        [
            (ring(a, "y"), (2, 4, 32, 896), put_second("y")),
            (ring(b, "x"), (2, 4, 32, 768), put_second("x")),
        ]
    )
    return ring(a, "x"), ring(b, "y")


def gather_rest(rest_a, rest_b):
    rows = chip_rows(rest_a, rest_b)
    w1, w2, wo = rows[:, :HID], rows[:, HID : 2 * HID], rows[:, 2 * HID :]
    w1, w2, wo = assemble(
        [
            (ring(w1, ZRING), (2, 2, 16, HID), put_z_first(0, HID)),
            (ring(w2, "x"), (4, 16, HID), put_first("x")),
            (ring(wo, "y"), (4, 16, D), put_first("y")),
        ]
    )
    w1 = w1.reshape(2, 32, HID)
    w1, w2, wo = assemble(
        [
            (ring(w1, "y"), (2, 4, 32, HID), put_second("y")),
            (ring(w2, ZRING), (2, 4, 2, 16, HID), put_z_second),
            (ring(wo, "x"), (4, 4, 16, D), put_first("x")),
        ]
    )
    wo = wo.reshape(16, 16, D)
    w2 = w2.reshape(2, 4, 32, HID)
    return ring_halves(w1, "x"), ring_halves(w2, "y"), ring(wo, ZRING)


def dot(left, right):
    return jnp.dot(left, right, preferred_element_type=F32)


def dot_last(left, right):
    return lax.dot_general(left, right, (((1,), (1,)), ((), ())), preferred_element_type=F32)


def dot_first(left, right):
    return lax.dot_general(left, right, (((0,), (0,)), ((), ())), preferred_element_type=F32)


def normalise(rows):
    centered = rows - jnp.mean(rows, axis=-1, keepdims=True)
    inverse = lax.rsqrt(jnp.mean(centered * centered, axis=-1, keepdims=True) + EPS)
    return centered * inverse, inverse


def norm_back(upstream, normed, inverse, gain):
    scaled = upstream * gain
    return inverse * (
        scaled
        - jnp.mean(scaled, axis=-1, keepdims=True)
        - normed * jnp.mean(scaled * normed, axis=-1, keepdims=True)
    )


def start_all(copies):
    for copy in copies:
        copy.start()


def wait_all(copies):
    for copy in copies:
        copy.wait()


def own_half():
    c = lax.axis_index("c")
    own = pl.ds(pl.multiple_of(c * HALF, HALF), HALF)
    other = pl.ds(pl.multiple_of((1 - c) * HALF, HALF), HALF)
    return own, other


def project_kernel(*refs):
    tok_own, tok_sib = refs[:2]
    a_pieces, b_pieces = refs[2:6], refs[6:10]
    down, raised = refs[10:12]
    q, k, v, low, n1, joint_out, vec_out = refs[12:19]
    tok, joint, vec, sem = refs[19:]
    own, other = own_half()
    copies = [
        pltpu.make_async_copy(tok_own, tok.at[own], sem.at[0]),
        pltpu.make_async_copy(tok_sib, tok.at[other], sem.at[1]),
    ]
    for step in range(4):
        (x,), (y,) = place_of("x", step), place_of("y", step)
        a, b = a_pieces[step], b_pieces[step]
        copies += [
            pltpu.make_async_copy(a.at[:, :, :, 768:896], vec.at[:, x], sem.at[2 + step]),
            pltpu.make_async_copy(
                a.at[:, :, :, 0:768], joint.at[:, x, :, :, 0:768], sem.at[6 + step]
            ),
            pltpu.make_async_copy(b, joint.at[:, :, y, :, 768:1536], sem.at[10 + step]),
        ]
    start_all(copies)
    wait_all(copies)
    save = pltpu.make_async_copy(joint, joint_out, sem.at[14])
    save.start()
    vec_out[...] = jnp.transpose(vec[...].reshape(D, 128).astype(F32))[:16]
    gain, shift = vec_out[0:1], vec_out[2:3]
    bias_q, bias_v = vec_out[4:5, own], vec_out[5:6, own]

    @pl.loop(0, 4)
    def _(i):
        rows = pl.ds(pl.multiple_of(i * 256, 256), 256)
        normed, _ = normalise(tok[rows].astype(F32))
        normed = (normed * gain + shift).astype(BF)
        n1[rows] = normed
        reduced = dot(normed, down[...]).astype(BF)
        low[rows] = reduced
        added = dot(reduced, raised[...])
        weights = joint[...].reshape(D, 3 * HALF)
        both = dot(normed, weights)
        q[rows] = ((both[:, :512] + bias_q + added[:, :512]).astype(BF) * 0.125).astype(BF)
        k[rows] = both[:, 512:1024].astype(BF)
        v[rows] = (both[:, 1024:] + bias_v + added[:, 512:]).astype(BF)

    save.wait()


def project(tok_own, tok_sib, a_pieces, b_pieces, down, raised):
    shape = jax.ShapeDtypeStruct
    return pl.pallas_call(
        project_kernel,
        out_shape=[
            shape((D, HALF), BF),
            shape((D, HALF), BF),
            shape((D, HALF), BF),
            shape((D, 128), BF),
            shape((D, D), BF),
            shape((2, 4, 4, 32, 3 * HALF), BF),
            shape((16, D), F32),
        ],
        in_specs=[ANY] * 10 + [VMEM] * 2,
        out_specs=[VMEM] * 5 + [ANY, VMEM],
        scratch_shapes=[
            pltpu.VMEM((D, D), BF),
            pltpu.VMEM((2, 4, 4, 32, 3 * HALF), BF),
            pltpu.VMEM((2, 4, 4, 32, 128), BF),
            pltpu.SemaphoreType.DMA((15,)),
        ],
        compiler_params=pltpu.CompilerParams(vmem_limit_bytes=VMEM_LIMIT),
        cost_estimate=cost(2 * D * D * 1536, 16e6),
    )(tok_own, tok_sib, *a_pieces, *b_pieces, down, raised)


def head_mask(head, rows):
    lane = lax.broadcasted_iota(jnp.int32, (rows, 128), 1)
    return (lane >= 64) if head else (lane < 64)


def attend_kernel(q, k, v, out_own, out_sib, probs, out):
    own, other = own_half()
    for i in range(D // BQ):
        out[i * BQ : (i + 1) * BQ] = jnp.zeros((BQ, 128), F32)
    below = lax.broadcasted_iota(jnp.int32, (BQ, BQ), 0) <= lax.broadcasted_iota(
        jnp.int32, (BQ, BQ), 1
    )
    for head in range(2):
        mask = head_mask(head, D)
        v_head = jnp.where(mask, v[...], 0)
        for i in range(D // BQ):
            rows = slice(i * BQ, (i + 1) * BQ)
            keys = (i + 1) * BQ
            q_head = jnp.where(mask[:BQ], q[rows], 0)
            scores = dot_last(k[:keys], q_head)
            last = jnp.where(below, scores[i * BQ :], -1e30)
            scores = jnp.concatenate([scores[: i * BQ], last], axis=0) if i else last
            top = jnp.max(scores, axis=0, keepdims=True)
            e = jnp.exp(scores - top)
            p = (e * (1.0 / jnp.sum(e, axis=0, keepdims=True))).astype(BF)
            probs[head, :keys, rows] = p
            out[rows] += dot_first(p, v_head[:keys])
    out_own[...] = out[own].astype(BF)
    out_sib[...] = out[other].astype(BF)


def attend(q, k, v):
    shape = jax.ShapeDtypeStruct
    columns = pl.BlockSpec((D, 128), lambda j: (0, j))
    halves = pl.BlockSpec((HALF, 128), lambda j: (0, j))
    return pl.pallas_call(
        attend_kernel,
        grid=(4,),
        out_shape=[shape((HALF, HALF), BF), shape((HALF, HALF), BF), shape((8, D, D), BF)],
        in_specs=[columns] * 3,
        out_specs=[halves, halves, pl.BlockSpec((2, D, D), lambda j: (j, 0, 0))],
        scratch_shapes=[pltpu.VMEM((D, 128), F32)],
        compiler_params=pltpu.CompilerParams(vmem_limit_bytes=VMEM_LIMIT),
        cost_estimate=cost(8e9, 20e6, 8 * D * D),
    )(q, k, v)


def attend_back_kernel(q, k, v, d_own, d_sib, probs, dq, dk, dv, d_out, d_scores):
    own, other = own_half()
    d_out[own] = d_own[...]
    d_out[other] = d_sib[...]
    blocks = D // BQ
    for head in range(2):
        mask = head_mask(head, D)
        d_head = jnp.where(mask, d_out[...], 0)
        for i in range(blocks):
            rows = slice(i * BQ, (i + 1) * BQ)
            keys = (i + 1) * BQ
            p = probs[head, :keys, rows].astype(F32)
            weighted = p * dot_last(v[:keys], d_head[rows])
            ds = weighted - p * jnp.sum(weighted, axis=0, keepdims=True)
            d_scores[head, :keys, rows] = ds.astype(BF)
    masks = [head_mask(head, D) for head in range(2)]
    for i in range(blocks):
        rows = slice(i * BQ, (i + 1) * BQ)
        keys = (i + 1) * BQ
        total_q, total_k, total_v = 0.0, 0.0, 0.0
        for head in range(2):
            mask = masks[head]
            k_head = jnp.where(mask[:keys], k[:keys], 0)
            q_head = jnp.where(mask[i * BQ :], q[i * BQ :], 0)
            d_head = jnp.where(mask[i * BQ :], d_out[i * BQ :], 0)
            total_q += dot_first(d_scores[head, :keys, rows], k_head)
            total_k += dot(d_scores[head, rows, i * BQ :], q_head)
            total_v += dot(probs[head, rows, i * BQ :], d_head)
        dq[rows] = (total_q * 0.125).astype(BF)
        dk[rows] = total_k.astype(BF)
        dv[rows] = total_v.astype(BF)


def attend_back(q, k, v, d_own, d_sib, probs):
    shape = jax.ShapeDtypeStruct
    columns = pl.BlockSpec((D, 128), lambda j: (0, j))
    halves = pl.BlockSpec((HALF, 128), lambda j: (0, j))
    return pl.pallas_call(
        attend_back_kernel,
        grid=(4,),
        out_shape=[shape((D, HALF), BF)] * 3,
        in_specs=[columns] * 3 + [halves] * 2 + [pl.BlockSpec((2, D, D), lambda j: (j, 0, 0))],
        out_specs=[columns] * 3,
        scratch_shapes=[pltpu.VMEM((D, 128), BF), pltpu.VMEM((2, D, D), BF)],
        compiler_params=pltpu.CompilerParams(vmem_limit_bytes=VMEM_LIMIT),
        cost_estimate=cost(16e9, 20e6),
    )(q, k, v, d_own, d_sib, probs)


def after_attention_kernel(*refs):
    mixed_own, mixed_other, tok, vec = refs[:4]
    pieces = refs[4:8]
    residual, n2, wo_out = refs[8:11]
    wo, sem = refs[11:]
    own, other = own_half()
    copies = []
    for step in range(4):
        zl, zh = place_of("z", step)
        copies.append(pltpu.make_async_copy(pieces[step], wo.at[zl, :, zh], sem.at[step]))
    start_all(copies)
    wait_all(copies)
    save = pltpu.make_async_copy(wo, wo_out, sem.at[4])
    save.start()
    weights = wo[...].reshape(D, D)
    c = lax.axis_index("c")
    low = jnp.where(c == 0, mixed_own[...], mixed_other[...])
    high = jnp.where(c == 0, mixed_other[...], mixed_own[...])
    attended = dot(low, weights[:HALF]) + dot(high, weights[HALF:])
    rows = tok[...].astype(F32) + attended + vec[6:7]
    residual[...] = rows
    normed, _ = normalise(rows)
    n2[...] = (normed * vec[1:2] + vec[3:4]).astype(BF)
    save.wait()


def after_attention(mixed_own, mixed_other, tok, vec, pieces):
    shape = jax.ShapeDtypeStruct
    return pl.pallas_call(
        after_attention_kernel,
        out_shape=[shape((HALF, D), F32), shape((HALF, D), BF), shape((2, 16, 2, 16, D), BF)],
        in_specs=[VMEM] * 4 + [ANY] * 4,
        out_specs=[VMEM, VMEM, ANY],
        scratch_shapes=[pltpu.VMEM((2, 16, 2, 16, D), BF), pltpu.SemaphoreType.DMA((5,))],
        compiler_params=pltpu.CompilerParams(vmem_limit_bytes=VMEM_LIMIT),
        cost_estimate=cost(2 * HALF * D * D, 12e6),
    )(mixed_own, mixed_other, tok, vec, *pieces)


def feed_forward_kernel(*refs):
    n2, cot, vec = refs[:3]
    w1_pieces, w2_pieces = refs[3:8], refs[8:13]
    out, d_n2 = refs[13:15]
    w1, w2, total, d_total, sem = refs[15:]
    (x0,), (x1,), (x2,), (x3,) = [place_of("x", step) for step in range(4)]
    (y0,), (y1,), (y2,), (y3,) = [place_of("y", step) for step in range(4)]
    chunks = HID // CHUNK
    copies = []
    for j in range(chunks):
        cols = slice(j * CHUNK, (j + 1) * CHUNK)
        g, zl = j // 2, j % 2
        own, after, before, first, second = [piece.at[..., cols] for piece in w1_pieces]
        some = [
            (own, w1.at[j, :, x0]),
            (after, w1.at[j, :, x1]),
            (before, w1.at[j, :, x3]),
            (first.at[0], w1.at[j, 0, x2]),
            (second.at[0], w1.at[j, 1, x2]),
        ]
        wide = slice(g * D, (g + 1) * D)
        own, after, before = [piece.at[zl, :, :, wide] for piece in w2_pieces[:3]]
        some += [
            (own, w2.at[j, :, y0]),
            (after, w2.at[j, :, y1]),
            (before, w2.at[j, :, y3]),
            (w2_pieces[3 + zl].at[0, :, :, wide], w2.at[j, :, y2]),
        ]
        copies.append(
            [pltpu.make_async_copy(s, d, sem.at[j, n]) for n, (s, d) in enumerate(some)]
        )
    for some in copies:
        start_all(some)
    c = lax.axis_index("c")
    for j in range(chunks):
        wait_all(copies[j])
        g, part = j // 2, j % 2
        bias = vec[pl.ds(8 + 2 * c + g, 1), part * CHUNK : (part + 1) * CHUNK]
        expand = w1[j].reshape(D, CHUNK)
        shrink = w2[j].reshape(CHUNK, D)
        u = dot(n2[...], expand) + bias
        t = jnp.tanh(0.7978845608028654 * (u + 0.044715 * u * u * u))
        hidden = (0.5 * u * (1.0 + t)).astype(BF)
        slope = 0.5 * (1.0 + t) + 0.5 * u * (1.0 - t * t) * (
            0.7978845608028654 * (1.0 + 3 * 0.044715 * u * u)
        )
        d_gate = (dot_last(cot[...], shrink) * slope).astype(BF)
        if j == 0:
            total[...] = dot(hidden, shrink)
            d_total[...] = dot_last(d_gate, expand)
        else:
            total[...] += dot(hidden, shrink)
            d_total[...] += dot_last(d_gate, expand)
    out[...] = total[...].astype(out.dtype)
    d_n2[...] = d_total[...].astype(d_n2.dtype)


def feed_forward(n2, cot, vec, w1_pieces, w2_pieces, dtype):
    return pl.pallas_call(
        feed_forward_kernel,
        out_shape=[jax.ShapeDtypeStruct((HALF, D), dtype)] * 2,
        in_specs=[VMEM] * 3 + [ANY] * 10,
        out_specs=[VMEM, VMEM],
        scratch_shapes=[
            pltpu.VMEM((4, 2, 4, 4, 32, CHUNK), BF),
            pltpu.VMEM((4, 4, 4, 32, D), BF),
            pltpu.VMEM((HALF, D), F32),
            pltpu.VMEM((HALF, D), F32),
            pltpu.SemaphoreType.DMA((4, 9)),
        ],
        compiler_params=pltpu.CompilerParams(vmem_limit_bytes=VMEM_LIMIT),
        cost_estimate=cost(8 * HALF * D * HID, 16e6, HALF * HID),
    )(n2, cot, vec, *w1_pieces, *w2_pieces)


def before_attention_kernel(
    residual, cot, d_own, d_recv, vec, wo, d_residual, d_mixed_own, d_mixed_sib
):
    normed, inverse = normalise(residual[...])
    d_n2 = d_own[...] + d_recv[...].astype(F32)
    d_rows = cot[...].astype(F32) + norm_back(d_n2, normed, inverse, vec[1:2])
    d_residual[...] = d_rows
    d_attended = d_rows.astype(BF)
    own, other = own_half()
    d_mixed_sib[...] = dot_last(d_attended, wo[other]).astype(BF)
    d_mixed_own[...] = dot_last(d_attended, wo[own]).astype(BF)


def before_attention(residual, cot, d_own, d_recv, vec, wo):
    shape = jax.ShapeDtypeStruct
    return pl.pallas_call(
        before_attention_kernel,
        out_shape=[shape((HALF, D), F32), shape((HALF, HALF), BF), shape((HALF, HALF), BF)],
        in_specs=[VMEM] * 6,
        out_specs=[VMEM] * 3,
        compiler_params=pltpu.CompilerParams(vmem_limit_bytes=VMEM_LIMIT),
        cost_estimate=cost(2 * HALF * D * D, 12e6),
    )(residual, cot, d_own, d_recv, vec, wo)


def adapter_kernel(n1, low, dq, dk, dv, raised, sums, d_low_out):
    grads = jnp.concatenate([dq[...], dv[...]], axis=1)
    d_low = dot_last(grads, raised[...]).astype(BF)
    d_low_out[...] = d_low
    sums[0:8] = dot_first(d_low, n1[...])[:8]
    raise_sums = dot_first(low[...], grads)[:8] * ADAPTER_SCALE
    own, other = own_half()
    top = lax.broadcasted_iota(jnp.int32, (8, HALF), 0) < 4
    sums[8:16, own] = jnp.where(top, raise_sums[:, :HALF], raise_sums[:, HALF:])
    sums[8:16, other] = jnp.zeros((8, HALF), F32)


def adapter_sums(n1, low, dq, dk, dv, raised):
    shape = jax.ShapeDtypeStruct
    return pl.pallas_call(
        adapter_kernel,
        out_shape=[shape((16, D), F32), shape((D, 128), BF)],
        in_specs=[VMEM] * 6,
        out_specs=[VMEM] * 2,
        compiler_params=pltpu.CompilerParams(vmem_limit_bytes=VMEM_LIMIT),
        cost_estimate=cost(3 * 2 * D * D * 128, 6e6),
    )(n1, low, dq, dk, dv, raised)


def input_part_kernel(dq, dk, dv, d_low, joint, down, out, *, mine):
    own, other = own_half()
    rows = own if mine else other
    total = dot_last(d_low[rows], down[...])
    total += dot_last(dq[rows], joint[:, :HALF])
    total += dot_last(dk[rows], joint[:, HALF:D])
    total += dot_last(dv[rows], joint[:, D:])
    out[...] = total.astype(out.dtype)


def input_part(dq, dk, dv, d_low, joint, down, mine):
    def kernel(*refs):
        input_part_kernel(*refs, mine=mine)

    return pl.pallas_call(
        kernel,
        out_shape=jax.ShapeDtypeStruct((HALF, D), F32 if mine else BF),
        in_specs=[VMEM] * 6,
        out_specs=VMEM,
        compiler_params=pltpu.CompilerParams(vmem_limit_bytes=VMEM_LIMIT),
        cost_estimate=cost(2 * HALF * D * 1664, 8e6),
    )(dq, dk, dv, d_low, joint, down)


def input_kernel(tok, d_residual, part, recv, vec, out):
    normed, inverse = normalise(tok[...].astype(F32))
    d_n1 = part[...] + recv[...].astype(F32)
    out[...] = (d_residual[...] + norm_back(d_n1, normed, inverse, vec[0:1])).astype(BF)


def input_rows(tok, d_residual, part, recv, vec):
    return pl.pallas_call(
        input_kernel,
        out_shape=jax.ShapeDtypeStruct((HALF, D), BF),
        in_specs=[VMEM] * 5,
        out_specs=VMEM,
        compiler_params=pltpu.CompilerParams(vmem_limit_bytes=VMEM_LIMIT),
        cost_estimate=cost(0, 8e6),
    )(tok, d_residual, part, recv, vec)


def local(
    tokens,
    norm_gains,
    norm_shifts,
    query_value_offsets_bias,
    output_biases,
    expand_bias,
    joint_weight,
    output_weight,
    expand_weight,
    shrink_weight,
    query_down,
    query_raise_factor,
    value_down,
    value_raise_factor,
    cotangent,
):
    vectors = jnp.concatenate(
        [
            norm_gains,
            norm_shifts,
            query_value_offsets_bias,
            output_biases,
            expand_bias.reshape(4, 8),
        ],
        axis=0,
    )
    vectors = jnp.pad(vectors.T, ((0, 0), (0, 116)))
    first_a, first_b, rest_a, rest_b = pack(
        joint_weight, output_weight, expand_weight, shrink_weight, vectors
    )
    joint_a, joint_b = gather_joint(first_a, first_b)
    w1_pieces, w2_pieces, wo_pieces = gather_rest(rest_a, rest_b)

    tok = lax.ppermute(tokens, PAIR, SWAP)
    tok_sib = from_sibling(tok)
    cot = lax.ppermute(cotangent, PAIR, SWAP)
    cot_sib = from_sibling(cot)

    c = lax.axis_index("c")
    down = jnp.pad(jnp.concatenate([query_down, value_down], axis=1), ((0, 0), (0, 120)))
    raise_q = lax.dynamic_slice_in_dim(query_raise_factor, c * HALF, HALF, axis=1)
    raise_v = lax.dynamic_slice_in_dim(value_raise_factor, c * HALF, HALF, axis=1)
    raised = ADAPTER_SCALE * jnp.concatenate(
        [jnp.pad(raise_q, ((0, 124), (0, 0))), jnp.pad(raise_v, ((4, 120), (0, 0)))], axis=1
    )
    raised = raised.astype(BF)

    q, k, v, low, n1, joint, vec = project(tok, tok_sib, joint_a, joint_b, down, raised)
    joint = joint.reshape(D, 3 * HALF)
    mixed_own, mixed_sib, probs = attend(q, k, v)
    mixed_other = from_sibling(mixed_sib)
    residual, n2, wo = after_attention(mixed_own, mixed_other, tok, vec, wo_pieces)
    wo = wo.reshape(D, D)
    n2_sib = from_sibling(n2)
    out_own, d_own = feed_forward(n2, cot, vec, w1_pieces, w2_pieces, F32)
    out_sib, d_sib = feed_forward(n2_sib, cot_sib, vec, w1_pieces, w2_pieces, BF)
    d_recv = from_sibling(d_sib)
    out_recv = from_sibling(out_sib)
    d_residual, d_mixed_own, d_mixed_sib = before_attention(
        residual, cot, d_own, d_recv, vec, wo
    )
    block_rows = (residual + out_own + out_recv.astype(F32) + vec[7]).astype(BF)
    block_output = lax.ppermute(block_rows, PAIR, SWAP)
    d_mixed_other = from_sibling(d_mixed_sib)
    dq, dk, dv = attend_back(q, k, v, d_mixed_own, d_mixed_other, probs)
    sums, d_low = adapter_sums(n1, low, dq, dk, dv, raised)
    sums = everywhere_sum(sums) / 64.0
    part_sib = input_part(dq, dk, dv, d_low, joint, down, False)
    part_recv = from_sibling(part_sib)
    part_own = input_part(dq, dk, dv, d_low, joint, down, True)
    grad = input_rows(tok, d_residual, part_own, part_recv, vec)
    input_grad = lax.ppermute(grad, PAIR, SWAP).astype(F32)
    return (
        block_output,
        input_grad,
        sums[0:4].T,
        sums[8:12],
        sums[4:8].T,
        sums[12:16],
    )


def solution(mesh):
    fine = Mesh(mesh.devices.reshape(2, 4, 4, 2, 2), AXES)
    rows, columns = P(AXES, None), P(None, AXES)
    placed = (
        (rows,) + (columns,) * 4 + (P(AXES),) + (rows,) * 4 + (P(),) * 4 + (rows,)
    )
    return jax.shard_map(
        local,
        mesh=fine,
        in_specs=placed,
        out_specs=(rows, rows, P(), P(), P(), P()),
        check_vma=False,
    )
```

```python
import math

import jax
import jax.numpy as jnp
from jax import lax
from jax.experimental import pallas as pl
from jax.experimental.pallas import tpu as pltpu
from jax.sharding import Mesh, PartitionSpec as P

AXES = ("zl", "x", "y", "c", "zh")
PAIR = ("c", "zh")
ZRING = ("zl", "zh")
Z_PLACE = (0, 2, 1, 3)
SWAP = [(0, 0), (1, 2), (2, 1), (3, 3)]
FLIP = [(0, 1), (1, 0)]
FROM_NEXT = [(i, (i - 1) % 4) for i in range(4)]
FROM_PREV = [(i, (i + 1) % 4) for i in range(4)]
FROM_OPPOSITE = [(i, (i + 2) % 4) for i in range(4)]

EPS = 1e-05
ADAPTER_SCALE = 8.0
D = 1024
HALF = 512
HID = 2048
CHUNK = 512
A_FIRST = 1408
B_FIRST = 1280
B_AT = A_FIRST + HID
VMEM_LIMIT = 24 * 2**20
BF = jnp.bfloat16
F32 = jnp.float32

ANY = pl.BlockSpec(memory_space=pl.ANY)
HBM = pl.BlockSpec(memory_space=pltpu.HBM)
VMEM = pl.BlockSpec(memory_space=pltpu.VMEM)


def permute(value, axis, pairs):
    if axis == ZRING:
        pairs = [(Z_PLACE[i], Z_PLACE[j]) for i, j in pairs]
    return lax.ppermute(value, axis, pairs)


def from_sibling(value):
    return lax.ppermute(value, "c", FLIP)


def ring(value, axis):
    return (
        value,
        permute(value, axis, FROM_NEXT),
        permute(value, axis, FROM_OPPOSITE),
        permute(value, axis, FROM_PREV),
    )


def parity_pairs(axis, back):
    pairs = []
    for i in range(4):
        for c in range(2):
            j = (i + (1 if (c == 0) != back else -1)) % 4
            if axis == ZRING:
                i_at, j_at = (4 * (i % 2) + 2 * c + i // 2, 4 * (j % 2) + 2 * c + j // 2)
            else:
                i_at, j_at = 2 * i + c, 2 * j + c
            pairs.append((i_at, j_at))
    return pairs


def ahead(value, axis):
    names = ("zl", "c", "zh") if axis == ZRING else (axis, "c")
    return lax.ppermute(value, names, parity_pairs(axis, False))


def near(value, axis):
    names = ("zl", "c", "zh") if axis == ZRING else (axis, "c")
    return ahead(value, axis), lax.ppermute(value, names, parity_pairs(axis, True))


def ring_sum(pieces):
    own, after, opposite, before = pieces
    return (own + opposite) + (after + before)


def places():
    z = lax.axis_index("zh") * 2 + lax.axis_index("zl")
    return {"x": lax.axis_index("x"), "y": lax.axis_index("y"), "z": z}


def place_of(axis, step):
    spot = lax.rem(places()[axis] + step, 4)
    if axis == "z":
        return lax.rem(spot, 2), lax.div(spot, 2)
    return (spot,)


def turn_of(axis, step):
    way = 1 + 2 * lax.axis_index("c") if step % 2 else 1
    return lax.rem(places()[axis] + (4 - step) * way, 4)


def cost(flops, nbytes, transcendentals=0):
    return pl.CostEstimate(
        flops=int(flops), bytes_accessed=int(nbytes), transcendentals=int(transcendentals)
    )


def pack_first_kernel(
    joint, gains, shifts, offsets, biases, expand_bias, own, sibling, rows
):
    c = lax.axis_index("c")
    rows[...] = jnp.zeros_like(rows)
    for at, pair in enumerate((gains, shifts, offsets, biases)):
        rows[2 * at : 2 * at + 2, :8] = pair[...].astype(F32)
    rows[8:9, :32] = expand_bias[...].astype(F32)
    bias = rows[8:16]
    for part in range(1, 4):
        rows[8 + part : 9 + part] = pltpu.roll(bias, 128 - 8 * part, axis=1)[0:1]
    vectors = jnp.transpose(rows[...])[:8].astype(BF)
    for half, out in ((c, own), (1 - c, sibling)):
        q, k, v = [joint[:, pl.ds(pl.multiple_of(n * D + half * HALF, 128), HALF)] for n in range(3)]
        out[:, 0:512] = q
        out[:, 512:768] = k[:, 0:256]
        out[:, 768:896] = vectors
        out[:, B_AT : B_AT + 256] = k[:, 256:512]
        out[:, B_AT + 256 : B_AT + 768] = v


def pack_rest_kernel(wo, w1, w2, own, sibling, shuffled):
    c = lax.axis_index("c")
    rows = jnp.concatenate(
        [w1[:, s * 512 : (s + 1) * 512].astype(F32) for s in range(8)], axis=0
    ).astype(BF)
    lane = lax.broadcasted_iota(jnp.int32, (512, 512), 0)
    out = lax.broadcasted_iota(jnp.int32, (512, 512), 1)
    match = (lane >> 5) == ((out & 127) >> 3)
    match = match & (((lane & 31) >> 3) == (out >> 7)) & ((lane & 7) == (out & 7))
    mixed = jnp.dot(rows, jnp.where(match, 1.0, 0.0).astype(BF), preferred_element_type=F32)
    for s in range(8):
        for part in range(4):
            shuffled[part, :, s * 128 : (s + 1) * 128] = mixed[
                s * 8 : (s + 1) * 8, part * 128 : (part + 1) * 128
            ]
    for half, rest in ((c, own), (1 - c, sibling)):
        for g in range(2):
            at = A_FIRST + g * D
            rest[:, at : at + D] = shuffled[2 * half + g].astype(BF)
            at = B_AT + B_FIRST + g * D
            rest[:, at : at + D] = w2[2 * half + g]
        rest[:, 896:A_FIRST] = wo[:, :HALF]
        rest[:, B_AT + 768 : B_AT + B_FIRST] = wo[:, HALF:]


def pack_kernel(*refs):
    first, rest = refs[:6], refs[6:9]
    own, sibling = refs[9:11]
    rows, shuffled = refs[11:]
    pack_first_kernel(*first, own, sibling, rows)
    pack_rest_kernel(*rest, own, sibling, shuffled)


def pack(joint, gains, shifts, offsets, biases, expand_bias, wo, w1, w2):
    return pl.pallas_call(
        pack_kernel,
        out_shape=[jax.ShapeDtypeStruct((8, B_AT + B_FIRST + HID), BF)] * 2,
        in_specs=[VMEM] * 9,
        out_specs=[VMEM] * 2,
        scratch_shapes=[pltpu.VMEM((128, 128), F32), pltpu.VMEM((4, 8, D), F32)],
        cost_estimate=cost(2 * 64 * 512 * 512, 700_000),
    )(joint, gains, shifts, offsets, biases, expand_bias.reshape(1, 32), wo, w1, w2.reshape(4, 8, D))


def chip_rows(own, sibling):
    return jnp.concatenate([own, from_sibling(sibling)], axis=0)


def assemble_z(pieces, widths):
    total = sum(widths)

    def kernel(*refs):
        outs, rows = refs[4:-1], refs[-1]
        c = lax.axis_index("c")
        for step in range(4):
            zl, zh = place_of("z", step)
            rows[zl, 2 * c + zh] = refs[step][0:8].astype(F32)
            rows[zl, 2 * (1 - c) + zh] = refs[step][8:16].astype(F32)
        for zl in range(2):
            at = 0
            for out, width in zip(outs, widths, strict=True):
                out[zl] = rows[zl, :, :, at : at + width].reshape(32, width).astype(BF)
                at += width

    return pl.pallas_call(
        kernel,
        out_shape=[jax.ShapeDtypeStruct((2, 32, width), BF) for width in widths],
        in_specs=[VMEM] * 4,
        out_specs=[VMEM] * len(widths),
        scratch_shapes=[pltpu.VMEM((2, 4, 8, total), F32)],
        cost_estimate=cost(0, 4 * 64 * total),
    )(*pieces)


def assemble_second(a_pieces, b_pieces, starts, widths):
    def kernel(*refs):
        outs = refs[8:]
        for n, axis in enumerate(("y", "x")):
            cols = slice(starts[n], starts[n] + widths[n])
            for step in range(4):
                spot = turn_of(axis, step)
                for zl in range(2):
                    outs[n][zl, spot] = refs[4 * n + step][zl, :, cols]

    return pl.pallas_call(
        kernel,
        out_shape=[jax.ShapeDtypeStruct((2, 4, 32, width), BF) for width in widths],
        in_specs=[VMEM] * 8,
        out_specs=[VMEM] * 2,
        compiler_params=pltpu.CompilerParams(vmem_limit_bytes=VMEM_LIMIT),
        cost_estimate=cost(0, 4 * 256 * sum(widths)),
    )(*a_pieces, *b_pieces)


def together(*arrays):
    return lax.optimization_barrier(arrays)


def dot(left, right):
    return jnp.dot(left, right, preferred_element_type=F32)


def dot_last(left, right):
    return lax.dot_general(left, right, (((1,), (1,)), ((), ())), preferred_element_type=F32)


def dot_first(left, right):
    return lax.dot_general(left, right, (((0,), (0,)), ((), ())), preferred_element_type=F32)


def normalise(rows):
    centered = rows - jnp.mean(rows, axis=-1, keepdims=True)
    inverse = lax.rsqrt(jnp.mean(centered * centered, axis=-1, keepdims=True) + EPS)
    return centered * inverse, inverse


def norm_back(upstream, normed, inverse, gain):
    scaled = upstream * gain
    return inverse * (
        scaled
        - jnp.mean(scaled, axis=-1, keepdims=True)
        - normed * jnp.mean(scaled * normed, axis=-1, keepdims=True)
    )


def start_all(copies):
    for copy in copies:
        copy.start()


def wait_all(copies):
    for copy in copies:
        copy.wait()


def own_half():
    c = lax.axis_index("c")
    own = pl.ds(pl.multiple_of(c * HALF, HALF), HALF)
    other = pl.ds(pl.multiple_of((1 - c) * HALF, HALF), HALF)
    return own, other


ROWS = 256


def joint_copies(a_pieces, b_pieces, joint, sem):
    copies = []
    for step in range(4):
        x, y = turn_of("x", step), turn_of("y", step)
        a, b = a_pieces[step].at[:, :, :, 0:768], b_pieces[step].at[:, :, :, 0:768]
        copies += [
            pltpu.make_async_copy(a, joint.at[:, x, :, :, 0:768], sem.at[step]),
            pltpu.make_async_copy(b, joint.at[:, :, y, :, 768:1536], sem.at[4 + step]),
        ]
    return copies


def output_copies(a_pieces, b_pieces, wo, sem):
    copies = []
    for step in range(4):
        x, y = turn_of("x", step), turn_of("y", step)
        a, b = a_pieces[step].at[:, :, :, 896:], b_pieces[step].at[:, :, :, 768:]
        copies += [
            pltpu.make_async_copy(a, wo.at[:, x, :, :, 0:HALF], sem.at[step]),
            pltpu.make_async_copy(b, wo.at[:, :, y, :, HALF:D], sem.at[4 + step]),
        ]
    return copies


def project_kernel(*refs):
    tok_own, tok_sib = refs[:2]
    a_pieces, b_pieces = refs[2:6], refs[6:10]
    down, raised = refs[10:12]
    q_t, k, k_t, v, v_t, low_t, n1, vec_out = refs[12:20]
    tok, joint, vec, sem = refs[20:]
    own, other = own_half()
    i = pl.program_id(0)
    tokens = [
        pltpu.make_async_copy(tok_own.at[0:HALF], tok.at[own], sem.at[0]),
        pltpu.make_async_copy(tok_sib.at[0:HALF], tok.at[other], sem.at[1]),
    ]
    vectors = [
        pltpu.make_async_copy(
            a_pieces[step].at[:, :, :, 768:896], vec.at[:, turn_of("x", step)], sem.at[2 + step]
        )
        for step in range(4)
    ]
    weights = joint_copies(a_pieces, b_pieces, joint, sem.at[pl.ds(6, 8)])

    @pl.when(i == 0)
    def _():
        start_all(vectors)
        start_all(tokens)
        start_all(weights)
        wait_all(vectors)
        vec_out[...] = jnp.transpose(vec[...].reshape(D, 128).astype(F32))[:16]
        wait_all(tokens)

    rows = pl.ds(pl.multiple_of(i * ROWS, ROWS), ROWS)
    normed, _ = normalise(tok[rows].astype(F32))
    normed = (normed * vec_out[0:1] + vec_out[2:3]).astype(BF)
    n1[...] = normed
    reduced = dot_last(normed, down[...]).astype(BF)
    low_t[...] = jnp.transpose(reduced)[:16]
    added = dot(reduced, raised[...])

    @pl.when(i == 0)
    def _():
        wait_all(weights)

    both = dot(normed, joint[...].reshape(D, 3 * HALF))
    q = (both[:, :512] + vec_out[4:5, own] + added[:, :512]).astype(BF) * 0.125
    q_t[...] = jnp.transpose(q.astype(BF))
    key = both[:, 512:1024].astype(BF)
    k[...] = key
    k_t[...] = jnp.transpose(key)
    value = (both[:, 1024:] + vec_out[5:6, own] + added[:, 512:]).astype(BF)
    v[...] = value
    v_t[...] = jnp.transpose(value)


def project(tok_own, tok_sib, a_pieces, b_pieces, down, raised):
    shape = jax.ShapeDtypeStruct
    down_rows = pl.BlockSpec((ROWS, HALF), lambda i: (i, 0))
    across = pl.BlockSpec((HALF, ROWS), lambda i: (0, i))
    wide, tall = shape((HALF, D), BF), shape((D, HALF), BF)
    return pl.pallas_call(
        project_kernel,
        grid=(D // ROWS,),
        out_shape=[wide, tall, wide, tall, wide, shape((16, D), BF), shape((D, D), BF), shape((16, D), F32)],
        in_specs=[HBM] * 10 + [pl.BlockSpec((128, D), lambda i: (0, 0))] * 2,
        out_specs=[
            across,
            down_rows,
            across,
            down_rows,
            across,
            pl.BlockSpec((16, ROWS), lambda i: (0, i)),
            pl.BlockSpec((ROWS, D), lambda i: (i, 0)),
            pl.BlockSpec((16, D), lambda i: (0, 0)),
        ],
        scratch_shapes=[
            pltpu.VMEM((D, D), BF),
            pltpu.VMEM((2, 4, 4, 32, 3 * HALF), BF),
            pltpu.VMEM((2, 4, 4, 32, 128), BF),
            pltpu.SemaphoreType.DMA((14,)),
        ],
        compiler_params=pltpu.CompilerParams(vmem_limit_bytes=VMEM_LIMIT),
        cost_estimate=cost(2 * D * D * 1536, 16e6),
    )(tok_own, tok_sib, *a_pieces, *b_pieces, down, raised)


def only_head(head, pair):
    zeros = jnp.zeros((64, pair.shape[1]), pair.dtype)
    part = pair[64 * head : 64 * head + 64]
    return jnp.concatenate([zeros, part] if head else [part, zeros], axis=0)


def attend_heads(q_t, k, k_t, v_t, out, exps, inverse, exact):
    first, second = slice(0, HALF), slice(HALF, D)
    causal = lax.broadcasted_iota(jnp.int32, (HALF, HALF), 0) <= lax.broadcasted_iota(
        jnp.int32, (HALF, HALF), 1
    )
    most = jnp.full((1, HALF), -1e30, F32)
    for head in range(2):
        dims = slice(64 * head, 64 * head + 64)
        q_head = only_head(head, q_t[...])
        level = jnp.sum(q_t[dims].astype(F32) * k_t[dims].astype(F32), axis=0, keepdims=True)
        scores = dot(k[first], q_head)
        one = jnp.where(causal, scores[:, first], -1e30)
        two = scores[:, second]
        three = jnp.where(causal, dot(k[second], q_head[:, second]), -1e30)
        level_one, level_two = level[:, first], level[:, second]
        if exact:
            level_one = jnp.max(one, axis=0, keepdims=True)
            level_two = jnp.max(jnp.maximum(two, three), axis=0, keepdims=True)
        one, two, three = one - level_one, two - level_two, three - level_two
        for part in (one, two, three):
            most = jnp.maximum(most, jnp.max(part, axis=0, keepdims=True))
        one, two, three = jnp.exp(one), jnp.exp(two), jnp.exp(three)
        scale_one = 1.0 / jnp.sum(one, axis=0, keepdims=True)
        scale_two = 1.0 / (
            jnp.sum(two, axis=0, keepdims=True) + jnp.sum(three, axis=0, keepdims=True)
        )
        for n, part in enumerate((one, two, three)):
            exps[head, n] = part.astype(BF)
        inverse[0, head : head + 1, first] = scale_one
        inverse[0, head : head + 1, second] = scale_two
        out[dims, first] = dot(v_t[dims, first], exps[head, 0]) * scale_one
        total = dot(v_t[dims, first], exps[head, 1]) + dot(v_t[dims, second], exps[head, 2])
        out[dims, second] = total * scale_two
    return jnp.max(most)


def attend_kernel(q_t, k, k_t, v_t, out_own, out_sib, out, exps, inverse):
    args = (q_t, k, k_t, v_t, out, exps, inverse)
    most = attend_heads(*args, False)

    @pl.when(most > 60.0)
    def _():
        attend_heads(*args, True)

    own, other = own_half()
    out_own[...] = out[:, own].astype(BF)
    out_sib[...] = out[:, other].astype(BF)


def attend(q_t, k, k_t, v_t):
    shape = jax.ShapeDtypeStruct
    wide = pl.BlockSpec((128, D), lambda j: (j, 0))
    halves = pl.BlockSpec((128, HALF), lambda j: (j, 0))
    return pl.pallas_call(
        attend_kernel,
        grid=(4,),
        out_shape=[
            shape((HALF, HALF), BF),
            shape((HALF, HALF), BF),
            shape((HALF, D), F32),
            pltpu.HBM((8, 3, HALF, HALF), BF),
            shape((4, 8, D), F32),
        ],
        in_specs=[wide, pl.BlockSpec((D, 128), lambda j: (0, j)), wide, wide],
        out_specs=[
            halves,
            halves,
            wide,
            pl.BlockSpec((2, 3, HALF, HALF), lambda j: (j, 0, 0, 0)),
            pl.BlockSpec((1, 8, D), lambda j: (j, 0, 0)),
        ],
        compiler_params=pltpu.CompilerParams(vmem_limit_bytes=VMEM_LIMIT),
        cost_estimate=cost(8e9, 20e6, 8 * D * D),
    )(q_t, k, k_t, v_t)


def attend_back_kernel(*refs):
    q_t, k_t, v, d_own, d_sib, out, exps, inverse, low_t, n1_in, raised, down = refs[:12]
    a_pieces, b_pieces = refs[12:16], refs[16:20]
    sums, part_own, part_sib = refs[20:23]
    dq_t, dk_t, dv_t, d_scores, d_low, grads, n1, joint, sem = refs[23:]
    copies = joint_copies(a_pieces, b_pieces, joint, sem.at[pl.ds(1, 8)])
    copies.append(pltpu.make_async_copy(n1_in, n1, sem.at[0]))

    c = lax.axis_index("c")
    own, other = own_half()
    step = pl.program_id(0)

    @pl.when(step == 0)
    def _():
        start_all(copies)

    low, high = jnp.where(c == 0, d_own[...], d_sib[...]), jnp.where(c == 0, d_sib[...], d_own[...])
    d_out = jnp.concatenate([low, high], axis=1).astype(F32)
    weighted = d_out * out[...]
    first, second = slice(0, HALF), slice(HALF, D)
    for head in range(2):
        dims = slice(64 * head, 64 * head + 64)
        scale = inverse[0, head : head + 1]
        mean = jnp.sum(weighted[dims], axis=0, keepdims=True) * scale
        scaled = (d_out * scale).astype(BF)
        d_head = only_head(head, scaled)
        d_probs = dot(v[first], d_head)
        parts = (
            d_probs[:, first] - mean[:, first],
            d_probs[:, second] - mean[:, second],
            dot(v[second], d_head[:, second]) - mean[:, second],
        )
        for n, part in enumerate(parts):
            d_scores[n] = (exps[head, n].astype(F32) * part).astype(BF)
        key, query, d_value = k_t[dims], q_t[dims], scaled[dims]
        dq_t[dims, first] = (dot(key[:, first], d_scores[0]) * 0.125).astype(BF)
        total = dot(key[:, first], d_scores[1]) + dot(key[:, second], d_scores[2])
        dq_t[dims, second] = (total * 0.125).astype(BF)
        total = dot_last(query[:, first], d_scores[0]) + dot_last(query[:, second], d_scores[1])
        dk_t[dims, first] = total.astype(BF)
        dk_t[dims, second] = dot_last(query[:, second], d_scores[2]).astype(BF)
        total = dot_last(d_value[:, first], exps[head, 0])
        total += dot_last(d_value[:, second], exps[head, 1])
        dv_t[dims, first] = total.astype(BF)
        dv_t[dims, second] = dot_last(d_value[:, second], exps[head, 2]).astype(BF)
    cols = pl.ds(pl.multiple_of(step * 128, 128), 128)
    value_cols = pl.ds(pl.multiple_of(HALF + step * 128, 128), 128)
    part = dot(raised[:16, cols], dq_t[...]) + dot(raised[:16, value_cols], dv_t[...])
    at = pl.ds(pl.multiple_of(c * HALF + step * 128, 128), 128)
    top = lax.broadcasted_iota(jnp.int32, (8, 128), 0) < 4
    from_q = dot_last(low_t[...], dq_t[...])[:8] * ADAPTER_SCALE
    from_v = dot_last(low_t[...], dv_t[...])[:8] * ADAPTER_SCALE

    @pl.when(step == 0)
    def _():
        d_low[...] = part
        sums[8:16] = jnp.zeros((8, D), F32)

    @pl.when(step > 0)
    def _():
        d_low[...] += part

    sums[8:16, at] = jnp.where(top, from_q, from_v)
    for n, grad in enumerate((dq_t, dk_t, dv_t)):
        at = pl.ds(pl.multiple_of(n * HALF + step * 128, 128), 128)
        grads[:, at] = jnp.transpose(grad[...])

    @pl.when(step == 3)
    def _():
        wait_all(copies)
        low = d_low[...].astype(BF)
        sums[0:8] = dot(low, n1[...])[:8]
        low = jnp.transpose(low)
        n1[:, 0:16] = low
        for rows, part in ((other, part_sib), (own, part_own)):
            total = dot_last(grads[rows], joint[...].reshape(D, 3 * HALF))
            total += dot(n1[rows, 0:16], down[:16])
            part[...] = total.astype(part.dtype)


def attend_back(q_t, k_t, v, d_own, d_sib, out, exps, inverse, low_t, n1, raised, down, a_pieces, b_pieces):
    shape = jax.ShapeDtypeStruct
    wide = pl.BlockSpec((128, D), lambda j: (j, 0))
    halves = pl.BlockSpec((128, HALF), lambda j: (j, 0))

    def whole(rows):
        return pl.BlockSpec((rows, D), lambda j: (0, 0))

    return pl.pallas_call(
        attend_back_kernel,
        grid=(4,),
        out_shape=[shape((16, D), F32), shape((HALF, D), F32), shape((HALF, D), BF)],
        in_specs=[
            wide,
            wide,
            pl.BlockSpec((D, 128), lambda j: (0, j)),
            halves,
            halves,
            wide,
            pl.BlockSpec((2, 3, HALF, HALF), lambda j: (j, 0, 0, 0)),
            pl.BlockSpec((1, 8, D), lambda j: (j, 0, 0)),
            whole(16),
            ANY,
            whole(128),
            whole(128),
        ]
        + [ANY] * 8,
        out_specs=[whole(16), whole(HALF), whole(HALF)],
        scratch_shapes=[pltpu.VMEM((128, D), BF)] * 3
        + [
            pltpu.VMEM((3, HALF, HALF), BF),
            pltpu.VMEM((16, D), F32),
            pltpu.VMEM((D, 3 * HALF), BF),
            pltpu.VMEM((D, D), BF),
            pltpu.VMEM((2, 4, 4, 32, 3 * HALF), BF),
            pltpu.SemaphoreType.DMA((9,)),
        ],
        compiler_params=pltpu.CompilerParams(vmem_limit_bytes=VMEM_LIMIT),
        cost_estimate=cost(20e9, 30e6),
    )(
        q_t, k_t, v, d_own, d_sib, out, pltpu.with_memory_space_constraint(exps, pltpu.HBM), inverse, low_t,
        n1, raised, down, *a_pieces, *b_pieces,
    )


PART = 256


def after_attention_kernel(*refs):
    mixed_own, mixed_other, tok, vec = refs[:4]
    a_pieces, b_pieces = refs[4:8], refs[8:12]
    residual, n2 = refs[12:14]
    wo, sem = refs[14:]
    copies = output_copies(a_pieces, b_pieces, wo, sem)

    @pl.when(pl.program_id(0) == 0)
    def _():
        start_all(copies)
        wait_all(copies)

    weights = wo[...].reshape(D, D)
    c = lax.axis_index("c")
    low = jnp.where(c == 0, mixed_own[...], mixed_other[...])
    high = jnp.where(c == 0, mixed_other[...], mixed_own[...])
    attended = dot_first(low, weights[:HALF]) + dot_first(high, weights[HALF:])
    rows = tok[...].astype(F32) + attended + vec[6:7]
    residual[...] = rows
    normed, _ = normalise(rows)
    n2[...] = (normed * vec[1:2] + vec[3:4]).astype(BF)


def after_attention(mixed_own, mixed_other, tok, vec, a_pieces, b_pieces):
    shape = jax.ShapeDtypeStruct
    across = pl.BlockSpec((HALF, PART), lambda i: (0, i))
    rows = pl.BlockSpec((PART, D), lambda i: (i, 0))
    return pl.pallas_call(
        after_attention_kernel,
        grid=(HALF // PART,),
        out_shape=[shape((HALF, D), F32), shape((HALF, D), BF)],
        in_specs=[across, across, rows, pl.BlockSpec((16, D), lambda i: (0, 0))] + [ANY] * 8,
        out_specs=[rows, rows],
        scratch_shapes=[pltpu.VMEM((2, 4, 4, 32, D), BF), pltpu.SemaphoreType.DMA((8,))],
        compiler_params=pltpu.CompilerParams(vmem_limit_bytes=VMEM_LIMIT),
        cost_estimate=cost(2 * HALF * D * D, 12e6),
    )(mixed_own, mixed_other, tok, vec, *a_pieces, *b_pieces)


def feed_forward_kernel(*refs):
    n2, cot, vec = refs[:3]
    a_pieces, b_pieces = refs[3:7], refs[7:11]
    out, d_n2 = refs[11:13]
    w1, w2, hidden, d_gate, sem = refs[13:]
    chunks = HID // CHUNK
    copies = []
    for j in range(chunks):
        cols = slice(j * CHUNK, (j + 1) * CHUNK)
        group, part = j // 2, j % 2
        wide = slice(group * D, (group + 1) * D)
        some = []
        for step in range(4):
            x, y = turn_of("x", step), turn_of("y", step)
            some.append((a_pieces[step].at[:, :, :, cols], w1.at[:, x, :, :, cols]))
            some.append((b_pieces[step].at[part, :, :, wide], w2.at[j, :, y]))
        copies.append(
            [pltpu.make_async_copy(s, d, sem.at[j, n]) for n, (s, d) in enumerate(some)]
        )
    start_all(copies[0])
    start_all(copies[1])
    c = lax.axis_index("c")
    for j in range(chunks):
        wait_all(copies[j])
        if j + 2 < chunks:
            start_all(copies[j + 2])
        g, part = j // 2, j % 2
        bias = vec[pl.ds(8 + 2 * c + g, 1), part * CHUNK : (part + 1) * CHUNK]
        cols = slice(j * CHUNK, (j + 1) * CHUNK)
        u = dot(n2[...], w1[..., cols].reshape(D, CHUNK)) + bias
        square = u * u
        t = jnp.tanh(u * (0.7978845608028654 + 0.7978845608028654 * 0.044715 * square))
        half = 0.5 * u
        more = 1.0 + t
        hidden[:, cols] = (half * more).astype(BF)
        slope = 0.5 * more + half * (1.0 - t * t) * (
            0.7978845608028654 + 3 * 0.7978845608028654 * 0.044715 * square
        )
        d_gate[:, cols] = (dot_last(cot[...], w2[j].reshape(CHUNK, D)) * slope).astype(BF)
    d_n2[...] = dot_last(d_gate[...], w1[...].reshape(D, HID)).astype(d_n2.dtype)
    out[...] = dot(hidden[...], w2[...].reshape(HID, D)).astype(out.dtype)


def feed_forward(n2, cot, vec, a_pieces, b_pieces):
    return pl.pallas_call(
        feed_forward_kernel,
        grid=(1,),
        out_shape=[jax.ShapeDtypeStruct((HALF, D), BF)] * 2,
        in_specs=[
            pl.BlockSpec((HALF, D), lambda i: (0, 0)),
            pl.BlockSpec((HALF, D), lambda i: (1, 0)),
            pl.BlockSpec((16, D), lambda i: (0, 0)),
        ]
        + [ANY] * 8,
        out_specs=[pl.BlockSpec((HALF, D), lambda i: (0, 0))] * 2,
        scratch_shapes=[
            pltpu.VMEM((2, 4, 4, 32, HID), BF),
            pltpu.VMEM((4, 4, 4, 32, D), BF),
            pltpu.VMEM((HALF, HID), BF),
            pltpu.VMEM((HALF, HID), BF),
            pltpu.SemaphoreType.DMA((4, 8)),
        ],
        compiler_params=pltpu.CompilerParams(vmem_limit_bytes=VMEM_LIMIT),
        cost_estimate=cost(8 * HALF * D * HID, 16e6, HALF * HID),
    )(n2, cot, vec, *a_pieces, *b_pieces)


def before_attention_kernel(*refs):
    residual, cot, d_own, d_recv, vec = refs[:5]
    a_pieces, b_pieces = refs[5:9], refs[9:13]
    d_residual, d_mixed_own, d_mixed_sib = refs[13:16]
    wo, sem = refs[16:]
    copies = output_copies(a_pieces, b_pieces, wo, sem)

    @pl.when(pl.program_id(0) == 0)
    def _():
        start_all(copies)

    normed, inverse = normalise(residual[...])
    d_n2 = d_own[...].astype(F32) + d_recv[...].astype(F32)
    d_rows = cot[...].astype(F32) + norm_back(d_n2, normed, inverse, vec[1:2])
    d_residual[...] = d_rows
    d_attended = d_rows.astype(BF)

    @pl.when(pl.program_id(0) == 0)
    def _():
        wait_all(copies)

    d_mixed = dot_last(wo[...].reshape(D, D), d_attended).astype(BF)
    first = lax.axis_index("c") == 0
    d_mixed_own[...] = jnp.where(first, d_mixed[:HALF], d_mixed[HALF:])
    d_mixed_sib[...] = jnp.where(first, d_mixed[HALF:], d_mixed[:HALF])


def before_attention(residual, cot, d_own, d_recv, vec, a_pieces, b_pieces):
    shape = jax.ShapeDtypeStruct
    rows = pl.BlockSpec((PART, D), lambda i: (i, 0))
    later = pl.BlockSpec((PART, D), lambda i: (i + HALF // PART, 0))
    across = pl.BlockSpec((HALF, PART), lambda i: (0, i))
    return pl.pallas_call(
        before_attention_kernel,
        grid=(HALF // PART,),
        out_shape=[shape((HALF, D), F32), shape((HALF, HALF), BF), shape((HALF, HALF), BF)],
        in_specs=[rows, later, rows, rows, pl.BlockSpec((16, D), lambda i: (0, 0))] + [ANY] * 8,
        out_specs=[rows, across, across],
        scratch_shapes=[pltpu.VMEM((2, 4, 4, 32, D), BF), pltpu.SemaphoreType.DMA((8,))],
        compiler_params=pltpu.CompilerParams(vmem_limit_bytes=VMEM_LIMIT),
        cost_estimate=cost(2 * HALF * D * D, 12e6),
    )(residual, cot, d_own, d_recv, vec, *a_pieces, *b_pieces)


def input_kernel(tok, d_residual, part, recv, vec, out):
    normed, inverse = normalise(tok[...].astype(F32))
    d_n1 = part[...] + recv[...].astype(F32)
    out[...] = (d_residual[...] + norm_back(d_n1, normed, inverse, vec[0:1])).astype(BF)


def input_rows(tok, d_residual, part, recv, vec):
    rows = pl.BlockSpec((PART, D), lambda i: (i, 0))
    return pl.pallas_call(
        input_kernel,
        grid=(HALF // PART,),
        out_shape=jax.ShapeDtypeStruct((HALF, D), BF),
        in_specs=[rows] * 4 + [pl.BlockSpec((16, D), lambda i: (0, 0))],
        out_specs=rows,
        compiler_params=pltpu.CompilerParams(vmem_limit_bytes=VMEM_LIMIT),
        cost_estimate=cost(0, 8e6),
    )(tok, d_residual, part, recv, vec)


def local(
    tokens,
    norm_gains,
    norm_shifts,
    query_value_offsets_bias,
    output_biases,
    expand_bias,
    joint_weight,
    output_weight,
    expand_weight,
    shrink_weight,
    query_down,
    query_raise_factor,
    value_down,
    value_raise_factor,
    cotangent,
):
    own, sibling = pack(
        joint_weight,
        norm_gains,
        norm_shifts,
        query_value_offsets_bias,
        output_biases,
        expand_bias,
        output_weight,
        expand_weight,
        shrink_weight,
    )
    a, b = assemble_z(ring(chip_rows(own, sibling), ZRING), (B_AT, B_FIRST + HID))
    a, b, rows = together(a, b, jnp.concatenate([tokens, cotangent], axis=0))
    rows = lax.ppermute(rows, PAIR, SWAP)
    a_near, b_near = together(near(a, "y"), near(b, "x"))
    a_far, b_far = ahead(a_near[0], "y"), ahead(b_near[0], "x")
    a_pieces = (a, a_near[0], a_far, a_near[1])
    b_pieces = (b, b_near[0], b_far, b_near[1])
    joint_a, joint_b = assemble_second(a_pieces, b_pieces, (0, 0), (A_FIRST, B_FIRST))
    joint_a, joint_b, rows = together(joint_a, joint_b, rows)
    rows_sib = from_sibling(rows)
    a, b = assemble_second(a_pieces, b_pieces, (A_FIRST, B_FIRST), (HID, HID))
    a_near, b_near = near(joint_a, "x"), near(joint_b, "y")
    a_near, b_near, rows_sib, a, b = together(a_near, b_near, rows_sib, a, b)
    a_far, b_far = ahead(a_near[0], "x"), ahead(b_near[0], "y")
    joint_a = (joint_a, a_near[0], a_far, a_near[1])
    joint_b = (joint_b, b_near[0], b_far, b_near[1])

    *joint, a, b = together(*joint_a, *joint_b, a, b)
    joint_a, joint_b = joint[:4], joint[4:]

    c = lax.axis_index("c")
    down = jnp.pad(jnp.concatenate([query_down.T, value_down.T], axis=0), ((0, 120), (0, 0)))
    raise_q = lax.dynamic_slice_in_dim(query_raise_factor, c * HALF, HALF, axis=1)
    raise_v = lax.dynamic_slice_in_dim(value_raise_factor, c * HALF, HALF, axis=1)
    raised = ADAPTER_SCALE * jnp.concatenate(
        [jnp.pad(raise_q, ((0, 124), (0, 0))), jnp.pad(raise_v, ((4, 120), (0, 0)))], axis=1
    )
    raised = raised.astype(BF)

    q_t, k, k_t, v, v_t, low_t, n1, vec = project(rows, rows_sib, joint_a, joint_b, down, raised)
    a_near, b_near = near(a, "x"), near(b, "y")
    mixed_own, mixed_sib, out, exps, inverse = attend(q_t, k, k_t, v_t)
    mixed_sib, a_near, b_near = together(mixed_sib, a_near, b_near)
    mixed_other = from_sibling(mixed_sib)
    a_far, b_far = ahead(a_near[0], "x"), ahead(b_near[0], "y")
    a_pieces = (a, a_near[0], a_far, a_near[1])
    b_pieces = (b, b_near[0], b_far, b_near[1])
    residual, n2 = after_attention(mixed_own, mixed_other, rows, vec, joint_a, joint_b)
    n2_sib = from_sibling(n2)
    out_own, d_own = feed_forward(n2, rows, vec, a_pieces, b_pieces)
    out_sib, d_sib = feed_forward(n2_sib, rows_sib, vec, a_pieces, b_pieces)
    d_recv = from_sibling(d_sib)
    out_recv = from_sibling(out_sib)
    d_residual, d_mixed_own, d_mixed_sib = before_attention(
        residual, rows, d_own, d_recv, vec, joint_a, joint_b
    )
    block_rows = (residual + out_own.astype(F32) + out_recv.astype(F32) + vec[7]).astype(BF)
    d_mixed_other = from_sibling(d_mixed_sib)
    q_t, block_rows = together(q_t, block_rows)
    block_output = lax.ppermute(block_rows, PAIR, SWAP)
    sums, part_own, part_sib = attend_back(
        q_t, k_t, v, d_mixed_own, d_mixed_other, out, exps, inverse, low_t, n1, raised, down, joint_a, joint_b
    )
    part_sib, sums, block_output = together(part_sib, sums, block_output)
    part_recv = from_sibling(part_sib)
    sums = sums + from_sibling(sums)
    part_recv, sums = together(part_recv, sums)
    sums = ring(sums, ZRING)
    grad = input_rows(rows, d_residual, part_own, part_recv, vec)
    grad, sums = together(grad, sums)
    sums = ring(ring_sum(sums), "x")
    input_grad = lax.ppermute(grad, PAIR, SWAP).astype(F32)
    sums = ring_sum(ring(ring_sum(sums), "y")) / 64.0
    return (
        block_output,
        input_grad,
        sums[0:4].T,
        sums[8:12],
        sums[4:8].T,
        sums[12:16],
    )


def solution(mesh):
    fine = Mesh(mesh.devices.reshape(2, 4, 4, 2, 2), AXES)
    rows, columns = P(AXES, None), P(None, AXES)
    placed = (
        (rows,) + (columns,) * 4 + (P(AXES),) + (rows,) * 4 + (P(),) * 4 + (rows,)
    )
    return jax.shard_map(
        local,
        mesh=fine,
        in_specs=placed,
        out_specs=(rows, rows, P(), P(), P(), P()),
        check_vma=False,
    )
```

```python
import math

import jax
import jax.numpy as jnp
from jax import lax
from jax.experimental import pallas as pl
from jax.experimental.pallas import tpu as pltpu
from jax.sharding import Mesh, PartitionSpec as P

AXES = ("zl", "x", "y", "c", "zh")
PAIR = ("c", "zh")
ZRING = ("zl", "zh")
Z_PLACE = (0, 2, 1, 3)
SWAP = [(0, 0), (1, 2), (2, 1), (3, 3)]
FLIP = [(0, 1), (1, 0)]
FROM_NEXT = [(i, (i - 1) % 4) for i in range(4)]
FROM_PREV = [(i, (i + 1) % 4) for i in range(4)]
FROM_OPPOSITE = [(i, (i + 2) % 4) for i in range(4)]

EPS = 1e-05
ADAPTER_SCALE = 8.0
D = 1024
HALF = 512
HID = 2048
CHUNK = 512
A_FIRST = 1152
B_FIRST = 1024
B_AT = A_FIRST + HID
VMEM_LIMIT = 24 * 2**20
BF = jnp.bfloat16
F32 = jnp.float32

ANY = pl.BlockSpec(memory_space=pl.ANY)
VMEM = pl.BlockSpec(memory_space=pltpu.VMEM)


def permute(value, axis, pairs):
    if axis == ZRING:
        pairs = [(Z_PLACE[i], Z_PLACE[j]) for i, j in pairs]
    return lax.ppermute(value, axis, pairs)


def from_sibling(value):
    return lax.ppermute(value, "c", FLIP)


def ring(value, axis):
    return (
        value,
        permute(value, axis, FROM_NEXT),
        permute(value, axis, FROM_OPPOSITE),
        permute(value, axis, FROM_PREV),
    )


def parity_pairs(axis, back):
    pairs = []
    for i in range(4):
        for c in range(2):
            j = (i + (1 if (c == 0) != back else -1)) % 4
            if axis == ZRING:
                i_at, j_at = (4 * (i % 2) + 2 * c + i // 2, 4 * (j % 2) + 2 * c + j // 2)
            else:
                i_at, j_at = 2 * i + c, 2 * j + c
            pairs.append((i_at, j_at))
    return pairs


def ahead(value, axis):
    names = ("zl", "c", "zh") if axis == ZRING else (axis, "c")
    return lax.ppermute(value, names, parity_pairs(axis, False))


def near(value, axis):
    names = ("zl", "c", "zh") if axis == ZRING else (axis, "c")
    return ahead(value, axis), lax.ppermute(value, names, parity_pairs(axis, True))


def ring_sum(pieces):
    own, after, opposite, before = pieces
    return (own + opposite) + (after + before)


def places():
    z = lax.axis_index("zh") * 2 + lax.axis_index("zl")
    return {"x": lax.axis_index("x"), "y": lax.axis_index("y"), "z": z}


def place_of(axis, step):
    spot = lax.rem(places()[axis] + step, 4)
    if axis == "z":
        return lax.rem(spot, 2), lax.div(spot, 2)
    return (spot,)


def turn_of(axis, step):
    way = 1 + 2 * lax.axis_index("c") if step % 2 else 1
    return lax.rem(places()[axis] + (4 - step) * way, 4)


def cost(flops, nbytes, transcendentals=0):
    return pl.CostEstimate(
        flops=int(flops), bytes_accessed=int(nbytes), transcendentals=int(transcendentals)
    )


def pack_first_kernel(
    joint, gains, shifts, offsets, biases, expand_bias, own, sibling, rows
):
    c = lax.axis_index("c")
    rows[...] = jnp.zeros_like(rows)
    for at, pair in enumerate((gains, shifts, offsets, biases)):
        rows[2 * at : 2 * at + 2, :8] = pair[...].astype(F32)
    rows[8:9, :32] = expand_bias[...].astype(F32)
    bias = rows[8:16]
    for part in range(1, 4):
        rows[8 + part : 9 + part] = pltpu.roll(bias, 128 - 8 * part, axis=1)[0:1]
    vectors = jnp.transpose(rows[...])[:8].astype(BF)
    for half, out in ((c, own), (1 - c, sibling)):
        q, k, v = [joint[:, pl.ds(pl.multiple_of(n * D + half * HALF, 128), HALF)] for n in range(3)]
        out[:, 0:512] = q
        out[:, 512:768] = k[:, 0:256]
        out[:, 768:896] = vectors
        out[:, B_AT : B_AT + 256] = k[:, 256:512]
        out[:, B_AT + 256 : B_AT + 768] = v


def pack_rest_kernel(wo, w1, w2, own, sibling, shuffled):
    c = lax.axis_index("c")
    rows = jnp.concatenate(
        [w1[:, s * 512 : (s + 1) * 512].astype(F32) for s in range(8)], axis=0
    ).astype(BF)
    lane = lax.broadcasted_iota(jnp.int32, (512, 512), 0)
    out = lax.broadcasted_iota(jnp.int32, (512, 512), 1)
    match = (lane >> 5) == ((out & 127) >> 3)
    match = match & (((lane & 31) >> 3) == (out >> 7)) & ((lane & 7) == (out & 7))
    mixed = jnp.dot(rows, jnp.where(match, 1.0, 0.0).astype(BF), preferred_element_type=F32)
    for s in range(8):
        for part in range(4):
            shuffled[part, :, s * 128 : (s + 1) * 128] = mixed[
                s * 8 : (s + 1) * 8, part * 128 : (part + 1) * 128
            ]
    for half, rest in ((c, own), (1 - c, sibling)):
        for g in range(2):
            at = A_FIRST + g * D
            rest[:, at : at + D] = shuffled[2 * half + g].astype(BF)
            at = B_AT + B_FIRST + g * D
            rest[:, at : at + D] = w2[2 * half + g]
        quarter = pl.multiple_of(half * HALF, 128)
        rest[:, 896:A_FIRST] = wo[:, pl.ds(quarter, 256)]
        rest[:, B_AT + 768 : B_AT + B_FIRST] = wo[:, pl.ds(quarter + 256, 256)]


def pack_kernel(*refs):
    first, rest = refs[:6], refs[6:9]
    own, sibling = refs[9:11]
    rows, shuffled = refs[11:]
    pack_first_kernel(*first, own, sibling, rows)
    pack_rest_kernel(*rest, own, sibling, shuffled)


def pack(joint, gains, shifts, offsets, biases, expand_bias, wo, w1, w2):
    return pl.pallas_call(
        pack_kernel,
        out_shape=[jax.ShapeDtypeStruct((8, B_AT + B_FIRST + HID), BF)] * 2,
        in_specs=[VMEM] * 9,
        out_specs=[VMEM] * 2,
        scratch_shapes=[pltpu.VMEM((128, 128), F32), pltpu.VMEM((4, 8, D), F32)],
        cost_estimate=cost(2 * 64 * 512 * 512, 700_000),
    )(joint, gains, shifts, offsets, biases, expand_bias.reshape(1, 32), wo, w1, w2.reshape(4, 8, D))


def chip_rows(own, sibling):
    return jnp.concatenate([own, from_sibling(sibling)], axis=0)


def assemble_z(pieces, widths):
    total = sum(widths)

    def kernel(*refs):
        outs, rows = refs[4:-1], refs[-1]
        c = lax.axis_index("c")
        for step in range(4):
            zl, zh = place_of("z", step)
            rows[zl, 2 * c + zh] = refs[step][0:8].astype(F32)
            rows[zl, 2 * (1 - c) + zh] = refs[step][8:16].astype(F32)
        for zl in range(2):
            at = 0
            for out, width in zip(outs, widths, strict=True):
                out[zl] = rows[zl, :, :, at : at + width].reshape(32, width).astype(BF)
                at += width

    return pl.pallas_call(
        kernel,
        out_shape=[pltpu.VMEM((2, 32, width), BF) for width in widths],
        in_specs=[VMEM] * 4,
        out_specs=[VMEM] * len(widths),
        scratch_shapes=[pltpu.VMEM((2, 4, 8, total), F32)],
        cost_estimate=cost(0, 4 * 64 * total),
    )(*pieces)


def assemble_second(a_pieces, b_pieces, starts, widths):
    def kernel(*refs):
        outs = refs[8:]
        for n, axis in enumerate(("y", "x")):
            cols = slice(starts[n], starts[n] + widths[n])
            for step in range(4):
                spot = turn_of(axis, step)
                for zl in range(2):
                    outs[n][zl, spot] = refs[4 * n + step][zl, :, cols]

    return pl.pallas_call(
        kernel,
        out_shape=[jax.ShapeDtypeStruct((2, 4, 32, width), BF) for width in widths],
        in_specs=[VMEM] * 8,
        out_specs=[VMEM] * 2,
        compiler_params=pltpu.CompilerParams(vmem_limit_bytes=VMEM_LIMIT),
        cost_estimate=cost(0, 4 * 256 * sum(widths)),
    )(*a_pieces, *b_pieces)


def together(*arrays):
    return lax.optimization_barrier(arrays)


def dot(left, right):
    return jnp.dot(left, right, preferred_element_type=F32)


def dot_last(left, right):
    return lax.dot_general(left, right, (((1,), (1,)), ((), ())), preferred_element_type=F32)


def dot_first(left, right):
    return lax.dot_general(left, right, (((0,), (0,)), ((), ())), preferred_element_type=F32)


def normalise(rows):
    centered = rows - jnp.mean(rows, axis=-1, keepdims=True)
    inverse = lax.rsqrt(jnp.mean(centered * centered, axis=-1, keepdims=True) + EPS)
    return centered * inverse, inverse


def norm_back(upstream, normed, inverse, gain):
    scaled = upstream * gain
    return inverse * (
        scaled
        - jnp.mean(scaled, axis=-1, keepdims=True)
        - normed * jnp.mean(scaled * normed, axis=-1, keepdims=True)
    )


def in_hbm(*arrays):
    return [pltpu.with_memory_space_constraint(a, pltpu.HBM) for a in arrays]


def start_all(copies):
    for copy in copies:
        copy.start()


def wait_all(copies):
    for copy in copies:
        copy.wait()


def own_half():
    c = lax.axis_index("c")
    own = pl.ds(pl.multiple_of(c * HALF, HALF), HALF)
    other = pl.ds(pl.multiple_of((1 - c) * HALF, HALF), HALF)
    return own, other


ROWS = 256


def joint_copies(a_pieces, b_pieces, joint, sem):
    copies = []
    for step in range(4):
        x, y = turn_of("x", step), turn_of("y", step)
        a, b = a_pieces[step].at[:, :, :, 0:768], b_pieces[step].at[:, :, :, 0:768]
        copies += [
            pltpu.make_async_copy(a, joint.at[:, x, :, :, 0:768], sem.at[step]),
            pltpu.make_async_copy(b, joint.at[:, :, y, :, 768:1536], sem.at[4 + step]),
        ]
    return copies


def project_kernel(*refs):
    tok_own, tok_sib = refs[:2]
    a_pieces, b_pieces = refs[2:6], refs[6:10]
    down, raised = refs[10:12]
    q_t, k, k_t, v, v_t, low_t, n1, vec_out, wo = refs[12:21]
    tok, joint, vec, sem = refs[21:]
    own, other = own_half()
    i = pl.program_id(0)
    tokens = [
        pltpu.make_async_copy(tok_own.at[0:HALF], tok.at[own], sem.at[0]),
        pltpu.make_async_copy(tok_sib.at[0:HALF], tok.at[other], sem.at[1]),
    ]
    vectors = [
        pltpu.make_async_copy(
            a_pieces[step].at[:, :, :, 768:896], vec.at[:, turn_of("x", step)], sem.at[2 + step]
        )
        for step in range(4)
    ]
    weights = joint_copies(a_pieces, b_pieces, joint, sem.at[pl.ds(6, 8)])
    outputs = []
    for step in range(4):
        x, y = turn_of("x", step), turn_of("y", step)
        a, b = a_pieces[step].at[:, :, :, 896:], b_pieces[step].at[:, :, :, 768:]
        outputs += [
            pltpu.make_async_copy(a, wo.at[:, x, :, :, 0:256], sem.at[14 + step]),
            pltpu.make_async_copy(b, wo.at[:, :, y, :, 256:512], sem.at[18 + step]),
        ]

    @pl.when(i == 0)
    def _():
        start_all(vectors)
        start_all(tokens)
        start_all(weights)
        start_all(outputs)
        wait_all(vectors)
        vec_out[...] = jnp.transpose(vec[...].reshape(D, 128).astype(F32))[:16]
        wait_all(tokens)

    rows = pl.ds(pl.multiple_of(i * ROWS, ROWS), ROWS)
    normed, _ = normalise(tok[rows].astype(F32))
    normed = (normed * vec_out[0:1] + vec_out[2:3]).astype(BF)
    n1[...] = normed
    reduced = dot_last(normed, down[...]).astype(BF)
    low_t[...] = jnp.transpose(reduced)[:16]
    added = dot(reduced, raised[...])

    @pl.when(i == 0)
    def _():
        wait_all(weights)

    both = dot(normed, joint[...].reshape(D, 3 * HALF))
    q = (both[:, :512] + vec_out[4:5, own] + added[:, :512]).astype(BF) * 0.125
    q_t[...] = jnp.transpose(q.astype(BF))
    key = both[:, 512:1024].astype(BF)
    k[...] = key
    k_t[...] = jnp.transpose(key)
    value = (both[:, 1024:] + vec_out[5:6, own] + added[:, 512:]).astype(BF)
    v[...] = value
    v_t[...] = jnp.transpose(value)

    @pl.when(i == D // ROWS - 1)
    def _():
        wait_all(outputs)


def project(tok_own, tok_sib, a_pieces, b_pieces, down, raised):
    shape = jax.ShapeDtypeStruct
    down_rows = pl.BlockSpec((ROWS, HALF), lambda i: (i, 0))
    across = pl.BlockSpec((HALF, ROWS), lambda i: (0, i))
    wide, tall = shape((HALF, D), BF), shape((D, HALF), BF)
    return pl.pallas_call(
        project_kernel,
        grid=(D // ROWS,),
        out_shape=[wide, tall, wide, tall, wide, shape((16, D), BF), shape((D, D), BF), shape((16, D), F32), shape((2, 4, 4, 32, HALF), BF)],
        in_specs=[ANY] * 10 + [pl.BlockSpec((128, D), lambda i: (0, 0))] * 2,
        out_specs=[
            across,
            down_rows,
            across,
            down_rows,
            across,
            pl.BlockSpec((16, ROWS), lambda i: (0, i)),
            pl.BlockSpec((ROWS, D), lambda i: (i, 0)),
            pl.BlockSpec((16, D), lambda i: (0, 0)),
            pl.BlockSpec((2, 4, 4, 32, HALF), lambda i: (0, 0, 0, 0, 0)),
        ],
        scratch_shapes=[
            pltpu.VMEM((D, D), BF),
            pltpu.VMEM((2, 4, 4, 32, 3 * HALF), BF),
            pltpu.VMEM((2, 4, 4, 32, 128), BF),
            pltpu.SemaphoreType.DMA((22,)),
        ],
        compiler_params=pltpu.CompilerParams(vmem_limit_bytes=VMEM_LIMIT),
        cost_estimate=cost(2 * D * D * 1536, 16e6),
    )(*in_hbm(tok_own, tok_sib, *a_pieces, *b_pieces), down, raised)


def only_head(head, pair):
    zeros = jnp.zeros((64, pair.shape[1]), pair.dtype)
    part = pair[64 * head : 64 * head + 64]
    return jnp.concatenate([zeros, part] if head else [part, zeros], axis=0)


def attend_heads(q_t, k, k_t, v_t, out, exps, inverse, exact):
    first, second = slice(0, HALF), slice(HALF, D)
    causal = lax.broadcasted_iota(jnp.int32, (HALF, HALF), 0) <= lax.broadcasted_iota(
        jnp.int32, (HALF, HALF), 1
    )
    most = jnp.full((1, HALF), -1e30, F32)
    for head in range(2):
        dims = slice(64 * head, 64 * head + 64)
        q_head = only_head(head, q_t[...])
        level = jnp.sum(q_t[dims].astype(F32) * k_t[dims].astype(F32), axis=0, keepdims=True)
        scores = dot(k[first], q_head)
        one = jnp.where(causal, scores[:, first], -1e30)
        two = scores[:, second]
        three = jnp.where(causal, dot(k[second], q_head[:, second]), -1e30)
        level_one, level_two = level[:, first], level[:, second]
        if exact:
            level_one = jnp.max(one, axis=0, keepdims=True)
            level_two = jnp.max(jnp.maximum(two, three), axis=0, keepdims=True)
        one, two, three = one - level_one, two - level_two, three - level_two
        for part in (one, two, three):
            most = jnp.maximum(most, jnp.max(part, axis=0, keepdims=True))
        one, two, three = jnp.exp(one), jnp.exp(two), jnp.exp(three)
        scale_one = 1.0 / jnp.sum(one, axis=0, keepdims=True)
        scale_two = 1.0 / (
            jnp.sum(two, axis=0, keepdims=True) + jnp.sum(three, axis=0, keepdims=True)
        )
        for n, part in enumerate((one, two, three)):
            exps[head, n] = part.astype(BF)
        inverse[0, head : head + 1, first] = scale_one
        inverse[0, head : head + 1, second] = scale_two
        out[dims, first] = dot(v_t[dims, first], exps[head, 0]) * scale_one
        total = dot(v_t[dims, first], exps[head, 1]) + dot(v_t[dims, second], exps[head, 2])
        out[dims, second] = total * scale_two
    return jnp.max(most)


def attend_kernel(q_t, k, k_t, v_t, out_own, out_sib, out, exps, inverse):
    args = (q_t, k, k_t, v_t, out, exps, inverse)
    most = attend_heads(*args, False)

    @pl.when(most > 60.0)
    def _():
        attend_heads(*args, True)

    own, other = own_half()
    out_own[...] = out[:, own].astype(BF)
    out_sib[...] = out[:, other].astype(BF)


def attend(q_t, k, k_t, v_t):
    shape = jax.ShapeDtypeStruct
    wide = pl.BlockSpec((128, D), lambda j: (j, 0))
    halves = pl.BlockSpec((128, HALF), lambda j: (j, 0))
    return pl.pallas_call(
        attend_kernel,
        grid=(4,),
        out_shape=[
            shape((HALF, HALF), BF),
            shape((HALF, HALF), BF),
            shape((HALF, D), F32),
            pltpu.HBM((8, 3, HALF, HALF), BF),
            shape((4, 8, D), F32),
        ],
        in_specs=[wide, pl.BlockSpec((D, 128), lambda j: (0, j)), wide, wide],
        out_specs=[
            halves,
            halves,
            wide,
            pl.BlockSpec((2, 3, HALF, HALF), lambda j: (j, 0, 0, 0)),
            pl.BlockSpec((1, 8, D), lambda j: (j, 0, 0)),
        ],
        compiler_params=pltpu.CompilerParams(vmem_limit_bytes=VMEM_LIMIT),
        cost_estimate=cost(8e9, 20e6, 8 * D * D),
    )(q_t, k, k_t, v_t)


def attend_back_kernel(*refs):
    q_t, k_t, v, d_own, d_sib, out, exps, inverse, low_t, n1_in, raised = refs[:11]
    sums, dq_t, dk_t, dv_t, d_low_out = refs[11:16]
    d_scores, d_low, n1, sem = refs[16:]
    copy = pltpu.make_async_copy(n1_in, n1, sem)

    c = lax.axis_index("c")
    own, other = own_half()
    step = pl.program_id(0)

    @pl.when(step == 0)
    def _():
        copy.start()

    low, high = jnp.where(c == 0, d_own[...], d_sib[...]), jnp.where(c == 0, d_sib[...], d_own[...])
    d_out = jnp.concatenate([low, high], axis=1).astype(F32)
    weighted = d_out * out[...]
    first, second = slice(0, HALF), slice(HALF, D)
    for head in range(2):
        dims = slice(64 * head, 64 * head + 64)
        scale = inverse[0, head : head + 1]
        mean = jnp.sum(weighted[dims], axis=0, keepdims=True) * scale
        scaled = (d_out * scale).astype(BF)
        d_head = only_head(head, scaled)
        d_probs = dot(v[first], d_head)
        parts = (
            d_probs[:, first] - mean[:, first],
            d_probs[:, second] - mean[:, second],
            dot(v[second], d_head[:, second]) - mean[:, second],
        )
        for n, part in enumerate(parts):
            d_scores[n] = (exps[head, n].astype(F32) * part).astype(BF)
        key, query, d_value = k_t[dims], q_t[dims], scaled[dims]
        dq_t[dims, first] = (dot(key[:, first], d_scores[0]) * 0.125).astype(BF)
        total = dot(key[:, first], d_scores[1]) + dot(key[:, second], d_scores[2])
        dq_t[dims, second] = (total * 0.125).astype(BF)
        total = dot_last(query[:, first], d_scores[0]) + dot_last(query[:, second], d_scores[1])
        dk_t[dims, first] = total.astype(BF)
        dk_t[dims, second] = dot_last(query[:, second], d_scores[2]).astype(BF)
        total = dot_last(d_value[:, first], exps[head, 0])
        total += dot_last(d_value[:, second], exps[head, 1])
        dv_t[dims, first] = total.astype(BF)
        dv_t[dims, second] = dot_last(d_value[:, second], exps[head, 2]).astype(BF)
    cols = pl.ds(pl.multiple_of(step * 128, 128), 128)
    value_cols = pl.ds(pl.multiple_of(HALF + step * 128, 128), 128)
    part = dot(raised[:16, cols], dq_t[...]) + dot(raised[:16, value_cols], dv_t[...])
    at = pl.ds(pl.multiple_of(c * HALF + step * 128, 128), 128)
    top = lax.broadcasted_iota(jnp.int32, (8, 128), 0) < 4
    from_q = dot_last(low_t[...], dq_t[...])[:8] * ADAPTER_SCALE
    from_v = dot_last(low_t[...], dv_t[...])[:8] * ADAPTER_SCALE

    @pl.when(step == 0)
    def _():
        d_low[...] = part
        sums[8:16] = jnp.zeros((8, D), F32)

    @pl.when(step > 0)
    def _():
        d_low[...] += part

    sums[8:16, at] = jnp.where(top, from_q, from_v)

    @pl.when(step == 3)
    def _():
        copy.wait()
        low = d_low[...].astype(BF)
        d_low_out[...] = low
        sums[0:8] = dot(low, n1[...])[:8]


def attend_back(q_t, k_t, v, d_own, d_sib, out, exps, inverse, low_t, n1, raised):
    shape = jax.ShapeDtypeStruct
    wide = pl.BlockSpec((128, D), lambda j: (j, 0))
    halves = pl.BlockSpec((128, HALF), lambda j: (j, 0))
    whole = pl.BlockSpec((16, D), lambda j: (0, 0))
    return pl.pallas_call(
        attend_back_kernel,
        grid=(4,),
        out_shape=[shape((16, D), F32)] + [shape((HALF, D), BF)] * 3 + [shape((16, D), BF)],
        in_specs=[
            wide,
            wide,
            pl.BlockSpec((D, 128), lambda j: (0, j)),
            halves,
            halves,
            wide,
            pl.BlockSpec((2, 3, HALF, HALF), lambda j: (j, 0, 0, 0)),
            pl.BlockSpec((1, 8, D), lambda j: (j, 0, 0)),
            whole,
            ANY,
            pl.BlockSpec((128, D), lambda j: (0, 0)),
        ],
        out_specs=[whole, wide, wide, wide, whole],
        scratch_shapes=[
            pltpu.VMEM((3, HALF, HALF), BF),
            pltpu.VMEM((16, D), F32),
            pltpu.VMEM((D, D), BF),
            pltpu.SemaphoreType.DMA,
        ],
        compiler_params=pltpu.CompilerParams(vmem_limit_bytes=VMEM_LIMIT),
        cost_estimate=cost(16e9, 30e6),
    )(q_t, k_t, v, d_own, d_sib, out, *in_hbm(exps), inverse, low_t, *in_hbm(n1), raised)


def input_part(dq_t, dk_t, dv_t, d_low_t, a_pieces, b_pieces, down, mine):
    def kernel(*refs):
        grads, d_low, down_ref, out = refs[:3], refs[3], refs[4], refs[13]
        joint, sem = refs[14:]
        copies = joint_copies(refs[5:9], refs[9:13], joint, sem)
        start_all(copies)
        own, other = own_half()
        rows = own if mine else other
        grad = jnp.concatenate([jnp.transpose(grad[:, rows]) for grad in grads], axis=1)
        total = dot(jnp.transpose(d_low[:, rows]), down_ref[:16])
        wait_all(copies)
        total += dot_last(grad, joint[...].reshape(D, 3 * HALF))
        out[...] = total.astype(out.dtype)

    return pl.pallas_call(
        kernel,
        out_shape=jax.ShapeDtypeStruct((HALF, D), F32 if mine else BF),
        in_specs=[VMEM] * 5 + [ANY] * 8,
        out_specs=VMEM,
        scratch_shapes=[pltpu.VMEM((2, 4, 4, 32, 3 * HALF), BF), pltpu.SemaphoreType.DMA((8,))],
        compiler_params=pltpu.CompilerParams(vmem_limit_bytes=VMEM_LIMIT),
        cost_estimate=cost(2 * HALF * D * 1664, 8e6),
    )(dq_t, dk_t, dv_t, d_low_t, down, *a_pieces, *b_pieces)


PART = 256


def in_order(own, other, axis):
    first = lax.axis_index("c") == 0
    return jnp.concatenate(
        [jnp.where(first, own, other), jnp.where(first, other, own)], axis=axis
    )


def after_attention_kernel(mixed_own, mixed_other, tok, vec, wo_own, wo_sib, residual, n2):
    mixed = in_order(mixed_own[...], mixed_other[...], 0)
    attended = in_order(dot_first(mixed, wo_own[...]), dot_first(mixed, wo_sib[...]), 1)
    rows = tok[...].astype(F32) + attended + vec[6:7]
    residual[...] = rows
    normed, _ = normalise(rows)
    n2[...] = (normed * vec[1:2] + vec[3:4]).astype(BF)


def after_attention(mixed_own, mixed_other, tok, vec, wo_own, wo_sib):
    shape = jax.ShapeDtypeStruct
    across = pl.BlockSpec((HALF, PART), lambda i: (0, i))
    rows = pl.BlockSpec((PART, D), lambda i: (i, 0))
    weight = pl.BlockSpec((D, HALF), lambda i: (0, 0))
    return pl.pallas_call(
        after_attention_kernel,
        grid=(HALF // PART,),
        out_shape=[shape((HALF, D), F32), shape((HALF, D), BF)],
        in_specs=[across, across, rows, pl.BlockSpec((16, D), lambda i: (0, 0)), weight, weight],
        out_specs=[rows, rows],
        compiler_params=pltpu.CompilerParams(vmem_limit_bytes=VMEM_LIMIT),
        cost_estimate=cost(2 * HALF * D * D, 12e6),
    )(mixed_own, mixed_other, tok, vec, wo_own, wo_sib)


def feed_forward_kernel(*refs):
    n2, cot, vec = refs[:3]
    a_pieces, b_pieces = refs[3:7], refs[7:11]
    out, d_n2 = refs[11:13]
    w1, w2, hidden, d_gate, sem = refs[13:]
    chunks = HID // CHUNK
    copies = []
    for j in range(chunks):
        cols = slice(j * CHUNK, (j + 1) * CHUNK)
        group, part = j // 2, j % 2
        wide = slice(group * D, (group + 1) * D)
        some = []
        for step in range(4):
            x, y = turn_of("x", step), turn_of("y", step)
            some.append((a_pieces[step].at[:, :, :, cols], w1.at[:, x, :, :, cols]))
            some.append((b_pieces[step].at[part, :, :, wide], w2.at[j, :, y]))
        copies.append(
            [pltpu.make_async_copy(s, d, sem.at[j, n]) for n, (s, d) in enumerate(some)]
        )
    start_all(copies[0])
    start_all(copies[1])
    c = lax.axis_index("c")
    for j in range(chunks):
        wait_all(copies[j])
        if j + 2 < chunks:
            start_all(copies[j + 2])
        g, part = j // 2, j % 2
        bias = vec[pl.ds(8 + 2 * c + g, 1), part * CHUNK : (part + 1) * CHUNK]
        cols = slice(j * CHUNK, (j + 1) * CHUNK)
        u = dot(n2[...], w1[..., cols].reshape(D, CHUNK)) + bias
        square = u * u
        t = jnp.tanh(u * (0.7978845608028654 + 0.7978845608028654 * 0.044715 * square))
        half = 0.5 * u
        more = 1.0 + t
        hidden[:, cols] = (half * more).astype(BF)
        slope = 0.5 * more + half * (1.0 - t * t) * (
            0.7978845608028654 + 3 * 0.7978845608028654 * 0.044715 * square
        )
        d_gate[:, cols] = (dot_last(cot[...], w2[j].reshape(CHUNK, D)) * slope).astype(BF)
    d_n2[...] = dot_last(d_gate[...], w1[...].reshape(D, HID)).astype(d_n2.dtype)
    out[...] = dot(hidden[...], w2[...].reshape(HID, D)).astype(out.dtype)


def feed_forward(n2, cot, vec, a_pieces, b_pieces):
    return pl.pallas_call(
        feed_forward_kernel,
        grid=(1,),
        out_shape=[jax.ShapeDtypeStruct((HALF, D), BF)] * 2,
        in_specs=[
            pl.BlockSpec((HALF, D), lambda i: (0, 0)),
            pl.BlockSpec((HALF, D), lambda i: (1, 0)),
            pl.BlockSpec((16, D), lambda i: (0, 0)),
        ]
        + [ANY] * 8,
        out_specs=[pl.BlockSpec((HALF, D), lambda i: (0, 0))] * 2,
        scratch_shapes=[
            pltpu.VMEM((2, 4, 4, 32, HID), BF),
            pltpu.VMEM((4, 4, 4, 32, D), BF),
            pltpu.VMEM((HALF, HID), BF),
            pltpu.VMEM((HALF, HID), BF),
            pltpu.SemaphoreType.DMA((4, 8)),
        ],
        compiler_params=pltpu.CompilerParams(vmem_limit_bytes=VMEM_LIMIT),
        cost_estimate=cost(8 * HALF * D * HID, 16e6, HALF * HID),
    )(n2, cot, vec, *a_pieces, *b_pieces)


def before_attention_kernel(
    residual, cot, d_own, d_recv, vec, wo_own, wo_sib, d_residual, d_mixed_own, d_mixed_sib
):
    normed, inverse = normalise(residual[...])
    d_n2 = d_own[...].astype(F32) + d_recv[...].astype(F32)
    d_rows = cot[...].astype(F32) + norm_back(d_n2, normed, inverse, vec[1:2])
    d_residual[...] = d_rows
    d_attended = d_rows.astype(BF)
    left, right = d_attended[:, :HALF], d_attended[:, HALF:]
    first = lax.axis_index("c") == 0
    d_mixed = dot_last(wo_own[...], jnp.where(first, left, right))
    d_mixed += dot_last(wo_sib[...], jnp.where(first, right, left))
    d_mixed = d_mixed.astype(BF)
    d_mixed_own[...] = jnp.where(first, d_mixed[:HALF], d_mixed[HALF:])
    d_mixed_sib[...] = jnp.where(first, d_mixed[HALF:], d_mixed[:HALF])


def before_attention(residual, cot, d_own, d_recv, vec, wo_own, wo_sib):
    shape = jax.ShapeDtypeStruct
    rows = pl.BlockSpec((PART, D), lambda i: (i, 0))
    later = pl.BlockSpec((PART, D), lambda i: (i + HALF // PART, 0))
    across = pl.BlockSpec((HALF, PART), lambda i: (0, i))
    weight = pl.BlockSpec((D, HALF), lambda i: (0, 0))
    return pl.pallas_call(
        before_attention_kernel,
        grid=(HALF // PART,),
        out_shape=[shape((HALF, D), F32), shape((HALF, HALF), BF), shape((HALF, HALF), BF)],
        in_specs=[rows, later, rows, rows, pl.BlockSpec((16, D), lambda i: (0, 0)), weight, weight],
        out_specs=[rows, across, across],
        compiler_params=pltpu.CompilerParams(vmem_limit_bytes=VMEM_LIMIT),
        cost_estimate=cost(2 * HALF * D * D, 12e6),
    )(residual, cot, d_own, d_recv, vec, wo_own, wo_sib)


def input_kernel(tok, d_residual, part, recv, vec, out):
    normed, inverse = normalise(tok[...].astype(F32))
    d_n1 = part[...] + recv[...].astype(F32)
    out[...] = (d_residual[...] + norm_back(d_n1, normed, inverse, vec[0:1])).astype(BF)


def input_rows(tok, d_residual, part, recv, vec):
    rows = pl.BlockSpec((PART, D), lambda i: (i, 0))
    return pl.pallas_call(
        input_kernel,
        grid=(HALF // PART,),
        out_shape=jax.ShapeDtypeStruct((HALF, D), BF),
        in_specs=[rows] * 4 + [pl.BlockSpec((16, D), lambda i: (0, 0))],
        out_specs=rows,
        compiler_params=pltpu.CompilerParams(vmem_limit_bytes=VMEM_LIMIT),
        cost_estimate=cost(0, 8e6),
    )(tok, d_residual, part, recv, vec)


def copy_kernel(rows, out):
    out[...] = rows[...]


def copied(rows):
    return pl.pallas_call(
        copy_kernel,
        out_shape=jax.ShapeDtypeStruct(rows.shape, rows.dtype),
        in_specs=[VMEM],
        out_specs=VMEM,
        cost_estimate=cost(0, 2e6),
    )(rows)


def local(
    tokens,
    norm_gains,
    norm_shifts,
    query_value_offsets_bias,
    output_biases,
    expand_bias,
    joint_weight,
    output_weight,
    expand_weight,
    shrink_weight,
    query_down,
    query_raise_factor,
    value_down,
    value_raise_factor,
    cotangent,
):
    own, sibling = pack(
        joint_weight,
        norm_gains,
        norm_shifts,
        query_value_offsets_bias,
        output_biases,
        expand_bias,
        output_weight,
        expand_weight,
        shrink_weight,
    )
    a, b = assemble_z(ring(chip_rows(own, sibling), ZRING), (B_AT, B_FIRST + HID))
    rows = jnp.concatenate([tokens, cotangent], axis=0)
    a, b, rows = together(a, b, rows)
    a_near, b_near, rows = together(near(a, "y"), near(b, "x"), rows)
    rows = lax.ppermute(rows, PAIR, SWAP)
    a_far, b_far = ahead(a_near[0], "y"), ahead(b_near[0], "x")
    a_pieces = (a, a_near[0], a_far, a_near[1])
    b_pieces = (b, b_near[0], b_far, b_near[1])
    joint_a, joint_b = assemble_second(a_pieces, b_pieces, (0, 0), (A_FIRST, B_FIRST))
    a, b = assemble_second(a_pieces, b_pieces, (A_FIRST, B_FIRST), (HID, HID))
    a_near, b_near = near(joint_a, "x"), near(joint_b, "y")
    a_near, b_near, rows, a, b = together(a_near, b_near, rows, a, b)
    rows_sib = from_sibling(rows)
    a_far, b_far = ahead(a_near[0], "x"), ahead(b_near[0], "y")
    joint_a = (joint_a, a_near[0], a_far, a_near[1])
    joint_b = (joint_b, b_near[0], b_far, b_near[1])

    *joint, a, b = together(*joint_a, *joint_b, a, b)
    joint_a, joint_b = joint[:4], joint[4:]

    c = lax.axis_index("c")
    down = jnp.pad(jnp.concatenate([query_down.T, value_down.T], axis=0), ((0, 120), (0, 0)))
    raise_q = lax.dynamic_slice_in_dim(query_raise_factor, c * HALF, HALF, axis=1)
    raise_v = lax.dynamic_slice_in_dim(value_raise_factor, c * HALF, HALF, axis=1)
    raised = ADAPTER_SCALE * jnp.concatenate(
        [jnp.pad(raise_q, ((0, 124), (0, 0))), jnp.pad(raise_v, ((4, 120), (0, 0)))], axis=1
    )
    raised = raised.astype(BF)

    q_t, k, k_t, v, v_t, low_t, n1, vec, wo_own = project(rows, rows_sib, joint_a, joint_b, down, raised)
    a_near, b_near = near(a, "x"), near(b, "y")
    wo_own = wo_own.reshape(D, HALF)
    mixed_own, mixed_sib, out, exps, inverse = attend(q_t, k, k_t, v_t)
    mixed_sib, a_near, b_near, wo_own = together(mixed_sib, a_near, b_near, wo_own)
    mixed_other, wo_sib = from_sibling(mixed_sib), from_sibling(wo_own)
    a_far, b_far = ahead(a_near[0], "x"), ahead(b_near[0], "y")
    a_pieces = (a, a_near[0], a_far, a_near[1])
    b_pieces = (b, b_near[0], b_far, b_near[1])
    residual, n2 = after_attention(mixed_own, mixed_other, rows, vec, wo_own, wo_sib)
    n2_sib = from_sibling(n2)
    out_own, d_own = feed_forward(n2, rows, vec, a_pieces, b_pieces)
    out_sib, d_sib = feed_forward(n2_sib, rows_sib, vec, a_pieces, b_pieces)
    d_recv = from_sibling(d_sib)
    out_recv = from_sibling(out_sib)
    d_residual, d_mixed_own, d_mixed_sib = before_attention(
        residual, rows, d_own, d_recv, vec, wo_own, wo_sib
    )
    block_rows = (residual + out_own.astype(F32) + out_recv.astype(F32) + vec[7]).astype(BF)
    d_mixed_other = from_sibling(d_mixed_sib)
    q_t, block_rows = together(q_t, block_rows)
    block_output = lax.ppermute(block_rows, PAIR, SWAP)
    sums, dq_t, dk_t, dv_t, d_low_t = attend_back(
        q_t, k_t, v, d_mixed_own, d_mixed_other, out, exps, inverse, low_t, n1, raised
    )
    dq_t, sums, block_output = together(dq_t, sums, block_output)
    sums_sib = from_sibling(sums)
    part_sib = input_part(dq_t, dk_t, dv_t, d_low_t, joint_a, joint_b, down, False)
    part_sib, sums, sums_sib, dq_t = together(part_sib, sums, sums_sib, dq_t)
    part_recv = from_sibling(part_sib)
    sums = ring(sums + sums_sib, ZRING)
    part_own = input_part(dq_t, dk_t, dv_t, d_low_t, joint_a, joint_b, down, True)
    grad = input_rows(rows, d_residual, part_own, part_recv, vec)
    grad, sums = together(grad, sums)
    sums = ring(ring_sum(sums), "x")
    grad = lax.ppermute(grad, PAIR, SWAP)
    sums, block_output = together(ring_sum(sums), block_output)
    sums = ring(sums, "y")
    block_output, input_grad, sums = together(copied(block_output), grad.astype(F32), sums)
    sums = ring_sum(sums) / 64.0
    return (
        block_output,
        input_grad,
        sums[0:4].T,
        sums[8:12],
        sums[4:8].T,
        sums[12:16],
    )


def solution(mesh):
    fine = Mesh(mesh.devices.reshape(2, 4, 4, 2, 2), AXES)
    rows, columns = P(AXES, None), P(None, AXES)
    placed = (
        (rows,) + (columns,) * 4 + (P(AXES),) + (rows,) * 4 + (P(),) * 4 + (rows,)
    )
    return jax.shard_map(
        local,
        mesh=fine,
        in_specs=placed,
        out_specs=(rows, rows, P(), P(), P(), P()),
        check_vma=False,
    )
```

```python
import math

import jax
import jax.numpy as jnp
from jax import lax
from jax.experimental import pallas as pl
from jax.experimental.pallas import tpu as pltpu
from jax.sharding import Mesh, PartitionSpec as P

AXES = ("zl", "x", "y", "c", "zh")
PAIR = ("c", "zh")
ZRING = ("zl", "zh")
Z_PLACE = (0, 2, 1, 3)
SWAP = [(0, 0), (1, 2), (2, 1), (3, 3)]
FLIP = [(0, 1), (1, 0)]
FROM_NEXT = [(i, (i - 1) % 4) for i in range(4)]
FROM_PREV = [(i, (i + 1) % 4) for i in range(4)]
FROM_OPPOSITE = [(i, (i + 2) % 4) for i in range(4)]

EPS = 1e-05
ADAPTER_SCALE = 8.0
D = 1024
HALF = 512
HID = 2048
CHUNK = 512
A_FIRST = 1152
B_FIRST = 1024
B_AT = A_FIRST + HID
VMEM_LIMIT = 24 * 2**20
BF = jnp.bfloat16
F32 = jnp.float32

ANY = pl.BlockSpec(memory_space=pl.ANY)
VMEM = pl.BlockSpec(memory_space=pltpu.VMEM)


def permute(value, axis, pairs):
    if axis == ZRING:
        pairs = [(Z_PLACE[i], Z_PLACE[j]) for i, j in pairs]
    return lax.ppermute(value, axis, pairs)


def from_sibling(value):
    return lax.ppermute(value, "c", FLIP)


def ring(value, axis):
    return (
        value,
        permute(value, axis, FROM_NEXT),
        permute(value, axis, FROM_OPPOSITE),
        permute(value, axis, FROM_PREV),
    )


def parity_pairs(axis, back):
    pairs = []
    for i in range(4):
        for c in range(2):
            j = (i + (1 if (c == 0) != back else -1)) % 4
            if axis == ZRING:
                i_at, j_at = (4 * (i % 2) + 2 * c + i // 2, 4 * (j % 2) + 2 * c + j // 2)
            else:
                i_at, j_at = 2 * i + c, 2 * j + c
            pairs.append((i_at, j_at))
    return pairs


def ahead(value, axis):
    names = ("zl", "c", "zh") if axis == ZRING else (axis, "c")
    return lax.ppermute(value, names, parity_pairs(axis, False))


def back(value, axis):
    names = ("zl", "c", "zh") if axis == ZRING else (axis, "c")
    return lax.ppermute(value, names, parity_pairs(axis, True))


def near(value, axis):
    return ahead(value, axis), back(value, axis)


def ring_sum(pieces):
    own, after, opposite, before = pieces
    return (own + opposite) + (after + before)


def places():
    z = lax.axis_index("zh") * 2 + lax.axis_index("zl")
    return {"x": lax.axis_index("x"), "y": lax.axis_index("y"), "z": z}


def place_of(axis, step):
    spot = lax.rem(places()[axis] + step, 4)
    if axis == "z":
        return lax.rem(spot, 2), lax.div(spot, 2)
    return (spot,)


def turn_of(axis, step):
    way = 1 + 2 * lax.axis_index("c") if step % 2 else 1
    return lax.rem(places()[axis] + (4 - step) * way, 4)


def cost(flops, nbytes, transcendentals=0):
    return pl.CostEstimate(
        flops=int(flops), bytes_accessed=int(nbytes), transcendentals=int(transcendentals)
    )


def pack_first_kernel(
    joint, gains, shifts, offsets, biases, expand_bias, own, sibling, rows
):
    c = lax.axis_index("c")
    rows[...] = jnp.zeros_like(rows)
    for at, pair in enumerate((gains, shifts, offsets, biases)):
        rows[2 * at : 2 * at + 2, :8] = pair[...].astype(F32)
    rows[8:9, :32] = expand_bias[...].astype(F32)
    bias = rows[8:16]
    for part in range(1, 4):
        rows[8 + part : 9 + part] = pltpu.roll(bias, 128 - 8 * part, axis=1)[0:1]
    vectors = jnp.transpose(rows[...])[:8].astype(BF)
    for half, out in ((c, own), (1 - c, sibling)):
        q, k, v = [joint[:, pl.ds(pl.multiple_of(n * D + half * HALF, 128), HALF)] for n in range(3)]
        out[:, 0:512] = q
        out[:, 512:768] = k[:, 0:256]
        out[:, 768:896] = vectors
        out[:, B_AT : B_AT + 256] = k[:, 256:512]
        out[:, B_AT + 256 : B_AT + 768] = v


def pack_rest_kernel(wo, w1, w2, own, sibling, shuffled):
    c = lax.axis_index("c")
    rows = jnp.concatenate(
        [w1[:, s * 512 : (s + 1) * 512].astype(F32) for s in range(8)], axis=0
    ).astype(BF)
    lane = lax.broadcasted_iota(jnp.int32, (512, 512), 0)
    out = lax.broadcasted_iota(jnp.int32, (512, 512), 1)
    match = (lane >> 5) == ((out & 127) >> 3)
    match = match & (((lane & 31) >> 3) == (out >> 7)) & ((lane & 7) == (out & 7))
    mixed = jnp.dot(rows, jnp.where(match, 1.0, 0.0).astype(BF), preferred_element_type=F32)
    for s in range(8):
        for part in range(4):
            shuffled[part, :, s * 128 : (s + 1) * 128] = mixed[
                s * 8 : (s + 1) * 8, part * 128 : (part + 1) * 128
            ]
    for half, rest in ((c, own), (1 - c, sibling)):
        for g in range(2):
            at = A_FIRST + g * D
            rest[:, at : at + D] = shuffled[2 * half + g].astype(BF)
            at = B_AT + B_FIRST + g * D
            rest[:, at : at + D] = w2[2 * half + g]
        quarter = pl.multiple_of(half * HALF, 128)
        rest[:, 896:A_FIRST] = wo[:, pl.ds(quarter, 256)]
        rest[:, B_AT + 768 : B_AT + B_FIRST] = wo[:, pl.ds(quarter + 256, 256)]


def pack_kernel(*refs):
    first, rest = refs[:6], refs[6:9]
    own, sibling = refs[9:11]
    rows, shuffled = refs[11:]
    pack_first_kernel(*first, own, sibling, rows)
    pack_rest_kernel(*rest, own, sibling, shuffled)


def pack(joint, gains, shifts, offsets, biases, expand_bias, wo, w1, w2):
    return pl.pallas_call(
        pack_kernel,
        out_shape=[jax.ShapeDtypeStruct((8, B_AT + B_FIRST + HID), BF)] * 2,
        in_specs=[VMEM] * 9,
        out_specs=[VMEM] * 2,
        scratch_shapes=[pltpu.VMEM((128, 128), F32), pltpu.VMEM((4, 8, D), F32)],
        cost_estimate=cost(2 * 64 * 512 * 512, 700_000),
    )(joint, gains, shifts, offsets, biases, expand_bias.reshape(1, 32), wo, w1, w2.reshape(4, 8, D))


def chip_rows(own, sibling):
    return jnp.concatenate([own, from_sibling(sibling)], axis=0)


def assemble_z(pieces, widths):
    total = sum(widths)

    def kernel(*refs):
        outs, rows = refs[4:-1], refs[-1]
        c = lax.axis_index("c")
        for step in range(4):
            zl, zh = place_of("z", step)
            rows[zl, 2 * c + zh] = refs[step][0:8].astype(F32)
            rows[zl, 2 * (1 - c) + zh] = refs[step][8:16].astype(F32)
        for zl in range(2):
            at = 0
            for out, width in zip(outs, widths, strict=True):
                out[zl] = rows[zl, :, :, at : at + width].reshape(32, width).astype(BF)
                at += width

    return pl.pallas_call(
        kernel,
        out_shape=[pltpu.VMEM((2, 32, width), BF) for width in widths],
        in_specs=[VMEM] * 4,
        out_specs=[VMEM] * len(widths),
        scratch_shapes=[pltpu.VMEM((2, 4, 8, total), F32)],
        cost_estimate=cost(0, 4 * 64 * total),
    )(*pieces)


def assemble_second(a_pieces, b_pieces, starts, widths):
    def kernel(*refs):
        outs = refs[8:]
        for n, axis in enumerate(("y", "x")):
            cols = slice(starts[n], starts[n] + widths[n])
            for step in range(4):
                spot = turn_of(axis, step)
                for zl in range(2):
                    outs[n][zl, spot] = refs[4 * n + step][zl, :, cols]

    return pl.pallas_call(
        kernel,
        out_shape=[jax.ShapeDtypeStruct((2, 4, 32, width), BF) for width in widths],
        in_specs=[VMEM] * 8,
        out_specs=[VMEM] * 2,
        compiler_params=pltpu.CompilerParams(vmem_limit_bytes=VMEM_LIMIT),
        cost_estimate=cost(0, 4 * 256 * sum(widths)),
    )(*a_pieces, *b_pieces)


def together(*arrays):
    return lax.optimization_barrier(arrays)


def dot(left, right):
    return jnp.dot(left, right, preferred_element_type=F32)


def dot_last(left, right):
    return lax.dot_general(left, right, (((1,), (1,)), ((), ())), preferred_element_type=F32)


def dot_first(left, right):
    return lax.dot_general(left, right, (((0,), (0,)), ((), ())), preferred_element_type=F32)


def normalise(rows):
    centered = rows - jnp.mean(rows, axis=-1, keepdims=True)
    inverse = lax.rsqrt(jnp.mean(centered * centered, axis=-1, keepdims=True) + EPS)
    return centered * inverse, inverse


def norm_back(upstream, normed, inverse, gain):
    scaled = upstream * gain
    return inverse * (
        scaled
        - jnp.mean(scaled, axis=-1, keepdims=True)
        - normed * jnp.mean(scaled * normed, axis=-1, keepdims=True)
    )


def in_hbm(*arrays):
    return [pltpu.with_memory_space_constraint(a, pltpu.HBM) for a in arrays]


def start_all(copies):
    for copy in copies:
        copy.start()


def wait_all(copies):
    for copy in copies:
        copy.wait()


def own_half():
    c = lax.axis_index("c")
    own = pl.ds(pl.multiple_of(c * HALF, HALF), HALF)
    other = pl.ds(pl.multiple_of((1 - c) * HALF, HALF), HALF)
    return own, other


ROWS = 256


def joint_copies(a_pieces, b_pieces, joint, sem):
    copies = []
    for step in range(4):
        x, y = turn_of("x", step), turn_of("y", step)
        a, b = a_pieces[step].at[:, :, :, 0:768], b_pieces[step].at[:, :, :, 0:768]
        copies += [
            pltpu.make_async_copy(a, joint.at[:, x, :, :, 0:768], sem.at[step]),
            pltpu.make_async_copy(b, joint.at[:, :, y, :, 768:1536], sem.at[4 + step]),
        ]
    return copies


def project_kernel(*refs):
    tok_own, tok_sib = refs[:2]
    a_pieces, b_pieces = refs[2:6], refs[6:10]
    down, raised = refs[10:12]
    q_t, k, k_t, v, v_t, low_t, n1, vec_out, wo = refs[12:21]
    tok, joint, vec, sem = refs[21:]
    own, other = own_half()
    i = pl.program_id(0)
    tokens = [
        pltpu.make_async_copy(tok_own.at[0:HALF], tok.at[own], sem.at[0]),
        pltpu.make_async_copy(tok_sib.at[0:HALF], tok.at[other], sem.at[1]),
    ]
    vectors = [
        pltpu.make_async_copy(
            a_pieces[step].at[:, :, :, 768:896], vec.at[:, turn_of("x", step)], sem.at[2 + step]
        )
        for step in range(4)
    ]
    weights = joint_copies(a_pieces, b_pieces, joint, sem.at[pl.ds(6, 8)])
    outputs = []
    for step in range(4):
        x, y = turn_of("x", step), turn_of("y", step)
        a, b = a_pieces[step].at[:, :, :, 896:], b_pieces[step].at[:, :, :, 768:]
        outputs += [
            pltpu.make_async_copy(a, wo.at[:, x, :, :, 0:256], sem.at[14 + step]),
            pltpu.make_async_copy(b, wo.at[:, :, y, :, 256:512], sem.at[18 + step]),
        ]

    @pl.when(i == 0)
    def _():
        start_all(vectors)
        start_all(tokens)
        start_all(weights)
        start_all(outputs)
        wait_all(vectors)
        vec_out[...] = jnp.transpose(vec[...].reshape(D, 128).astype(F32))[:16]
        wait_all(tokens)

    rows = pl.ds(pl.multiple_of(i * ROWS, ROWS), ROWS)
    normed, _ = normalise(tok[rows].astype(F32))
    normed = (normed * vec_out[0:1] + vec_out[2:3]).astype(BF)
    n1[...] = normed
    reduced = dot_last(normed, down[...]).astype(BF)
    low_t[...] = jnp.transpose(reduced)[:16]
    added = dot(reduced, raised[...])

    @pl.when(i == 0)
    def _():
        wait_all(weights)

    both = dot(normed, joint[...].reshape(D, 3 * HALF))
    q = (both[:, :512] + vec_out[4:5, own] + added[:, :512]).astype(BF) * 0.125
    q_t[...] = jnp.transpose(q.astype(BF))
    key = both[:, 512:1024].astype(BF)
    k[...] = key
    k_t[...] = jnp.transpose(key)
    value = (both[:, 1024:] + vec_out[5:6, own] + added[:, 512:]).astype(BF)
    v[...] = value
    v_t[...] = jnp.transpose(value)

    @pl.when(i == D // ROWS - 1)
    def _():
        wait_all(outputs)


def project(tok_own, tok_sib, a_pieces, b_pieces, down, raised):
    shape = jax.ShapeDtypeStruct
    down_rows = pl.BlockSpec((ROWS, HALF), lambda i: (i, 0))
    across = pl.BlockSpec((HALF, ROWS), lambda i: (0, i))
    wide, tall = shape((HALF, D), BF), shape((D, HALF), BF)
    return pl.pallas_call(
        project_kernel,
        grid=(D // ROWS,),
        out_shape=[wide, tall, wide, tall, wide, shape((16, D), BF), pltpu.HBM((D, D), BF), shape((16, D), F32), shape((2, 4, 4, 32, HALF), BF)],
        in_specs=[ANY] * 10 + [pl.BlockSpec((128, D), lambda i: (0, 0))] * 2,
        out_specs=[
            across,
            down_rows,
            across,
            down_rows,
            across,
            pl.BlockSpec((16, ROWS), lambda i: (0, i)),
            pl.BlockSpec((ROWS, D), lambda i: (i, 0)),
            pl.BlockSpec((16, D), lambda i: (0, 0)),
            pl.BlockSpec((2, 4, 4, 32, HALF), lambda i: (0, 0, 0, 0, 0)),
        ],
        scratch_shapes=[
            pltpu.VMEM((D, D), BF),
            pltpu.VMEM((2, 4, 4, 32, 3 * HALF), BF),
            pltpu.VMEM((2, 4, 4, 32, 128), BF),
            pltpu.SemaphoreType.DMA((22,)),
        ],
        compiler_params=pltpu.CompilerParams(vmem_limit_bytes=VMEM_LIMIT),
        cost_estimate=cost(2 * D * D * 1536, 16e6),
    )(*in_hbm(tok_own, tok_sib, *a_pieces, *b_pieces), down, raised)


def only_head(head, pair):
    zeros = jnp.zeros((64, pair.shape[1]), pair.dtype)
    part = pair[64 * head : 64 * head + 64]
    return jnp.concatenate([zeros, part] if head else [part, zeros], axis=0)


def attend_heads(q_t, k, k_t, v_t, out, exps, inverse, exact):
    first, second = slice(0, HALF), slice(HALF, D)
    causal = lax.broadcasted_iota(jnp.int32, (HALF, HALF), 0) <= lax.broadcasted_iota(
        jnp.int32, (HALF, HALF), 1
    )
    most = jnp.full((1, HALF), -1e30, F32)
    for head in range(2):
        dims = slice(64 * head, 64 * head + 64)
        q_head = only_head(head, q_t[...])
        level = jnp.sum(q_t[dims].astype(F32) * k_t[dims].astype(F32), axis=0, keepdims=True)
        scores = dot(k[first], q_head)
        one = jnp.where(causal, scores[:, first], -1e30)
        two = scores[:, second]
        three = jnp.where(causal, dot(k[second], q_head[:, second]), -1e30)
        level_one, level_two = level[:, first], level[:, second]
        if exact:
            level_one = jnp.max(one, axis=0, keepdims=True)
            level_two = jnp.max(jnp.maximum(two, three), axis=0, keepdims=True)
        one, two, three = one - level_one, two - level_two, three - level_two
        for part in (one, two, three):
            most = jnp.maximum(most, jnp.max(part, axis=0, keepdims=True))
        one, two, three = jnp.exp(one), jnp.exp(two), jnp.exp(three)
        scale_one = 1.0 / jnp.sum(one, axis=0, keepdims=True)
        scale_two = 1.0 / (
            jnp.sum(two, axis=0, keepdims=True) + jnp.sum(three, axis=0, keepdims=True)
        )
        for n, part in enumerate((one, two, three)):
            exps[head, n] = part.astype(BF)
        inverse[0, head : head + 1, first] = scale_one
        inverse[0, head : head + 1, second] = scale_two
        out[dims, first] = dot(v_t[dims, first], exps[head, 0]) * scale_one
        total = dot(v_t[dims, first], exps[head, 1]) + dot(v_t[dims, second], exps[head, 2])
        out[dims, second] = total * scale_two
    return jnp.max(most)


def attend_kernel(q_t, k, k_t, v_t, mixed, out, exps, inverse):
    args = (q_t, k, k_t, v_t, out, exps, inverse)
    most = attend_heads(*args, False)

    @pl.when(most > 60.0)
    def _():
        attend_heads(*args, True)

    own, other = own_half()
    mixed[0] = out[:, own].astype(BF)
    mixed[1] = out[:, other].astype(BF)


def attend(q_t, k, k_t, v_t):
    shape = jax.ShapeDtypeStruct
    wide = pl.BlockSpec((128, D), lambda j: (j, 0))
    return pl.pallas_call(
        attend_kernel,
        grid=(4,),
        out_shape=[
            shape((2, HALF, HALF), BF),
            shape((HALF, D), F32),
            pltpu.HBM((8, 3, HALF, HALF), BF),
            shape((4, 8, D), F32),
        ],
        in_specs=[wide, pl.BlockSpec((D, 128), lambda j: (0, j)), wide, wide],
        out_specs=[
            pl.BlockSpec((2, 128, HALF), lambda j: (0, j, 0)),
            wide,
            pl.BlockSpec((2, 3, HALF, HALF), lambda j: (j, 0, 0, 0)),
            pl.BlockSpec((1, 8, D), lambda j: (j, 0, 0)),
        ],
        compiler_params=pltpu.CompilerParams(vmem_limit_bytes=VMEM_LIMIT),
        cost_estimate=cost(8e9, 20e6, 8 * D * D),
    )(q_t, k, k_t, v_t)


def attend_back_kernel(*refs):
    q_t, k_t, v, d_own, d_sib, out, exps, inverse, low_t, n1_in, raised = refs[:11]
    sums, dq_t, dk_t, dv_t, d_low_out = refs[11:16]
    d_scores, d_low, n1, sem = refs[16:]
    copy = pltpu.make_async_copy(n1_in, n1, sem)

    c = lax.axis_index("c")
    own, other = own_half()
    step = pl.program_id(0)

    @pl.when(step == 0)
    def _():
        copy.start()

    low, high = jnp.where(c == 0, d_own[...], d_sib[...]), jnp.where(c == 0, d_sib[...], d_own[...])
    d_out = jnp.concatenate([low, high], axis=1).astype(F32)
    weighted = d_out * out[...]
    first, second = slice(0, HALF), slice(HALF, D)
    for head in range(2):
        dims = slice(64 * head, 64 * head + 64)
        scale = inverse[0, head : head + 1]
        mean = jnp.sum(weighted[dims], axis=0, keepdims=True) * scale
        scaled = (d_out * scale).astype(BF)
        d_head = only_head(head, scaled)
        low, high = slice(0, 256), slice(256, HALF)
        for n, keys, cols in ((0, 0, 0), (1, 0, HALF), (2, HALF, HALF)):
            for rows, part in ((low, slice(0, HALF)), (high, slice(0 if n == 1 else 256, HALF))):
                at = slice(cols + part.start, cols + part.stop)
                d_probs = dot(v[keys + rows.start : keys + rows.stop], d_head[:, at])
                ds = exps[head, n, rows, part].astype(F32) * (d_probs - mean[:, at])
                d_scores[n, rows, part] = ds.astype(BF)
        key, query, d_value = k_t[dims], q_t[dims], scaled[dims]
        dq_t[dims, 0:256] = (dot(key[:, 0:256], d_scores[0, low, low]) * 0.125).astype(BF)
        dq_t[dims, 256:512] = (dot(key[:, 0:512], d_scores[0, :, high]) * 0.125).astype(BF)
        total = dot(key[:, first], d_scores[1])
        one = total[:, low] + dot(key[:, 512:768], d_scores[2, low, low])
        two = total[:, high] + dot(key[:, second], d_scores[2, :, high])
        dq_t[dims, 512:768] = (one * 0.125).astype(BF)
        dq_t[dims, 768:1024] = (two * 0.125).astype(BF)
        for grad, left, right in (
            (dk_t, query, d_scores),
            (dv_t, d_value, exps.at[head]),
        ):
            total = dot_last(left[:, second], right[1])
            one = total[:, low] + dot_last(left[:, first], right[0, low])
            two = total[:, high] + dot_last(left[:, 256:512], right[0, high, high])
            grad[dims, 0:256] = one.astype(BF)
            grad[dims, 256:512] = two.astype(BF)
            grad[dims, 512:768] = dot_last(left[:, second], right[2, low]).astype(BF)
            grad[dims, 768:1024] = dot_last(left[:, 768:1024], right[2, high, high]).astype(BF)
    cols = pl.ds(pl.multiple_of(step * 128, 128), 128)
    value_cols = pl.ds(pl.multiple_of(HALF + step * 128, 128), 128)
    part = dot(raised[:16, cols], dq_t[...]) + dot(raised[:16, value_cols], dv_t[...])
    at = pl.ds(pl.multiple_of(c * HALF + step * 128, 128), 128)
    top = lax.broadcasted_iota(jnp.int32, (8, 128), 0) < 4
    from_q = dot_last(low_t[...], dq_t[...])[:8] * ADAPTER_SCALE
    from_v = dot_last(low_t[...], dv_t[...])[:8] * ADAPTER_SCALE

    @pl.when(step == 0)
    def _():
        d_low[...] = part
        sums[8:16] = jnp.zeros((8, D), F32)

    @pl.when(step > 0)
    def _():
        d_low[...] += part

    sums[8:16, at] = jnp.where(top, from_q, from_v)

    @pl.when(step == 3)
    def _():
        copy.wait()
        low = d_low[...].astype(BF)
        d_low_out[...] = low
        sums[0:8] = dot(low, n1[...])[:8]


def attend_back(q_t, k_t, v, d_own, d_sib, out, exps, inverse, low_t, n1, raised):
    shape = jax.ShapeDtypeStruct
    wide = pl.BlockSpec((128, D), lambda j: (j, 0))
    halves = pl.BlockSpec((128, HALF), lambda j: (j, 0))
    whole = pl.BlockSpec((16, D), lambda j: (0, 0))
    return pl.pallas_call(
        attend_back_kernel,
        grid=(4,),
        out_shape=[shape((16, D), F32)] + [shape((HALF, D), BF)] * 3 + [shape((16, D), BF)],
        in_specs=[
            wide,
            wide,
            pl.BlockSpec((D, 128), lambda j: (0, j)),
            halves,
            halves,
            wide,
            pl.BlockSpec((2, 3, HALF, HALF), lambda j: (j, 0, 0, 0)),
            pl.BlockSpec((1, 8, D), lambda j: (j, 0, 0)),
            whole,
            ANY,
            pl.BlockSpec((128, D), lambda j: (0, 0)),
        ],
        out_specs=[whole, wide, wide, wide, whole],
        scratch_shapes=[
            pltpu.VMEM((3, HALF, HALF), BF),
            pltpu.VMEM((16, D), F32),
            pltpu.VMEM((D, D), BF),
            pltpu.SemaphoreType.DMA,
        ],
        compiler_params=pltpu.CompilerParams(vmem_limit_bytes=VMEM_LIMIT),
        cost_estimate=cost(16e9, 30e6),
    )(q_t, k_t, v, d_own, d_sib, out, *in_hbm(exps), inverse, low_t, *in_hbm(n1), raised)


def input_part(grads, d_low, down, a_pieces, b_pieces, joint, sem, mine):
    copies = joint_copies(a_pieces, b_pieces, joint, sem)
    start_all(copies)
    own, other = own_half()
    rows = own if mine else other
    grad = jnp.concatenate([jnp.transpose(grad[:, rows]) for grad in grads], axis=1)
    total = dot(jnp.transpose(d_low[:, rows]), down[:16])
    wait_all(copies)
    return total + dot_last(grad, joint[...].reshape(D, 3 * HALF))


def sibling_part_kernel(*refs):
    out, joint, sem = refs[13:]
    out[...] = input_part(refs[:3], refs[3], refs[4], refs[5:9], refs[9:13], joint, sem, False).astype(BF)


def sibling_part(dq_t, dk_t, dv_t, d_low_t, down, a_pieces, b_pieces):
    return pl.pallas_call(
        sibling_part_kernel,
        out_shape=jax.ShapeDtypeStruct((HALF, D), BF),
        in_specs=[VMEM] * 5 + [ANY] * 8,
        out_specs=VMEM,
        scratch_shapes=[pltpu.VMEM((2, 4, 4, 32, 3 * HALF), BF), pltpu.SemaphoreType.DMA((8,))],
        compiler_params=pltpu.CompilerParams(vmem_limit_bytes=VMEM_LIMIT),
        cost_estimate=cost(2 * HALF * D * 1664, 8e6),
    )(dq_t, dk_t, dv_t, d_low_t, down, *a_pieces, *b_pieces)


def input_kernel(*refs):
    tok, d_residual, recv, vec = refs[13:17]
    out, joint, sem = refs[17:]
    part = input_part(refs[:3], refs[3], refs[4], refs[5:9], refs[9:13], joint, sem, True)
    normed, inverse = normalise(tok[...].astype(F32))
    d_n1 = part + recv[...].astype(F32)
    out[...] = (d_residual[...] + norm_back(d_n1, normed, inverse, vec[0:1])).astype(BF)


def input_rows(dq_t, dk_t, dv_t, d_low_t, down, a_pieces, b_pieces, tok, d_residual, recv, vec):
    def whole(rows):
        return pl.BlockSpec((rows, D), lambda i: (0, 0))

    heads = [whole(HALF)] * 3 + [whole(16), whole(128)]
    return pl.pallas_call(
        input_kernel,
        grid=(1,),
        out_shape=jax.ShapeDtypeStruct((HALF, D), BF),
        in_specs=heads + [ANY] * 8 + [whole(HALF)] * 3 + [whole(16)],
        out_specs=whole(HALF),
        scratch_shapes=[pltpu.VMEM((2, 4, 4, 32, 3 * HALF), BF), pltpu.SemaphoreType.DMA((8,))],
        compiler_params=pltpu.CompilerParams(vmem_limit_bytes=VMEM_LIMIT),
        cost_estimate=cost(2 * HALF * D * 1664, 8e6),
    )(dq_t, dk_t, dv_t, d_low_t, down, *a_pieces, *b_pieces, tok, d_residual, recv, vec)


PART = 256


def in_order(own, other, axis):
    first = lax.axis_index("c") == 0
    return jnp.concatenate(
        [jnp.where(first, own, other), jnp.where(first, other, own)], axis=axis
    )


def after_attention_kernel(mixed_own, mixed_other, tok, tok_sib, vec, wo_own, wo_sib, residual, n2, n2_sib):
    mine = pl.program_id(0) < HALF // PART
    mixed = in_order(mixed_own[0], mixed_other[0], 0)
    attended = in_order(dot_first(mixed, wo_own[...]), dot_first(mixed, wo_sib[...]), 1)
    rows = jnp.where(mine, tok[...], tok_sib[...]).astype(F32) + attended + vec[6:7]
    normed, _ = normalise(rows)
    normed = (normed * vec[1:2] + vec[3:4]).astype(BF)

    @pl.when(mine)
    def _():
        residual[...] = rows
        n2[...] = normed

    @pl.when(jnp.logical_not(mine))
    def _():
        n2_sib[...] = normed


def after_attention(mixed_own, mixed_other, tok, tok_sib, vec, wo_own, wo_sib):
    shape = jax.ShapeDtypeStruct
    parts = HALF // PART
    weight = pl.BlockSpec((D, HALF), lambda i: (0, 0))
    rows = pl.BlockSpec((PART, D), lambda i: (jnp.minimum(i, parts - 1), 0))
    rows_sib = pl.BlockSpec((PART, D), lambda i: (jnp.maximum(i - parts, 0), 0))
    return pl.pallas_call(
        after_attention_kernel,
        grid=(2 * parts,),
        out_shape=[shape((HALF, D), F32), shape((HALF, D), BF), shape((HALF, D), BF)],
        in_specs=[
            pl.BlockSpec((1, HALF, PART), lambda i: (i // parts, 0, i % parts)),
            pl.BlockSpec((1, HALF, PART), lambda i: (1 - i // parts, 0, i % parts)),
            rows,
            rows_sib,
            pl.BlockSpec((16, D), lambda i: (0, 0)),
            weight,
            weight,
        ],
        out_specs=[rows, rows, rows_sib],
        compiler_params=pltpu.CompilerParams(vmem_limit_bytes=VMEM_LIMIT),
        cost_estimate=cost(4 * HALF * D * D, 16e6),
    )(mixed_own, mixed_other, tok, tok_sib, vec, wo_own, wo_sib)


def feed_forward_kernel(*refs):
    n2, cot, vec = refs[:3]
    a_pieces, b_pieces = refs[3:7], refs[7:11]
    out, d_n2 = refs[11:13]
    w1, w2, hidden, d_gate, sem = refs[13:]
    chunks = HID // CHUNK
    copies = []
    for j in range(chunks):
        cols = slice(j * CHUNK, (j + 1) * CHUNK)
        group, part = j // 2, j % 2
        wide = slice(group * D, (group + 1) * D)
        some = []
        for step in range(4):
            x, y = turn_of("x", step), turn_of("y", step)
            some.append((a_pieces[step].at[:, :, :, cols], w1.at[:, x, :, :, cols]))
            some.append((b_pieces[step].at[part, :, :, wide], w2.at[j, :, y]))
        copies.append(
            [pltpu.make_async_copy(s, d, sem.at[j, n]) for n, (s, d) in enumerate(some)]
        )
    for some in copies:
        start_all(some)
    c = lax.axis_index("c")
    for j in range(chunks):
        wait_all(copies[j])
        g, part = j // 2, j % 2
        bias = vec[pl.ds(8 + 2 * c + g, 1), part * CHUNK : (part + 1) * CHUNK]
        cols = slice(j * CHUNK, (j + 1) * CHUNK)
        u = dot(n2[...], w1[..., cols].reshape(D, CHUNK)) + bias
        square = u * u
        t = jnp.tanh(u * (0.7978845608028654 + 0.7978845608028654 * 0.044715 * square))
        half = 0.5 * u
        more = 1.0 + t
        hidden[:, cols] = (half * more).astype(BF)
        slope = 0.5 * more + half * (1.0 - t * t) * (
            0.7978845608028654 + 3 * 0.7978845608028654 * 0.044715 * square
        )
        d_gate[:, cols] = (dot_last(cot[...], w2[j].reshape(CHUNK, D)) * slope).astype(BF)
    d_n2[...] = dot_last(d_gate[...], w1[...].reshape(D, HID)).astype(d_n2.dtype)
    out[...] = dot(hidden[...], w2[...].reshape(HID, D)).astype(out.dtype)


def feed_forward(n2, cot, vec, a_pieces, b_pieces):
    return pl.pallas_call(
        feed_forward_kernel,
        grid=(1,),
        out_shape=[jax.ShapeDtypeStruct((HALF, D), BF)] * 2,
        in_specs=[
            pl.BlockSpec((HALF, D), lambda i: (0, 0)),
            pl.BlockSpec((HALF, D), lambda i: (1, 0)),
            pl.BlockSpec((16, D), lambda i: (0, 0)),
        ]
        + [ANY] * 8,
        out_specs=[pl.BlockSpec((HALF, D), lambda i: (0, 0))] * 2,
        scratch_shapes=[
            pltpu.VMEM((2, 4, 4, 32, HID), BF),
            pltpu.VMEM((4, 4, 4, 32, D), BF),
            pltpu.VMEM((HALF, HID), BF),
            pltpu.VMEM((HALF, HID), BF),
            pltpu.SemaphoreType.DMA((4, 8)),
        ],
        compiler_params=pltpu.CompilerParams(vmem_limit_bytes=VMEM_LIMIT),
        cost_estimate=cost(8 * HALF * D * HID, 16e6, HALF * HID),
    )(n2, cot, vec, *a_pieces, *b_pieces)


def before_attention_kernel(
    residual, cot, d_own, d_recv, vec, wo_own, wo_sib, d_residual, d_mixed_own, d_mixed_sib
):
    normed, inverse = normalise(residual[...])
    d_n2 = d_own[...].astype(F32) + d_recv[...].astype(F32)
    d_rows = cot[...].astype(F32) + norm_back(d_n2, normed, inverse, vec[1:2])
    d_residual[...] = d_rows
    d_attended = d_rows.astype(BF)
    left, right = d_attended[:, :HALF], d_attended[:, HALF:]
    first = lax.axis_index("c") == 0
    d_mixed = dot_last(wo_own[...], jnp.where(first, left, right))
    d_mixed += dot_last(wo_sib[...], jnp.where(first, right, left))
    d_mixed = d_mixed.astype(BF)
    d_mixed_own[...] = jnp.where(first, d_mixed[:HALF], d_mixed[HALF:])
    d_mixed_sib[...] = jnp.where(first, d_mixed[HALF:], d_mixed[:HALF])


def before_attention(residual, cot, d_own, d_recv, vec, wo_own, wo_sib):
    shape = jax.ShapeDtypeStruct
    rows = pl.BlockSpec((PART, D), lambda i: (i, 0))
    later = pl.BlockSpec((PART, D), lambda i: (i + HALF // PART, 0))
    across = pl.BlockSpec((HALF, PART), lambda i: (0, i))
    weight = pl.BlockSpec((D, HALF), lambda i: (0, 0))
    return pl.pallas_call(
        before_attention_kernel,
        grid=(HALF // PART,),
        out_shape=[shape((HALF, D), F32), shape((HALF, HALF), BF), shape((HALF, HALF), BF)],
        in_specs=[rows, later, rows, rows, pl.BlockSpec((16, D), lambda i: (0, 0)), weight, weight],
        out_specs=[rows, across, across],
        compiler_params=pltpu.CompilerParams(vmem_limit_bytes=VMEM_LIMIT),
        cost_estimate=cost(2 * HALF * D * D, 12e6),
    )(residual, cot, d_own, d_recv, vec, wo_own, wo_sib)


def copy_kernel(rows, out):
    out[...] = rows[...]


def copied(rows):
    return pl.pallas_call(
        copy_kernel,
        out_shape=jax.ShapeDtypeStruct(rows.shape, rows.dtype),
        in_specs=[VMEM],
        out_specs=VMEM,
        cost_estimate=cost(0, 2e6),
    )(rows)


def local(
    tokens,
    norm_gains,
    norm_shifts,
    query_value_offsets_bias,
    output_biases,
    expand_bias,
    joint_weight,
    output_weight,
    expand_weight,
    shrink_weight,
    query_down,
    query_raise_factor,
    value_down,
    value_raise_factor,
    cotangent,
):
    own, sibling = pack(
        joint_weight,
        norm_gains,
        norm_shifts,
        query_value_offsets_bias,
        output_biases,
        expand_bias,
        output_weight,
        expand_weight,
        shrink_weight,
    )
    a, b = assemble_z(ring(chip_rows(own, sibling), ZRING), (B_AT, B_FIRST + HID))
    rows = jnp.concatenate([tokens, cotangent], axis=0)
    a, b, rows = together(a, b, rows)
    a_near, b_near, rows = together(near(a, "y"), near(b, "x"), rows)
    rows = lax.ppermute(rows, PAIR, SWAP)
    a_far, b_far = ahead(a_near[0], "y"), ahead(b_near[0], "x")
    a_pieces = (a, a_near[0], a_far, a_near[1])
    b_pieces = (b, b_near[0], b_far, b_near[1])
    joint_a, joint_b = assemble_second(a_pieces, b_pieces, (0, 0), (A_FIRST, B_FIRST))
    a, b = assemble_second(a_pieces, b_pieces, (A_FIRST, B_FIRST), (HID, HID))
    a_near, b_near = near(joint_a, "x"), near(joint_b, "y")
    a_near, b_near, rows, a, b = together(a_near, b_near, rows, a, b)
    rows_sib = from_sibling(rows)
    a_far, b_far = ahead(a_near[0], "x"), ahead(b_near[0], "y")
    joint_a = (joint_a, a_near[0], a_far, a_near[1])
    joint_b = (joint_b, b_near[0], b_far, b_near[1])

    a_ahead, b_ahead = ahead(a, "x"), ahead(b, "y")
    *joint, a, b = together(*joint_a, *joint_b, a, b)
    joint_a, joint_b = joint[:4], joint[4:]

    c = lax.axis_index("c")
    down = jnp.pad(jnp.concatenate([query_down.T, value_down.T], axis=0), ((0, 120), (0, 0)))
    raise_q = lax.dynamic_slice_in_dim(query_raise_factor, c * HALF, HALF, axis=1)
    raise_v = lax.dynamic_slice_in_dim(value_raise_factor, c * HALF, HALF, axis=1)
    raised = ADAPTER_SCALE * jnp.concatenate(
        [jnp.pad(raise_q, ((0, 124), (0, 0))), jnp.pad(raise_v, ((4, 120), (0, 0)))], axis=1
    )
    raised = raised.astype(BF)

    q_t, k, k_t, v, v_t, low_t, n1, vec, wo_own = project(rows, rows_sib, joint_a, joint_b, down, raised)
    a_near, b_near = (a_ahead, back(a, "x")), (b_ahead, back(b, "y"))
    wo_own = wo_own.reshape(D, HALF)
    mixed, out, exps, inverse = attend(q_t, k, k_t, v_t)
    mixed, a_near, b_near, wo_own = together(mixed, a_near, b_near, wo_own)
    mixed_other, wo_sib = from_sibling(mixed), from_sibling(wo_own)
    a_far, b_far = ahead(a_near[0], "x"), ahead(b_near[0], "y")
    a_pieces = (a, a_near[0], a_far, a_near[1])
    b_pieces = (b, b_near[0], b_far, b_near[1])
    residual, n2, n2_sib = after_attention(
        mixed, mixed_other, rows, rows_sib, vec, wo_own, wo_sib
    )
    out_own, d_own = feed_forward(n2, rows, vec, a_pieces, b_pieces)
    out_sib, d_sib = feed_forward(n2_sib, rows_sib, vec, a_pieces, b_pieces)
    d_recv = from_sibling(d_sib)
    out_recv = from_sibling(out_sib)
    d_residual, d_mixed_own, d_mixed_sib = before_attention(
        residual, rows, d_own, d_recv, vec, wo_own, wo_sib
    )
    block_rows = (residual + out_own.astype(F32) + out_recv.astype(F32) + vec[7]).astype(BF)
    d_mixed_other = from_sibling(d_mixed_sib)
    q_t, block_rows = together(q_t, block_rows)
    block_output = lax.ppermute(block_rows, PAIR, SWAP)
    sums, dq_t, dk_t, dv_t, d_low_t = attend_back(
        q_t, k_t, v, d_mixed_own, d_mixed_other, out, exps, inverse, low_t, n1, raised
    )
    dq_t, sums, block_output = together(dq_t, sums, block_output)
    sums_sib = from_sibling(sums)
    heads = (dk_t, dv_t, d_low_t, down, joint_a, joint_b)
    part_sib = sibling_part(dq_t, *heads)
    part_sib, sums, sums_sib, dq_t = together(part_sib, sums, sums_sib, dq_t)
    part_recv = from_sibling(part_sib)
    sums = ring(sums + sums_sib, ZRING)
    grad = input_rows(dq_t, *heads, rows, d_residual, part_recv, vec)
    grad, sums = together(grad, sums)
    sums = ring(ring_sum(sums), "x")
    grad = lax.ppermute(grad, PAIR, SWAP)
    sums, block_output = together(ring_sum(sums), block_output)
    sums = ring(sums, "y")
    block_output, input_grad, sums = together(copied(block_output), grad.astype(F32), sums)
    sums = ring_sum(sums) / 64.0
    return (
        block_output,
        input_grad,
        sums[0:4].T,
        sums[8:12],
        sums[4:8].T,
        sums[12:16],
    )


def solution(mesh):
    fine = Mesh(mesh.devices.reshape(2, 4, 4, 2, 2), AXES)
    rows, columns = P(AXES, None), P(None, AXES)
    placed = (
        (rows,) + (columns,) * 4 + (P(AXES),) + (rows,) * 4 + (P(),) * 4 + (rows,)
    )
    return jax.shard_map(
        local,
        mesh=fine,
        in_specs=placed,
        out_specs=(rows, rows, P(), P(), P(), P()),
        check_vma=False,
    )
```

```python
import math

import jax
import jax.numpy as jnp
from jax import lax
from jax.experimental import pallas as pl
from jax.experimental.pallas import tpu as pltpu
from jax.sharding import Mesh, PartitionSpec as P

AXES = ("zl", "x", "y", "c", "zh")
PAIR = ("c", "zh")
ZRING = ("zl", "zh")
Z_PLACE = (0, 2, 1, 3)
SWAP = [(0, 0), (1, 2), (2, 1), (3, 3)]
FLIP = [(0, 1), (1, 0)]
FROM_NEXT = [(i, (i - 1) % 4) for i in range(4)]
FROM_PREV = [(i, (i + 1) % 4) for i in range(4)]
FROM_OPPOSITE = [(i, (i + 2) % 4) for i in range(4)]

EPS = 1e-05
ADAPTER_SCALE = 8.0
D = 1024
HALF = 512
HID = 2048
CHUNK = 512
A_FIRST = 1152
B_FIRST = 1024
B_AT = A_FIRST + HID
VMEM_LIMIT = 24 * 2**20
BF = jnp.bfloat16
F32 = jnp.float32

ANY = pl.BlockSpec(memory_space=pl.ANY)
VMEM = pl.BlockSpec(memory_space=pltpu.VMEM)


def permute(value, axis, pairs):
    if axis == ZRING:
        pairs = [(Z_PLACE[i], Z_PLACE[j]) for i, j in pairs]
    return lax.ppermute(value, axis, pairs)


def from_sibling(value):
    return lax.ppermute(value, "c", FLIP)


def ring(value, axis):
    return (
        value,
        permute(value, axis, FROM_NEXT),
        permute(value, axis, FROM_OPPOSITE),
        permute(value, axis, FROM_PREV),
    )


def parity_pairs(axis, back):
    pairs = []
    for i in range(4):
        for c in range(2):
            j = (i + (1 if (c == 0) != back else -1)) % 4
            if axis == ZRING:
                i_at, j_at = (4 * (i % 2) + 2 * c + i // 2, 4 * (j % 2) + 2 * c + j // 2)
            else:
                i_at, j_at = 2 * i + c, 2 * j + c
            pairs.append((i_at, j_at))
    return pairs


def ahead(value, axis):
    names = ("zl", "c", "zh") if axis == ZRING else (axis, "c")
    return lax.ppermute(value, names, parity_pairs(axis, False))


def back(value, axis):
    names = ("zl", "c", "zh") if axis == ZRING else (axis, "c")
    return lax.ppermute(value, names, parity_pairs(axis, True))


def near(value, axis):
    return ahead(value, axis), back(value, axis)


def ring_sum(pieces):
    own, after, opposite, before = pieces
    return (own + opposite) + (after + before)


def places():
    z = lax.axis_index("zh") * 2 + lax.axis_index("zl")
    return {"x": lax.axis_index("x"), "y": lax.axis_index("y"), "z": z}


def place_of(axis, step):
    spot = lax.rem(places()[axis] + step, 4)
    if axis == "z":
        return lax.rem(spot, 2), lax.div(spot, 2)
    return (spot,)


def turn_of(axis, step):
    way = 1 + 2 * lax.axis_index("c") if step % 2 else 1
    return lax.rem(places()[axis] + (4 - step) * way, 4)


def cost(flops, nbytes, transcendentals=0):
    return pl.CostEstimate(
        flops=int(flops), bytes_accessed=int(nbytes), transcendentals=int(transcendentals)
    )


def pack_first_kernel(
    joint, gains, shifts, offsets, biases, expand_bias, own, sibling, rows
):
    c = lax.axis_index("c")
    rows[...] = jnp.zeros_like(rows)
    for at, pair in enumerate((gains, shifts, offsets, biases)):
        rows[2 * at : 2 * at + 2, :8] = pair[...].astype(F32)
    rows[8:9, :32] = expand_bias[...].astype(F32)
    bias = rows[8:16]
    for part in range(1, 4):
        rows[8 + part : 9 + part] = pltpu.roll(bias, 128 - 8 * part, axis=1)[0:1]
    vectors = jnp.transpose(rows[...])[:8].astype(BF)
    for half, out in ((c, own), (1 - c, sibling)):
        q, k, v = [joint[:, pl.ds(pl.multiple_of(n * D + half * HALF, 128), HALF)] for n in range(3)]
        out[:, 0:512] = q
        out[:, 512:768] = k[:, 0:256]
        out[:, 768:896] = vectors
        out[:, B_AT : B_AT + 256] = k[:, 256:512]
        out[:, B_AT + 256 : B_AT + 768] = v


def pack_rest_kernel(wo, w1, w2, own, sibling, shuffled):
    c = lax.axis_index("c")
    rows = jnp.concatenate(
        [w1[:, s * 512 : (s + 1) * 512].astype(F32) for s in range(8)], axis=0
    ).astype(BF)
    lane = lax.broadcasted_iota(jnp.int32, (512, 512), 0)
    out = lax.broadcasted_iota(jnp.int32, (512, 512), 1)
    match = (lane >> 5) == ((out & 127) >> 3)
    match = match & (((lane & 31) >> 3) == (out >> 7)) & ((lane & 7) == (out & 7))
    mixed = jnp.dot(rows, jnp.where(match, 1.0, 0.0).astype(BF), preferred_element_type=F32)
    for s in range(8):
        for part in range(4):
            shuffled[part, :, s * 128 : (s + 1) * 128] = mixed[
                s * 8 : (s + 1) * 8, part * 128 : (part + 1) * 128
            ]
    for half, rest in ((c, own), (1 - c, sibling)):
        for g in range(2):
            at = A_FIRST + g * D
            rest[:, at : at + D] = shuffled[2 * half + g].astype(BF)
            at = B_AT + B_FIRST + g * D
            rest[:, at : at + D] = w2[2 * half + g]
        quarter = pl.multiple_of(half * HALF, 128)
        rest[:, 896:A_FIRST] = wo[:, pl.ds(quarter, 256)]
        rest[:, B_AT + 768 : B_AT + B_FIRST] = wo[:, pl.ds(quarter + 256, 256)]


def pack_kernel(*refs):
    first, rest = refs[:6], refs[6:9]
    own, sibling = refs[9:11]
    rows, shuffled = refs[11:]
    pack_first_kernel(*first, own, sibling, rows)
    pack_rest_kernel(*rest, own, sibling, shuffled)


def pack(joint, gains, shifts, offsets, biases, expand_bias, wo, w1, w2):
    return pl.pallas_call(
        pack_kernel,
        out_shape=[jax.ShapeDtypeStruct((8, B_AT + B_FIRST + HID), BF)] * 2,
        in_specs=[VMEM] * 9,
        out_specs=[VMEM] * 2,
        scratch_shapes=[pltpu.VMEM((128, 128), F32), pltpu.VMEM((4, 8, D), F32)],
        cost_estimate=cost(2 * 64 * 512 * 512, 700_000),
    )(joint, gains, shifts, offsets, biases, expand_bias.reshape(1, 32), wo, w1, w2.reshape(4, 8, D))


def chip_rows(own, sibling):
    return jnp.concatenate([own, from_sibling(sibling)], axis=0)


def assemble_z(pieces, widths):
    total = sum(widths)

    def kernel(*refs):
        outs, rows = refs[4:-1], refs[-1]
        c = lax.axis_index("c")
        for step in range(4):
            zl, zh = place_of("z", step)
            rows[zl, 2 * c + zh] = refs[step][0:8].astype(F32)
            rows[zl, 2 * (1 - c) + zh] = refs[step][8:16].astype(F32)
        for zl in range(2):
            at = 0
            for out, width in zip(outs, widths, strict=True):
                out[zl] = rows[zl, :, :, at : at + width].reshape(32, width).astype(BF)
                at += width

    return pl.pallas_call(
        kernel,
        out_shape=[pltpu.VMEM((2, 32, width), BF) for width in widths],
        in_specs=[VMEM] * 4,
        out_specs=[VMEM] * len(widths),
        scratch_shapes=[pltpu.VMEM((2, 4, 8, total), F32)],
        cost_estimate=cost(0, 4 * 64 * total),
    )(*pieces)


def assemble_second(a_pieces, b_pieces, starts, widths):
    def kernel(*refs):
        outs = refs[8:]
        for n, axis in enumerate(("y", "x")):
            cols = slice(starts[n], starts[n] + widths[n])
            for step in range(4):
                spot = turn_of(axis, step)
                for zl in range(2):
                    outs[n][zl, spot] = refs[4 * n + step][zl, :, cols]

    return pl.pallas_call(
        kernel,
        out_shape=[jax.ShapeDtypeStruct((2, 4, 32, width), BF) for width in widths],
        in_specs=[VMEM] * 8,
        out_specs=[VMEM] * 2,
        compiler_params=pltpu.CompilerParams(vmem_limit_bytes=VMEM_LIMIT),
        cost_estimate=cost(0, 4 * 256 * sum(widths)),
    )(*a_pieces, *b_pieces)


def together(*arrays):
    return lax.optimization_barrier(arrays)


def dot(left, right):
    return jnp.dot(left, right, preferred_element_type=F32)


def dot_last(left, right):
    return lax.dot_general(left, right, (((1,), (1,)), ((), ())), preferred_element_type=F32)


def dot_first(left, right):
    return lax.dot_general(left, right, (((0,), (0,)), ((), ())), preferred_element_type=F32)


def normalise(rows):
    centered = rows - jnp.mean(rows, axis=-1, keepdims=True)
    inverse = lax.rsqrt(jnp.mean(centered * centered, axis=-1, keepdims=True) + EPS)
    return centered * inverse, inverse


def norm_back(upstream, normed, inverse, gain):
    scaled = upstream * gain
    return inverse * (
        scaled
        - jnp.mean(scaled, axis=-1, keepdims=True)
        - normed * jnp.mean(scaled * normed, axis=-1, keepdims=True)
    )


def in_hbm(*arrays):
    return [pltpu.with_memory_space_constraint(a, pltpu.HBM) for a in arrays]


def start_all(copies):
    for copy in copies:
        copy.start()


def wait_all(copies):
    for copy in copies:
        copy.wait()


def own_half():
    c = lax.axis_index("c")
    own = pl.ds(pl.multiple_of(c * HALF, HALF), HALF)
    other = pl.ds(pl.multiple_of((1 - c) * HALF, HALF), HALF)
    return own, other


ROWS = 256


def joint_copies(a_pieces, b_pieces, joint, sem):
    copies = []
    for step in range(4):
        x, y = turn_of("x", step), turn_of("y", step)
        a, b = a_pieces[step].at[:, :, :, 0:768], b_pieces[step].at[:, :, :, 0:768]
        copies += [
            pltpu.make_async_copy(a, joint.at[:, x, :, :, 0:768], sem.at[step]),
            pltpu.make_async_copy(b, joint.at[:, :, y, :, 768:1536], sem.at[4 + step]),
        ]
    return copies


def project_kernel(*refs):
    tok_own, tok_sib = refs[:2]
    a_pieces, b_pieces = refs[2:6], refs[6:10]
    down, raised = refs[10:12]
    q_t, k, k_t, v, v_t, low_t, n1, vec_out, joint_out, *wo = refs[12:23]
    tok, joint, vec, sem = refs[23:]
    own, other = own_half()
    i = pl.program_id(0)
    tokens = [
        pltpu.make_async_copy(tok_own.at[0:HALF], tok.at[own], sem.at[0]),
        pltpu.make_async_copy(tok_sib.at[0:HALF], tok.at[other], sem.at[1]),
    ]
    vectors = [
        pltpu.make_async_copy(
            a_pieces[step].at[:, :, :, 768:896], vec.at[:, turn_of("x", step)], sem.at[2 + step]
        )
        for step in range(4)
    ]
    weights = joint_copies(a_pieces, b_pieces, joint, sem.at[pl.ds(6, 8)])
    outputs = []
    for step in range(4):
        x, y = turn_of("x", step), turn_of("y", step)
        for zl in range(2):
            a, b = a_pieces[step].at[zl, :, :, 896:], b_pieces[step].at[zl, :, :, 768:]
            outputs += [
                pltpu.make_async_copy(a, wo[zl].at[x, :, :, 0:256], sem.at[14 + 4 * step + zl]),
                pltpu.make_async_copy(b, wo[zl].at[:, y, :, 256:512], sem.at[16 + 4 * step + zl]),
            ]
    save = pltpu.make_async_copy(joint, joint_out, sem.at[30])

    @pl.when(i == 0)
    def _():
        start_all(vectors)
        start_all(tokens)
        start_all(weights)
        start_all(outputs)
        wait_all(vectors)
        vec_out[...] = jnp.transpose(vec[...].reshape(D, 128).astype(F32))[:16]
        wait_all(tokens)

    rows = pl.ds(pl.multiple_of(i * ROWS, ROWS), ROWS)
    normed, _ = normalise(tok[rows].astype(F32))
    normed = (normed * vec_out[0:1] + vec_out[2:3]).astype(BF)
    n1[...] = normed
    reduced = dot_last(normed, down[...]).astype(BF)
    low_t[...] = jnp.transpose(reduced)[:16]
    added = dot(reduced, raised[...])

    @pl.when(i == 0)
    def _():
        wait_all(weights)
        save.start()

    both = dot(normed, joint[...].reshape(D, 3 * HALF))
    q = (both[:, :512] + vec_out[4:5, own] + added[:, :512]).astype(BF) * 0.125
    q_t[...] = jnp.transpose(q.astype(BF))
    key = both[:, 512:1024].astype(BF)
    k[...] = key
    k_t[...] = jnp.transpose(key)
    value = (both[:, 1024:] + vec_out[5:6, own] + added[:, 512:]).astype(BF)
    v[...] = value
    v_t[...] = jnp.transpose(value)

    @pl.when(i == D // ROWS - 1)
    def _():
        wait_all(outputs)
        save.wait()


def project(tok_own, tok_sib, a_pieces, b_pieces, down, raised):
    shape = jax.ShapeDtypeStruct
    down_rows = pl.BlockSpec((ROWS, HALF), lambda i: (i, 0))
    across = pl.BlockSpec((HALF, ROWS), lambda i: (0, i))
    wide, tall = shape((HALF, D), BF), shape((D, HALF), BF)
    return pl.pallas_call(
        project_kernel,
        grid=(D // ROWS,),
        out_shape=[wide, tall, wide, tall, wide, shape((16, D), BF), pltpu.HBM((D, D), BF), shape((16, D), F32), pltpu.HBM((2, 4, 4, 32, 3 * HALF), BF)] + [shape((4, 4, 32, HALF), BF)] * 2,
        in_specs=[ANY] * 10 + [pl.BlockSpec((128, D), lambda i: (0, 0))] * 2,
        out_specs=[
            across,
            down_rows,
            across,
            down_rows,
            across,
            pl.BlockSpec((16, ROWS), lambda i: (0, i)),
            pl.BlockSpec((ROWS, D), lambda i: (i, 0)),
            pl.BlockSpec((16, D), lambda i: (0, 0)),
            ANY,
        ]
        + [pl.BlockSpec((4, 4, 32, HALF), lambda i: (0, 0, 0, 0))] * 2,
        scratch_shapes=[
            pltpu.VMEM((D, D), BF),
            pltpu.VMEM((2, 4, 4, 32, 3 * HALF), BF),
            pltpu.VMEM((2, 4, 4, 32, 128), BF),
            pltpu.SemaphoreType.DMA((31,)),
        ],
        compiler_params=pltpu.CompilerParams(vmem_limit_bytes=VMEM_LIMIT),
        cost_estimate=cost(2 * D * D * 1536, 16e6),
    )(*in_hbm(tok_own, tok_sib, *a_pieces, *b_pieces), down, raised)


def only_head(head, pair):
    zeros = jnp.zeros((64, pair.shape[1]), pair.dtype)
    part = pair[64 * head : 64 * head + 64]
    return jnp.concatenate([zeros, part] if head else [part, zeros], axis=0)


def attend_heads(q_t, k, k_t, v_t, out, exps, inverse, exact):
    first, second = slice(0, HALF), slice(HALF, D)
    causal = lax.broadcasted_iota(jnp.int32, (HALF, HALF), 0) <= lax.broadcasted_iota(
        jnp.int32, (HALF, HALF), 1
    )
    most = jnp.full((1, HALF), -1e30, F32)
    for head in range(2):
        dims = slice(64 * head, 64 * head + 64)
        q_head = only_head(head, q_t[...])
        level = jnp.sum(q_t[dims].astype(F32) * k_t[dims].astype(F32), axis=0, keepdims=True)
        scores = dot(k[first], q_head)
        one = jnp.where(causal, scores[:, first], -1e30)
        two = scores[:, second]
        three = jnp.where(causal, dot(k[second], q_head[:, second]), -1e30)
        level_one, level_two = level[:, first], level[:, second]
        if exact:
            level_one = jnp.max(one, axis=0, keepdims=True)
            level_two = jnp.max(jnp.maximum(two, three), axis=0, keepdims=True)
        one, two, three = one - level_one, two - level_two, three - level_two
        for part in (one, two, three):
            most = jnp.maximum(most, jnp.max(part, axis=0, keepdims=True))
        one, two, three = jnp.exp(one), jnp.exp(two), jnp.exp(three)
        scale_one = 1.0 / jnp.sum(one, axis=0, keepdims=True)
        scale_two = 1.0 / (
            jnp.sum(two, axis=0, keepdims=True) + jnp.sum(three, axis=0, keepdims=True)
        )
        for n, part in enumerate((one, two, three)):
            exps[head, n] = part.astype(BF)
        inverse[0, head : head + 1, first] = scale_one
        inverse[0, head : head + 1, second] = scale_two
        out[dims, first] = dot(v_t[dims, first], exps[head, 0]) * scale_one
        total = dot(v_t[dims, first], exps[head, 1]) + dot(v_t[dims, second], exps[head, 2])
        out[dims, second] = total * scale_two
    return jnp.max(most)


def attend_kernel(q_t, k, k_t, v_t, mixed_own, mixed_sib, out, exps, inverse):
    args = (q_t, k, k_t, v_t, out, exps, inverse)
    most = attend_heads(*args, False)

    @pl.when(most > 60.0)
    def _():
        attend_heads(*args, True)

    own, other = own_half()
    mixed_own[...] = out[:, own].astype(BF)
    mixed_sib[...] = out[:, other].astype(BF)


def attend(q_t, k, k_t, v_t):
    shape = jax.ShapeDtypeStruct
    halves = pl.BlockSpec((128, HALF), lambda j: (j, 0))
    wide = pl.BlockSpec((128, D), lambda j: (j, 0))
    return pl.pallas_call(
        attend_kernel,
        grid=(4,),
        out_shape=[
            shape((HALF, HALF), BF),
            shape((HALF, HALF), BF),
            shape((HALF, D), F32),
            pltpu.HBM((8, 3, HALF, HALF), BF),
            shape((4, 8, D), F32),
        ],
        in_specs=[wide, pl.BlockSpec((D, 128), lambda j: (0, j)), wide, wide],
        out_specs=[
            halves,
            halves,
            wide,
            pl.BlockSpec((2, 3, HALF, HALF), lambda j: (j, 0, 0, 0)),
            pl.BlockSpec((1, 8, D), lambda j: (j, 0, 0)),
        ],
        compiler_params=pltpu.CompilerParams(vmem_limit_bytes=VMEM_LIMIT),
        cost_estimate=cost(8e9, 20e6, 8 * D * D),
    )(q_t, k, k_t, v_t)


def attend_back_kernel(*refs):
    q_t, k_t, v, d_own, d_sib, out, exps, inverse, low_t, n1_in, raised = refs[:11]
    sums, dq_t, dk_t, dv_t, d_low_out = refs[11:16]
    d_scores, d_low, n1, sem = refs[16:]
    copy = pltpu.make_async_copy(n1_in, n1, sem)

    c = lax.axis_index("c")
    own, other = own_half()
    step = pl.program_id(0)

    @pl.when(step == 0)
    def _():
        copy.start()

    low, high = jnp.where(c == 0, d_own[...], d_sib[...]), jnp.where(c == 0, d_sib[...], d_own[...])
    d_out = jnp.concatenate([low, high], axis=1).astype(F32)
    weighted = d_out * out[...]
    first, second = slice(0, HALF), slice(HALF, D)
    for head in range(2):
        dims = slice(64 * head, 64 * head + 64)
        scale = inverse[0, head : head + 1]
        mean = jnp.sum(weighted[dims], axis=0, keepdims=True) * scale
        scaled = (d_out * scale).astype(BF)
        d_head = only_head(head, scaled)
        low, high = slice(0, 256), slice(256, HALF)
        for n, keys, cols in ((0, 0, 0), (1, 0, HALF), (2, HALF, HALF)):
            for rows, part in ((low, slice(0, HALF)), (high, slice(0 if n == 1 else 256, HALF))):
                at = slice(cols + part.start, cols + part.stop)
                d_probs = dot(v[keys + rows.start : keys + rows.stop], d_head[:, at])
                ds = exps[head, n, rows, part].astype(F32) * (d_probs - mean[:, at])
                d_scores[n, rows, part] = ds.astype(BF)
        key, query, d_value = k_t[dims], q_t[dims], scaled[dims]
        dq_t[dims, 0:256] = (dot(key[:, 0:256], d_scores[0, low, low]) * 0.125).astype(BF)
        dq_t[dims, 256:512] = (dot(key[:, 0:512], d_scores[0, :, high]) * 0.125).astype(BF)
        total = dot(key[:, first], d_scores[1])
        one = total[:, low] + dot(key[:, 512:768], d_scores[2, low, low])
        two = total[:, high] + dot(key[:, second], d_scores[2, :, high])
        dq_t[dims, 512:768] = (one * 0.125).astype(BF)
        dq_t[dims, 768:1024] = (two * 0.125).astype(BF)
        for grad, left, right in (
            (dk_t, query, d_scores),
            (dv_t, d_value, exps.at[head]),
        ):
            total = dot_last(left[:, second], right[1])
            one = total[:, low] + dot_last(left[:, first], right[0, low])
            two = total[:, high] + dot_last(left[:, 256:512], right[0, high, high])
            grad[dims, 0:256] = one.astype(BF)
            grad[dims, 256:512] = two.astype(BF)
            grad[dims, 512:768] = dot_last(left[:, second], right[2, low]).astype(BF)
            grad[dims, 768:1024] = dot_last(left[:, 768:1024], right[2, high, high]).astype(BF)
    cols = pl.ds(pl.multiple_of(step * 128, 128), 128)
    value_cols = pl.ds(pl.multiple_of(HALF + step * 128, 128), 128)
    part = dot(raised[:16, cols], dq_t[...]) + dot(raised[:16, value_cols], dv_t[...])
    at = pl.ds(pl.multiple_of(c * HALF + step * 128, 128), 128)
    top = lax.broadcasted_iota(jnp.int32, (8, 128), 0) < 4
    from_q = dot_last(low_t[...], dq_t[...])[:8] * ADAPTER_SCALE
    from_v = dot_last(low_t[...], dv_t[...])[:8] * ADAPTER_SCALE

    @pl.when(step == 0)
    def _():
        d_low[...] = part
        sums[8:16] = jnp.zeros((8, D), F32)

    @pl.when(step > 0)
    def _():
        d_low[...] += part

    sums[8:16, at] = jnp.where(top, from_q, from_v)

    @pl.when(step == 3)
    def _():
        copy.wait()
        low = d_low[...].astype(BF)
        d_low_out[...] = low
        sums[0:8] = dot(low, n1[...])[:8]


def attend_back(q_t, k_t, v, d_own, d_sib, out, exps, inverse, low_t, n1, raised):
    shape = jax.ShapeDtypeStruct
    wide = pl.BlockSpec((128, D), lambda j: (j, 0))
    halves = pl.BlockSpec((128, HALF), lambda j: (j, 0))
    whole = pl.BlockSpec((16, D), lambda j: (0, 0))
    return pl.pallas_call(
        attend_back_kernel,
        grid=(4,),
        out_shape=[shape((16, D), F32)] + [shape((HALF, D), BF)] * 3 + [shape((16, D), BF)],
        in_specs=[
            wide,
            wide,
            pl.BlockSpec((D, 128), lambda j: (0, j)),
            halves,
            halves,
            wide,
            pl.BlockSpec((2, 3, HALF, HALF), lambda j: (j, 0, 0, 0)),
            pl.BlockSpec((1, 8, D), lambda j: (j, 0, 0)),
            whole,
            ANY,
            pl.BlockSpec((128, D), lambda j: (0, 0)),
        ],
        out_specs=[whole, wide, wide, wide, whole],
        scratch_shapes=[
            pltpu.VMEM((3, HALF, HALF), BF),
            pltpu.VMEM((16, D), F32),
            pltpu.VMEM((D, D), BF),
            pltpu.SemaphoreType.DMA,
        ],
        compiler_params=pltpu.CompilerParams(vmem_limit_bytes=VMEM_LIMIT),
        cost_estimate=cost(16e9, 30e6),
    )(q_t, k_t, v, d_own, d_sib, out, *in_hbm(exps), inverse, low_t, *in_hbm(n1), raised)


def input_part(grads, d_low, down, joint, mine):
    own, other = own_half()
    rows = own if mine else other
    grad = jnp.concatenate([jnp.transpose(grad[:, rows]) for grad in grads], axis=1)
    total = dot(jnp.transpose(d_low[:, rows]), down[:16])
    return total + dot_last(grad, joint[...])


def sibling_part_kernel(dq_t, dk_t, dv_t, d_low, down, joint, out):
    out[...] = input_part((dq_t, dk_t, dv_t), d_low, down, joint, False).astype(BF)


def sibling_part(dq_t, dk_t, dv_t, d_low_t, down, joint):
    return pl.pallas_call(
        sibling_part_kernel,
        out_shape=jax.ShapeDtypeStruct((HALF, D), BF),
        in_specs=[VMEM] * 6,
        out_specs=VMEM,
        compiler_params=pltpu.CompilerParams(vmem_limit_bytes=VMEM_LIMIT),
        cost_estimate=cost(2 * HALF * D * 1664, 8e6),
    )(dq_t, dk_t, dv_t, d_low_t, down, joint)


def input_kernel(dq_t, dk_t, dv_t, d_low, down, joint, tok, d_residual, recv, vec, out):
    part = input_part((dq_t, dk_t, dv_t), d_low, down, joint, True)
    normed, inverse = normalise(tok[...].astype(F32))
    d_n1 = part + recv[...].astype(F32)
    out[...] = (d_residual[...] + norm_back(d_n1, normed, inverse, vec[0:1])).astype(BF)


def input_rows(dq_t, dk_t, dv_t, d_low_t, down, joint, tok, d_residual, recv, vec):
    def whole(rows):
        return pl.BlockSpec((rows, D), lambda i: (0, 0))

    weight = pl.BlockSpec((D, 3 * HALF), lambda i: (0, 0))
    return pl.pallas_call(
        input_kernel,
        grid=(1,),
        out_shape=jax.ShapeDtypeStruct((HALF, D), BF),
        in_specs=[whole(HALF)] * 3 + [whole(16), whole(128), weight] + [whole(HALF)] * 3 + [whole(16)],
        out_specs=whole(HALF),
        compiler_params=pltpu.CompilerParams(vmem_limit_bytes=VMEM_LIMIT),
        cost_estimate=cost(2 * HALF * D * 1664, 8e6),
    )(dq_t, dk_t, dv_t, d_low_t, down, joint, tok, d_residual, recv, vec)


PART = 256


def in_order(own, other, axis):
    first = lax.axis_index("c") == 0
    return jnp.concatenate(
        [jnp.where(first, own, other), jnp.where(first, other, own)], axis=axis
    )


def output_product(mixed, wo):
    return dot_first(mixed[:HALF], wo[0][...]) + dot_first(mixed[HALF:], wo[1][...])


def after_attention_kernel(*refs):
    own, sib, own_other, sib_other, tok, tok_sib, vec = refs[:7]
    wo_own, wo_sib = refs[7:9], refs[9:11]
    residual, n2, n2_sib = refs[11:]
    mine = pl.program_id(0) < HALF // PART
    mixed = in_order(
        jnp.where(mine, own[...], sib[...]), jnp.where(mine, own_other[...], sib_other[...]), 0
    )
    attended = in_order(output_product(mixed, wo_own), output_product(mixed, wo_sib), 1)
    rows = jnp.where(mine, tok[...], tok_sib[...]).astype(F32) + attended + vec[6:7]
    normed, _ = normalise(rows)
    normed = (normed * vec[1:2] + vec[3:4]).astype(BF)

    @pl.when(mine)
    def _():
        residual[...] = rows
        n2[...] = normed

    @pl.when(jnp.logical_not(mine))
    def _():
        n2_sib[...] = normed


def after_attention(own, sib, own_other, sib_other, tok, tok_sib, vec, wo_own, wo_sib):
    shape = jax.ShapeDtypeStruct
    parts = HALF // PART

    def mine(i):
        return jnp.minimum(i, parts - 1)

    def other(i):
        return jnp.maximum(i - parts, 0)

    weight = pl.BlockSpec((HALF, HALF), lambda i: (0, 0))
    rows = pl.BlockSpec((PART, D), lambda i: (mine(i), 0))
    rows_sib = pl.BlockSpec((PART, D), lambda i: (other(i), 0))
    columns = pl.BlockSpec((HALF, PART), lambda i: (0, mine(i)))
    columns_sib = pl.BlockSpec((HALF, PART), lambda i: (0, other(i)))
    return pl.pallas_call(
        after_attention_kernel,
        grid=(2 * parts,),
        out_shape=[shape((HALF, D), F32), shape((HALF, D), BF), shape((HALF, D), BF)],
        in_specs=[
            columns,
            columns_sib,
            columns,
            columns_sib,
            rows,
            rows_sib,
            pl.BlockSpec((16, D), lambda i: (0, 0)),
        ]
        + [weight] * 4,
        out_specs=[rows, rows, rows_sib],
        compiler_params=pltpu.CompilerParams(vmem_limit_bytes=VMEM_LIMIT),
        cost_estimate=cost(1e6, 1e5),
    )(own, sib, own_other, sib_other, tok, tok_sib, vec, *wo_own, *wo_sib)


def feed_forward_kernel(*refs):
    n2, cot, vec = refs[:3]
    a_pieces, b_pieces = refs[3:7], refs[7:11]
    out, d_n2 = refs[11:13]
    w1, w2, hidden, d_gate, sem = refs[13:]
    chunks = HID // CHUNK
    copies = []
    for j in range(chunks):
        cols = slice(j * CHUNK, (j + 1) * CHUNK)
        group, part = j // 2, j % 2
        wide = slice(group * D, (group + 1) * D)
        some = []
        for step in range(4):
            x, y = turn_of("x", step), turn_of("y", step)
            some.append((a_pieces[step].at[:, :, :, cols], w1.at[:, x, :, :, cols]))
            some.append((b_pieces[step].at[part, :, :, wide], w2.at[j, :, y]))
        copies.append(
            [pltpu.make_async_copy(s, d, sem.at[j, n]) for n, (s, d) in enumerate(some)]
        )
    for some in copies:
        start_all(some)
    c = lax.axis_index("c")
    for j in range(chunks):
        wait_all(copies[j])
        g, part = j // 2, j % 2
        bias = vec[pl.ds(8 + 2 * c + g, 1), part * CHUNK : (part + 1) * CHUNK]
        cols = slice(j * CHUNK, (j + 1) * CHUNK)
        u = dot(n2[...], w1[..., cols].reshape(D, CHUNK)) + bias
        square = u * u
        t = jnp.tanh(u * (0.7978845608028654 + 0.7978845608028654 * 0.044715 * square))
        half = 0.5 * u
        more = 1.0 + t
        hidden[:, cols] = (half * more).astype(BF)
        slope = 0.5 * more + half * (1.0 - t * t) * (
            0.7978845608028654 + 3 * 0.7978845608028654 * 0.044715 * square
        )
        d_gate[:, cols] = (dot_last(cot[...], w2[j].reshape(CHUNK, D)) * slope).astype(BF)
    d_n2[...] = dot_last(d_gate[...], w1[...].reshape(D, HID)).astype(d_n2.dtype)
    out[...] = dot(hidden[...], w2[...].reshape(HID, D)).astype(out.dtype)


def feed_forward(n2, cot, vec, a_pieces, b_pieces):
    return pl.pallas_call(
        feed_forward_kernel,
        grid=(1,),
        out_shape=[jax.ShapeDtypeStruct((HALF, D), BF)] * 2,
        in_specs=[
            pl.BlockSpec((HALF, D), lambda i: (0, 0)),
            pl.BlockSpec((HALF, D), lambda i: (1, 0)),
            pl.BlockSpec((16, D), lambda i: (0, 0)),
        ]
        + [ANY] * 8,
        out_specs=[pl.BlockSpec((HALF, D), lambda i: (0, 0))] * 2,
        scratch_shapes=[
            pltpu.VMEM((2, 4, 4, 32, HID), BF),
            pltpu.VMEM((4, 4, 4, 32, D), BF),
            pltpu.VMEM((HALF, HID), BF),
            pltpu.VMEM((HALF, HID), BF),
            pltpu.SemaphoreType.DMA((4, 8)),
        ],
        compiler_params=pltpu.CompilerParams(vmem_limit_bytes=VMEM_LIMIT),
        cost_estimate=cost(8 * HALF * D * HID, 16e6, HALF * HID),
    )(n2, cot, vec, *a_pieces, *b_pieces)


def before_attention_kernel(*refs):
    residual, cot, d_own, d_recv, vec = refs[:5]
    wo_own, wo_sib = refs[5:7], refs[7:9]
    d_residual, d_mixed_own, d_mixed_sib = refs[9:]
    normed, inverse = normalise(residual[...])
    d_n2 = d_own[...].astype(F32) + d_recv[...].astype(F32)
    d_rows = cot[...].astype(F32) + norm_back(d_n2, normed, inverse, vec[1:2])
    d_residual[...] = d_rows
    d_attended = d_rows.astype(BF)
    left, right = d_attended[:, :HALF], d_attended[:, HALF:]
    first = lax.axis_index("c") == 0
    mine, others = jnp.where(first, left, right), jnp.where(first, right, left)
    low = (dot_last(wo_own[0][...], mine) + dot_last(wo_sib[0][...], others)).astype(BF)
    high = (dot_last(wo_own[1][...], mine) + dot_last(wo_sib[1][...], others)).astype(BF)
    d_mixed_own[...] = jnp.where(first, low, high)
    d_mixed_sib[...] = jnp.where(first, high, low)


def before_attention(residual, cot, d_own, d_recv, vec, wo_own, wo_sib):
    shape = jax.ShapeDtypeStruct
    rows = pl.BlockSpec((PART, D), lambda i: (i, 0))
    later = pl.BlockSpec((PART, D), lambda i: (i + HALF // PART, 0))
    across = pl.BlockSpec((HALF, PART), lambda i: (0, i))
    weight = pl.BlockSpec((HALF, HALF), lambda i: (0, 0))
    return pl.pallas_call(
        before_attention_kernel,
        grid=(HALF // PART,),
        out_shape=[shape((HALF, D), F32), shape((HALF, HALF), BF), shape((HALF, HALF), BF)],
        in_specs=[rows, later, rows, rows, pl.BlockSpec((16, D), lambda i: (0, 0))] + [weight] * 4,
        out_specs=[rows, across, across],
        compiler_params=pltpu.CompilerParams(vmem_limit_bytes=VMEM_LIMIT),
        cost_estimate=cost(2 * HALF * D * D, 12e6),
    )(residual, cot, d_own, d_recv, vec, *wo_own, *wo_sib)


def copy_kernel(rows, out):
    out[...] = rows[...]


def copied(rows):
    return pl.pallas_call(
        copy_kernel,
        out_shape=jax.ShapeDtypeStruct(rows.shape, rows.dtype),
        in_specs=[VMEM],
        out_specs=VMEM,
        cost_estimate=cost(0, 2e6),
    )(rows)


def local(
    tokens,
    norm_gains,
    norm_shifts,
    query_value_offsets_bias,
    output_biases,
    expand_bias,
    joint_weight,
    output_weight,
    expand_weight,
    shrink_weight,
    query_down,
    query_raise_factor,
    value_down,
    value_raise_factor,
    cotangent,
):
    own, sibling = pack(
        joint_weight,
        norm_gains,
        norm_shifts,
        query_value_offsets_bias,
        output_biases,
        expand_bias,
        output_weight,
        expand_weight,
        shrink_weight,
    )
    a, b = assemble_z(ring(chip_rows(own, sibling), ZRING), (B_AT, B_FIRST + HID))
    rows = jnp.concatenate([tokens, cotangent], axis=0)
    a, b, rows = together(a, b, rows)
    a_near, b_near, rows = together(near(a, "y"), near(b, "x"), rows)
    rows = lax.ppermute(rows, PAIR, SWAP)
    a_far, b_far = ahead(a_near[0], "y"), ahead(b_near[0], "x")
    a_pieces = (a, a_near[0], a_far, a_near[1])
    b_pieces = (b, b_near[0], b_far, b_near[1])
    joint_a, joint_b = assemble_second(a_pieces, b_pieces, (0, 0), (A_FIRST, B_FIRST))
    a, b = assemble_second(a_pieces, b_pieces, (A_FIRST, B_FIRST), (HID, HID))
    a_near, b_near = near(joint_a, "x"), near(joint_b, "y")
    a_near, b_near, rows, a, b = together(a_near, b_near, rows, a, b)
    rows_sib = from_sibling(rows)
    a_far, b_far = ahead(a_near[0], "x"), ahead(b_near[0], "y")
    joint_a = (joint_a, a_near[0], a_far, a_near[1])
    joint_b = (joint_b, b_near[0], b_far, b_near[1])

    a_ahead, b_ahead = ahead(a, "x"), ahead(b, "y")
    *joint, a, b = together(*joint_a, *joint_b, a, b)
    joint_a, joint_b = joint[:4], joint[4:]

    c = lax.axis_index("c")
    down = jnp.pad(jnp.concatenate([query_down.T, value_down.T], axis=0), ((0, 120), (0, 0)))
    raise_q = lax.dynamic_slice_in_dim(query_raise_factor, c * HALF, HALF, axis=1)
    raise_v = lax.dynamic_slice_in_dim(value_raise_factor, c * HALF, HALF, axis=1)
    raised = ADAPTER_SCALE * jnp.concatenate(
        [jnp.pad(raise_q, ((0, 124), (0, 0))), jnp.pad(raise_v, ((4, 120), (0, 0)))], axis=1
    )
    raised = raised.astype(BF)

    q_t, k, k_t, v, v_t, low_t, n1, vec, joint, *wo_own = project(
        rows, rows_sib, joint_a, joint_b, down, raised
    )
    joint = joint.reshape(D, 3 * HALF)
    a_near, b_near = (a_ahead, back(a, "x")), (b_ahead, back(b, "y"))
    wo_own = [part.reshape(HALF, HALF) for part in wo_own]
    own, sib, out, exps, inverse = attend(q_t, k, k_t, v_t)
    own, sib, a_near, b_near, wo_own = together(own, sib, a_near, b_near, wo_own)
    own_other, sib_other = from_sibling(sib), from_sibling(own)
    wo_sib = [from_sibling(part) for part in wo_own]
    a_far, b_far = ahead(a_near[0], "x"), ahead(b_near[0], "y")
    a_pieces = (a, a_near[0], a_far, a_near[1])
    b_pieces = (b, b_near[0], b_far, b_near[1])
    residual, n2, n2_sib = after_attention(
        own, sib, own_other, sib_other, rows, rows_sib, vec, wo_own, wo_sib
    )
    out_own, d_own = feed_forward(n2, rows, vec, a_pieces, b_pieces)
    out_sib, d_sib = feed_forward(n2_sib, rows_sib, vec, a_pieces, b_pieces)
    d_recv = from_sibling(d_sib)
    out_recv = from_sibling(out_sib)
    d_residual, d_mixed_own, d_mixed_sib = before_attention(
        residual, rows, d_own, d_recv, vec, wo_own, wo_sib
    )
    block_rows = (residual + out_own.astype(F32) + out_recv.astype(F32) + vec[7]).astype(BF)
    d_mixed_other = from_sibling(d_mixed_sib)
    q_t, block_rows = together(q_t, block_rows)
    block_output = lax.ppermute(block_rows, PAIR, SWAP)
    sums, dq_t, dk_t, dv_t, d_low_t = attend_back(
        q_t, k_t, v, d_mixed_own, d_mixed_other, out, exps, inverse, low_t, n1, raised
    )
    dq_t, sums, block_output = together(dq_t, sums, block_output)
    sums_sib = from_sibling(sums)
    heads = (dk_t, dv_t, d_low_t, down, joint)
    part_sib = sibling_part(dq_t, *heads)
    part_sib, sums, sums_sib, dq_t = together(part_sib, sums, sums_sib, dq_t)
    part_recv = from_sibling(part_sib)
    sums = ring(sums + sums_sib, ZRING)
    grad = input_rows(dq_t, *heads, rows, d_residual, part_recv, vec)
    grad, sums = together(grad, sums)
    sums = ring(ring_sum(sums), "x")
    grad = lax.ppermute(grad, PAIR, SWAP)
    sums, block_output = together(ring_sum(sums), block_output)
    sums = ring(sums, "y")
    block_output, input_grad, sums = together(copied(block_output), grad.astype(F32), sums)
    sums = ring_sum(sums) / 64.0
    return (
        block_output,
        input_grad,
        sums[0:4].T,
        sums[8:12],
        sums[4:8].T,
        sums[12:16],
    )


def solution(mesh):
    fine = Mesh(mesh.devices.reshape(2, 4, 4, 2, 2), AXES)
    rows, columns = P(AXES, None), P(None, AXES)
    placed = (
        (rows,) + (columns,) * 4 + (P(AXES),) + (rows,) * 4 + (P(),) * 4 + (rows,)
    )
    return jax.shard_map(
        local,
        mesh=fine,
        in_specs=placed,
        out_specs=(rows, rows, P(), P(), P(), P()),
        check_vma=False,
    )
```

```python
import math

import jax
import jax.numpy as jnp
from jax import lax
from jax.experimental import pallas as pl
from jax.experimental.pallas import tpu as pltpu
from jax.sharding import Mesh, PartitionSpec as P

AXES = ("zl", "x", "y", "c", "zh")
PAIR = ("c", "zh")
ZRING = ("zl", "zh")
Z_PLACE = (0, 2, 1, 3)
SWAP = [(0, 0), (1, 2), (2, 1), (3, 3)]
FLIP = [(0, 1), (1, 0)]
FROM_NEXT = [(i, (i - 1) % 4) for i in range(4)]
FROM_PREV = [(i, (i + 1) % 4) for i in range(4)]
FROM_OPPOSITE = [(i, (i + 2) % 4) for i in range(4)]

EPS = 1e-05
ADAPTER_SCALE = 8.0
D = 1024
HALF = 512
HID = 2048
CHUNK = 512
A_FIRST = 1152
B_FIRST = 1024
B_AT = A_FIRST + HID
VMEM_LIMIT = 24 * 2**20
BF = jnp.bfloat16
F32 = jnp.float32

ANY = pl.BlockSpec(memory_space=pl.ANY)
VMEM = pl.BlockSpec(memory_space=pltpu.VMEM)


def permute(value, axis, pairs):
    if axis == ZRING:
        pairs = [(Z_PLACE[i], Z_PLACE[j]) for i, j in pairs]
    return lax.ppermute(value, axis, pairs)


def from_sibling(value):
    return lax.ppermute(value, "c", FLIP)


def ring(value, axis):
    return (
        value,
        permute(value, axis, FROM_NEXT),
        permute(value, axis, FROM_OPPOSITE),
        permute(value, axis, FROM_PREV),
    )


def parity_pairs(axis, back):
    pairs = []
    for i in range(4):
        for c in range(2):
            j = (i + (1 if (c == 0) != back else -1)) % 4
            if axis == ZRING:
                i_at, j_at = (4 * (i % 2) + 2 * c + i // 2, 4 * (j % 2) + 2 * c + j // 2)
            else:
                i_at, j_at = 2 * i + c, 2 * j + c
            pairs.append((i_at, j_at))
    return pairs


def ahead(value, axis):
    names = ("zl", "c", "zh") if axis == ZRING else (axis, "c")
    return lax.ppermute(value, names, parity_pairs(axis, False))


def back(value, axis):
    names = ("zl", "c", "zh") if axis == ZRING else (axis, "c")
    return lax.ppermute(value, names, parity_pairs(axis, True))


def near(value, axis):
    return ahead(value, axis), back(value, axis)


def ring_sum(pieces):
    own, after, opposite, before = pieces
    return (own + opposite) + (after + before)


def places():
    z = lax.axis_index("zh") * 2 + lax.axis_index("zl")
    return {"x": lax.axis_index("x"), "y": lax.axis_index("y"), "z": z}


def place_of(axis, step):
    spot = lax.rem(places()[axis] + step, 4)
    if axis == "z":
        return lax.rem(spot, 2), lax.div(spot, 2)
    return (spot,)


def turn_of(axis, step):
    way = 1 + 2 * lax.axis_index("c") if step % 2 else 1
    return lax.rem(places()[axis] + (4 - step) * way, 4)


def cost(flops, nbytes, transcendentals=0):
    return pl.CostEstimate(
        flops=int(flops), bytes_accessed=int(nbytes), transcendentals=int(transcendentals)
    )


def pack_first_kernel(
    joint, gains, shifts, offsets, biases, expand_bias, own, sibling, rows
):
    c = lax.axis_index("c")
    rows[...] = jnp.zeros_like(rows)
    for at, pair in enumerate((gains, shifts, offsets, biases)):
        rows[2 * at : 2 * at + 2, :8] = pair[...].astype(F32)
    rows[8:9, :32] = expand_bias[...].astype(F32)
    bias = rows[8:16]
    for part in range(1, 4):
        rows[8 + part : 9 + part] = pltpu.roll(bias, 128 - 8 * part, axis=1)[0:1]
    vectors = jnp.transpose(rows[...])[:8].astype(BF)
    for half, out in ((c, own), (1 - c, sibling)):
        q, k, v = [joint[:, pl.ds(pl.multiple_of(n * D + half * HALF, 128), HALF)] for n in range(3)]
        out[:, 0:512] = q
        out[:, 512:768] = k[:, 0:256]
        out[:, 768:896] = vectors
        out[:, B_AT : B_AT + 256] = k[:, 256:512]
        out[:, B_AT + 256 : B_AT + 768] = v


def pack_rest_kernel(wo, w1, w2, own, sibling, shuffled):
    c = lax.axis_index("c")
    rows = jnp.concatenate(
        [w1[:, s * 512 : (s + 1) * 512].astype(F32) for s in range(8)], axis=0
    ).astype(BF)
    lane = lax.broadcasted_iota(jnp.int32, (512, 512), 0)
    out = lax.broadcasted_iota(jnp.int32, (512, 512), 1)
    match = (lane >> 5) == ((out & 127) >> 3)
    match = match & (((lane & 31) >> 3) == (out >> 7)) & ((lane & 7) == (out & 7))
    mixed = jnp.dot(rows, jnp.where(match, 1.0, 0.0).astype(BF), preferred_element_type=F32)
    for s in range(8):
        for part in range(4):
            shuffled[part, :, s * 128 : (s + 1) * 128] = mixed[
                s * 8 : (s + 1) * 8, part * 128 : (part + 1) * 128
            ]
    for half, rest in ((c, own), (1 - c, sibling)):
        for g in range(2):
            at = A_FIRST + g * D
            rest[:, at : at + D] = shuffled[2 * half + g].astype(BF)
            at = B_AT + B_FIRST + g * D
            rest[:, at : at + D] = w2[2 * half + g]
        quarter = pl.multiple_of(half * HALF, 128)
        rest[:, 896:A_FIRST] = wo[:, pl.ds(quarter, 256)]
        rest[:, B_AT + 768 : B_AT + B_FIRST] = wo[:, pl.ds(quarter + 256, 256)]


def pack_kernel(*refs):
    first, rest = refs[:6], refs[6:9]
    own, sibling = refs[9:11]
    rows, shuffled = refs[11:]
    pack_first_kernel(*first, own, sibling, rows)
    pack_rest_kernel(*rest, own, sibling, shuffled)


def pack(joint, gains, shifts, offsets, biases, expand_bias, wo, w1, w2):
    return pl.pallas_call(
        pack_kernel,
        out_shape=[jax.ShapeDtypeStruct((8, B_AT + B_FIRST + HID), BF)] * 2,
        in_specs=[VMEM] * 9,
        out_specs=[VMEM] * 2,
        scratch_shapes=[pltpu.VMEM((128, 128), F32), pltpu.VMEM((4, 8, D), F32)],
        cost_estimate=cost(2 * 64 * 512 * 512, 700_000),
    )(joint, gains, shifts, offsets, biases, expand_bias.reshape(1, 32), wo, w1, w2.reshape(4, 8, D))


def chip_rows(own, sibling):
    return jnp.concatenate([own, from_sibling(sibling)], axis=0)


def assemble_z(pieces, widths):
    total = sum(widths)

    def kernel(*refs):
        outs, rows = refs[4:-1], refs[-1]
        c = lax.axis_index("c")
        for step in range(4):
            zl, zh = place_of("z", step)
            piece = refs[step][...].astype(F32)
            rows[zl, 2 * c + zh] = piece[0:8]
            rows[zl, 2 * (1 - c) + zh] = piece[8:16]
        for zl in range(2):
            at = 0
            for out, width in zip(outs, widths, strict=True):
                out[zl] = rows[zl, :, :, at : at + width].reshape(32, width).astype(BF)
                at += width

    return pl.pallas_call(
        kernel,
        out_shape=[pltpu.VMEM((2, 32, width), BF) for width in widths],
        in_specs=[VMEM] * 4,
        out_specs=[VMEM] * len(widths),
        scratch_shapes=[pltpu.VMEM((2, 4, 8, total), F32)],
        cost_estimate=cost(0, 4 * 64 * total),
    )(*pieces)


def assemble_second(a_pieces, b_pieces, starts, widths):
    def kernel(*refs):
        outs = refs[8:]
        for n, axis in enumerate(("y", "x")):
            cols = slice(starts[n], starts[n] + widths[n])
            for step in range(4):
                spot = turn_of(axis, step)
                for zl in range(2):
                    outs[n][zl, spot] = refs[4 * n + step][zl, :, cols]

    return pl.pallas_call(
        kernel,
        out_shape=[jax.ShapeDtypeStruct((2, 4, 32, width), BF) for width in widths],
        in_specs=[VMEM] * 8,
        out_specs=[VMEM] * 2,
        compiler_params=pltpu.CompilerParams(vmem_limit_bytes=VMEM_LIMIT),
        cost_estimate=cost(0, 4 * 256 * sum(widths)),
    )(*a_pieces, *b_pieces)


def together(*arrays):
    return lax.optimization_barrier(arrays)


def dot(left, right):
    return jnp.dot(left, right, preferred_element_type=F32)


def dot_last(left, right):
    return lax.dot_general(left, right, (((1,), (1,)), ((), ())), preferred_element_type=F32)


def dot_first(left, right):
    return lax.dot_general(left, right, (((0,), (0,)), ((), ())), preferred_element_type=F32)


def normalise(rows):
    centered = rows - jnp.mean(rows, axis=-1, keepdims=True)
    inverse = lax.rsqrt(jnp.mean(centered * centered, axis=-1, keepdims=True) + EPS)
    return centered * inverse, inverse


def norm_back(upstream, normed, inverse, gain):
    scaled = upstream * gain
    return inverse * (
        scaled
        - jnp.mean(scaled, axis=-1, keepdims=True)
        - normed * jnp.mean(scaled * normed, axis=-1, keepdims=True)
    )


def in_hbm(*arrays):
    return [pltpu.with_memory_space_constraint(a, pltpu.HBM) for a in arrays]


def start_all(copies):
    for copy in copies:
        copy.start()


def wait_all(copies):
    for copy in copies:
        copy.wait()


def own_half():
    c = lax.axis_index("c")
    own = pl.ds(pl.multiple_of(c * HALF, HALF), HALF)
    other = pl.ds(pl.multiple_of((1 - c) * HALF, HALF), HALF)
    return own, other


ROWS = 256


def joint_copies(a_pieces, b_pieces, joint, sem):
    copies = []
    for step in range(4):
        x, y = turn_of("x", step), turn_of("y", step)
        a, b = a_pieces[step].at[:, :, :, 0:768], b_pieces[step].at[:, :, :, 0:768]
        copies += [
            pltpu.make_async_copy(a, joint.at[:, x, :, :, 0:768], sem.at[step]),
            pltpu.make_async_copy(b, joint.at[:, :, y, :, 768:1536], sem.at[4 + step]),
        ]
    return copies


def project_kernel(*refs):
    tok_own, tok_sib = refs[:2]
    a_pieces, b_pieces = refs[2:6], refs[6:10]
    down, raised = refs[10:12]
    q_t, k, k_t, v, v_t, low_t, n1, vec_out, joint_out, *wo = refs[12:23]
    tok, joint, vec, sem = refs[23:]
    own, other = own_half()
    i = pl.program_id(0)
    tokens = [
        pltpu.make_async_copy(tok_own.at[0:HALF], tok.at[own], sem.at[0]),
        pltpu.make_async_copy(tok_sib.at[0:HALF], tok.at[other], sem.at[1]),
    ]
    vectors = [
        pltpu.make_async_copy(
            a_pieces[step].at[:, :, :, 768:896], vec.at[:, turn_of("x", step)], sem.at[2 + step]
        )
        for step in range(4)
    ]
    weights = joint_copies(a_pieces, b_pieces, joint, sem.at[pl.ds(6, 8)])
    outputs = []
    for step in range(4):
        x, y = turn_of("x", step), turn_of("y", step)
        for zl in range(2):
            a, b = a_pieces[step].at[zl, :, :, 896:], b_pieces[step].at[zl, :, :, 768:]
            outputs += [
                pltpu.make_async_copy(a, wo[zl].at[x, :, :, 0:256], sem.at[14 + 4 * step + zl]),
                pltpu.make_async_copy(b, wo[zl].at[:, y, :, 256:512], sem.at[16 + 4 * step + zl]),
            ]
    save = pltpu.make_async_copy(joint, joint_out, sem.at[30])

    @pl.when(i == 0)
    def _():
        start_all(vectors)
        start_all(tokens)
        start_all(weights)
        start_all(outputs)
        wait_all(vectors)
        vec_out[...] = jnp.transpose(vec[...].reshape(D, 128).astype(F32))[:16]
        wait_all(tokens)

    rows = pl.ds(pl.multiple_of(i * ROWS, ROWS), ROWS)
    normed, _ = normalise(tok[rows].astype(F32))
    normed = (normed * vec_out[0:1] + vec_out[2:3]).astype(BF)
    n1[...] = normed
    reduced = dot_last(normed, down[...]).astype(BF)
    low_t[...] = jnp.transpose(reduced)[:16]
    added = dot(reduced, raised[...])

    @pl.when(i == 0)
    def _():
        wait_all(weights)
        save.start()

    both = dot(normed, joint[...].reshape(D, 3 * HALF))
    q = (both[:, :512] + vec_out[4:5, own] + added[:, :512]).astype(BF) * 0.125
    q_t[...] = jnp.transpose(q.astype(BF))
    key = both[:, 512:1024].astype(BF)
    k[...] = key
    k_t[...] = jnp.transpose(key)
    value = (both[:, 1024:] + vec_out[5:6, own] + added[:, 512:]).astype(BF)
    v[...] = value
    v_t[...] = jnp.transpose(value)

    @pl.when(i == D // ROWS - 1)
    def _():
        wait_all(outputs)
        save.wait()


def project(tok_own, tok_sib, a_pieces, b_pieces, down, raised):
    shape = jax.ShapeDtypeStruct
    down_rows = pl.BlockSpec((ROWS, HALF), lambda i: (i, 0))
    across = pl.BlockSpec((HALF, ROWS), lambda i: (0, i))
    wide, tall = shape((HALF, D), BF), shape((D, HALF), BF)
    return pl.pallas_call(
        project_kernel,
        grid=(D // ROWS,),
        out_shape=[wide, tall, wide, tall, wide, shape((16, D), BF), pltpu.HBM((D, D), BF), shape((16, D), F32), pltpu.HBM((2, 4, 4, 32, 3 * HALF), BF)] + [shape((4, 4, 32, HALF), BF)] * 2,
        in_specs=[ANY] * 10 + [pl.BlockSpec((128, D), lambda i: (0, 0))] * 2,
        out_specs=[
            across,
            down_rows,
            across,
            down_rows,
            across,
            pl.BlockSpec((16, ROWS), lambda i: (0, i)),
            pl.BlockSpec((ROWS, D), lambda i: (i, 0)),
            pl.BlockSpec((16, D), lambda i: (0, 0)),
            ANY,
        ]
        + [pl.BlockSpec((4, 4, 32, HALF), lambda i: (0, 0, 0, 0))] * 2,
        scratch_shapes=[
            pltpu.VMEM((D, D), BF),
            pltpu.VMEM((2, 4, 4, 32, 3 * HALF), BF),
            pltpu.VMEM((2, 4, 4, 32, 128), BF),
            pltpu.SemaphoreType.DMA((31,)),
        ],
        compiler_params=pltpu.CompilerParams(vmem_limit_bytes=VMEM_LIMIT),
        cost_estimate=cost(2 * D * D * 1536, 16e6),
    )(*in_hbm(tok_own, tok_sib, *a_pieces, *b_pieces), down, raised)


def only_head(head, pair):
    zeros = jnp.zeros((64, pair.shape[1]), pair.dtype)
    part = pair[64 * head : 64 * head + 64]
    return jnp.concatenate([zeros, part] if head else [part, zeros], axis=0)


def attend_heads(q_t, k, k_t, v_t, out, exps, inverse, exact):
    first, second = slice(0, HALF), slice(HALF, D)
    causal = lax.broadcasted_iota(jnp.int32, (HALF, HALF), 0) <= lax.broadcasted_iota(
        jnp.int32, (HALF, HALF), 1
    )
    most = jnp.full((1, HALF), -1e30, F32)
    for head in range(2):
        dims = slice(64 * head, 64 * head + 64)
        q_head = only_head(head, q_t[...])
        level = jnp.sum(q_t[dims].astype(F32) * k_t[dims].astype(F32), axis=0, keepdims=True)
        scores = dot(k[first], q_head)
        one = jnp.where(causal, scores[:, first], -1e30)
        two = scores[:, second]
        three = jnp.where(causal, dot(k[second], q_head[:, second]), -1e30)
        level_one, level_two = level[:, first], level[:, second]
        if exact:
            level_one = jnp.max(one, axis=0, keepdims=True)
            level_two = jnp.max(jnp.maximum(two, three), axis=0, keepdims=True)
        one, two, three = one - level_one, two - level_two, three - level_two
        for part in (one, two, three):
            most = jnp.maximum(most, jnp.max(part, axis=0, keepdims=True))
        one, two, three = [jnp.exp(part).astype(BF) for part in (one, two, three)]
        for n, part in enumerate((one, two, three)):
            exps[head, n] = part
        one, two, three = [part.astype(F32) for part in (one, two, three)]
        scale_one = 1.0 / jnp.sum(one, axis=0, keepdims=True)
        scale_two = 1.0 / (
            jnp.sum(two, axis=0, keepdims=True) + jnp.sum(three, axis=0, keepdims=True)
        )
        inverse[0, head : head + 1, first] = scale_one
        inverse[0, head : head + 1, second] = scale_two
        out[dims, first] = dot(v_t[dims, first], exps[head, 0]) * scale_one
        total = dot(v_t[dims, first], exps[head, 1]) + dot(v_t[dims, second], exps[head, 2])
        out[dims, second] = total * scale_two
    return jnp.max(most)


def attend_kernel(q_t, k, k_t, v_t, mixed_own, mixed_sib, out, exps, inverse):
    args = (q_t, k, k_t, v_t, out, exps, inverse)
    most = attend_heads(*args, False)

    @pl.when(most > 60.0)
    def _():
        attend_heads(*args, True)

    own, other = own_half()
    mixed_own[...] = out[:, own].astype(BF)
    mixed_sib[...] = out[:, other].astype(BF)


def attend(q_t, k, k_t, v_t):
    shape = jax.ShapeDtypeStruct
    halves = pl.BlockSpec((128, HALF), lambda j: (j, 0))
    wide = pl.BlockSpec((128, D), lambda j: (j, 0))
    return pl.pallas_call(
        attend_kernel,
        grid=(4,),
        out_shape=[
            shape((HALF, HALF), BF),
            shape((HALF, HALF), BF),
            shape((HALF, D), F32),
            pltpu.HBM((8, 3, HALF, HALF), BF),
            shape((4, 8, D), F32),
        ],
        in_specs=[wide, pl.BlockSpec((D, 128), lambda j: (0, j)), wide, wide],
        out_specs=[
            halves,
            halves,
            wide,
            pl.BlockSpec((2, 3, HALF, HALF), lambda j: (j, 0, 0, 0)),
            pl.BlockSpec((1, 8, D), lambda j: (j, 0, 0)),
        ],
        compiler_params=pltpu.CompilerParams(vmem_limit_bytes=VMEM_LIMIT),
        cost_estimate=cost(8e9, 20e6, 8 * D * D),
    )(q_t, k, k_t, v_t)


def attend_back_kernel(*refs):
    q_t, k_t, v, d_own, d_sib, out, exps, inverse, low_t, n1_in, raised = refs[:11]
    sums, dq_t, dk_t, dv_t, d_low_out = refs[11:16]
    d_scores, d_low, n1, sem = refs[16:]
    copy = pltpu.make_async_copy(n1_in, n1, sem)

    c = lax.axis_index("c")
    own, other = own_half()
    step = pl.program_id(0)

    @pl.when(step == 0)
    def _():
        copy.start()

    low, high = jnp.where(c == 0, d_own[...], d_sib[...]), jnp.where(c == 0, d_sib[...], d_own[...])
    d_out = jnp.concatenate([low, high], axis=1).astype(F32)
    first, second = slice(0, HALF), slice(HALF, D)
    for head in range(2):
        dims = slice(64 * head, 64 * head + 64)
        scale = inverse[0, head : head + 1]
        scaled = (d_out * scale).astype(BF)
        mean = jnp.sum(scaled[dims].astype(F32) * out[dims], axis=0, keepdims=True)
        d_head = only_head(head, scaled)
        low, high = slice(0, 256), slice(256, HALF)
        for n, keys, cols in ((0, 0, 0), (1, 0, HALF), (2, HALF, HALF)):
            for rows, part in ((low, slice(0, HALF)), (high, slice(0 if n == 1 else 256, HALF))):
                at = slice(cols + part.start, cols + part.stop)
                d_probs = dot(v[keys + rows.start : keys + rows.stop], d_head[:, at])
                ds = exps[head, n, rows, part].astype(F32) * (d_probs - mean[:, at])
                d_scores[n, rows, part] = ds.astype(BF)
        key, query, d_value = k_t[dims], q_t[dims], scaled[dims]
        dq_t[dims, 0:256] = (dot(key[:, 0:256], d_scores[0, low, low]) * 0.125).astype(BF)
        dq_t[dims, 256:512] = (dot(key[:, 0:512], d_scores[0, :, high]) * 0.125).astype(BF)
        total = dot(key[:, first], d_scores[1])
        one = total[:, low] + dot(key[:, 512:768], d_scores[2, low, low])
        two = total[:, high] + dot(key[:, second], d_scores[2, :, high])
        dq_t[dims, 512:768] = (one * 0.125).astype(BF)
        dq_t[dims, 768:1024] = (two * 0.125).astype(BF)
        for grad, left, right in (
            (dk_t, query, d_scores),
            (dv_t, d_value, exps.at[head]),
        ):
            total = dot_last(left[:, second], right[1])
            one = total[:, low] + dot_last(left[:, first], right[0, low])
            two = total[:, high] + dot_last(left[:, 256:512], right[0, high, high])
            grad[dims, 0:256] = one.astype(BF)
            grad[dims, 256:512] = two.astype(BF)
            grad[dims, 512:768] = dot_last(left[:, second], right[2, low]).astype(BF)
            grad[dims, 768:1024] = dot_last(left[:, 768:1024], right[2, high, high]).astype(BF)
    cols = pl.ds(pl.multiple_of(step * 128, 128), 128)
    value_cols = pl.ds(pl.multiple_of(HALF + step * 128, 128), 128)
    part = dot(raised[:16, cols], dq_t[...]) + dot(raised[:16, value_cols], dv_t[...])
    at = pl.ds(pl.multiple_of(c * HALF + step * 128, 128), 128)
    top = lax.broadcasted_iota(jnp.int32, (8, 128), 0) < 4
    from_q = dot_last(low_t[...], dq_t[...])[:8] * ADAPTER_SCALE
    from_v = dot_last(low_t[...], dv_t[...])[:8] * ADAPTER_SCALE

    @pl.when(step == 0)
    def _():
        d_low[...] = part
        sums[8:16] = jnp.zeros((8, D), F32)

    @pl.when(step > 0)
    def _():
        d_low[...] += part

    sums[8:16, at] = jnp.where(top, from_q, from_v)

    @pl.when(step == 3)
    def _():
        copy.wait()
        low = d_low[...].astype(BF)
        d_low_out[...] = low
        sums[0:8] = dot(low, n1[...])[:8]


def attend_back(q_t, k_t, v, d_own, d_sib, out, exps, inverse, low_t, n1, raised):
    shape = jax.ShapeDtypeStruct
    wide = pl.BlockSpec((128, D), lambda j: (j, 0))
    halves = pl.BlockSpec((128, HALF), lambda j: (j, 0))
    whole = pl.BlockSpec((16, D), lambda j: (0, 0))
    return pl.pallas_call(
        attend_back_kernel,
        grid=(4,),
        out_shape=[shape((16, D), F32)] + [shape((HALF, D), BF)] * 3 + [shape((16, D), BF)],
        in_specs=[
            wide,
            wide,
            pl.BlockSpec((D, 128), lambda j: (0, j)),
            halves,
            halves,
            wide,
            pl.BlockSpec((2, 3, HALF, HALF), lambda j: (j, 0, 0, 0)),
            pl.BlockSpec((1, 8, D), lambda j: (j, 0, 0)),
            whole,
            ANY,
            pl.BlockSpec((128, D), lambda j: (0, 0)),
        ],
        out_specs=[whole, wide, wide, wide, whole],
        scratch_shapes=[
            pltpu.VMEM((3, HALF, HALF), BF),
            pltpu.VMEM((16, D), F32),
            pltpu.VMEM((D, D), BF),
            pltpu.SemaphoreType.DMA,
        ],
        compiler_params=pltpu.CompilerParams(vmem_limit_bytes=VMEM_LIMIT),
        cost_estimate=cost(16e9, 30e6),
    )(q_t, k_t, v, d_own, d_sib, out, *in_hbm(exps), inverse, low_t, *in_hbm(n1), raised)


def input_part(grads, d_low, down, joint, mine):
    own, other = own_half()
    rows = own if mine else other
    grad = jnp.concatenate([jnp.transpose(grad[:, rows]) for grad in grads], axis=1)
    total = dot(jnp.transpose(d_low[:, rows]), down[:16])
    return total + dot_last(grad, joint[...])


def sibling_part_kernel(dq_t, dk_t, dv_t, d_low, down, joint, out):
    out[...] = input_part((dq_t, dk_t, dv_t), d_low, down, joint, False).astype(BF)


def sibling_part(dq_t, dk_t, dv_t, d_low_t, down, joint):
    return pl.pallas_call(
        sibling_part_kernel,
        out_shape=jax.ShapeDtypeStruct((HALF, D), BF),
        in_specs=[VMEM] * 6,
        out_specs=VMEM,
        compiler_params=pltpu.CompilerParams(vmem_limit_bytes=VMEM_LIMIT),
        cost_estimate=cost(2 * HALF * D * 1664, 8e6),
    )(dq_t, dk_t, dv_t, d_low_t, down, joint)


def input_kernel(dq_t, dk_t, dv_t, d_low, down, joint, tok, d_residual, recv, vec, out):
    part = input_part((dq_t, dk_t, dv_t), d_low, down, joint, True)
    normed, inverse = normalise(tok[...].astype(F32))
    d_n1 = part + recv[...].astype(F32)
    out[...] = (d_residual[...] + norm_back(d_n1, normed, inverse, vec[0:1])).astype(BF)


def input_rows(dq_t, dk_t, dv_t, d_low_t, down, joint, tok, d_residual, recv, vec):
    def whole(rows):
        return pl.BlockSpec((rows, D), lambda i: (0, 0))

    weight = pl.BlockSpec((D, 3 * HALF), lambda i: (0, 0))
    return pl.pallas_call(
        input_kernel,
        grid=(1,),
        out_shape=jax.ShapeDtypeStruct((HALF, D), BF),
        in_specs=[whole(HALF)] * 3 + [whole(16), whole(128), weight] + [whole(HALF)] * 3 + [whole(16)],
        out_specs=whole(HALF),
        compiler_params=pltpu.CompilerParams(vmem_limit_bytes=VMEM_LIMIT),
        cost_estimate=cost(2 * HALF * D * 1664, 8e6),
    )(dq_t, dk_t, dv_t, d_low_t, down, joint, tok, d_residual, recv, vec)


PART = 256


def in_order(own, other, axis):
    first = lax.axis_index("c") == 0
    return jnp.concatenate(
        [jnp.where(first, own, other), jnp.where(first, other, own)], axis=axis
    )


def output_product(mixed, wo):
    return dot_first(mixed[:HALF], wo[0][...]) + dot_first(mixed[HALF:], wo[1][...])


def after_attention_kernel(*refs):
    own, sib, own_other, sib_other, tok, tok_sib, vec = refs[:7]
    wo_own, wo_sib = refs[7:9], refs[9:11]
    residual, n2, n2_sib = refs[11:]
    mine = pl.program_id(0) < HALF // PART
    mixed = in_order(
        jnp.where(mine, own[...], sib[...]), jnp.where(mine, own_other[...], sib_other[...]), 0
    )
    attended = in_order(output_product(mixed, wo_own), output_product(mixed, wo_sib), 1)
    rows = jnp.where(mine, tok[...], tok_sib[...]).astype(F32) + attended + vec[6:7]
    normed, _ = normalise(rows)
    normed = (normed * vec[1:2] + vec[3:4]).astype(BF)

    @pl.when(mine)
    def _():
        residual[...] = rows
        n2[...] = normed

    @pl.when(jnp.logical_not(mine))
    def _():
        n2_sib[...] = normed


def after_attention(own, sib, own_other, sib_other, tok, tok_sib, vec, wo_own, wo_sib):
    shape = jax.ShapeDtypeStruct
    parts = HALF // PART

    def mine(i):
        return jnp.minimum(i, parts - 1)

    def other(i):
        return jnp.maximum(i - parts, 0)

    weight = pl.BlockSpec((HALF, HALF), lambda i: (0, 0))
    rows = pl.BlockSpec((PART, D), lambda i: (mine(i), 0))
    rows_sib = pl.BlockSpec((PART, D), lambda i: (other(i), 0))
    columns = pl.BlockSpec((HALF, PART), lambda i: (0, mine(i)))
    columns_sib = pl.BlockSpec((HALF, PART), lambda i: (0, other(i)))
    return pl.pallas_call(
        after_attention_kernel,
        grid=(2 * parts,),
        out_shape=[shape((HALF, D), F32), shape((HALF, D), BF), shape((HALF, D), BF)],
        in_specs=[
            columns,
            columns_sib,
            columns,
            columns_sib,
            rows,
            rows_sib,
            pl.BlockSpec((16, D), lambda i: (0, 0)),
        ]
        + [weight] * 4,
        out_specs=[rows, rows, rows_sib],
        compiler_params=pltpu.CompilerParams(vmem_limit_bytes=VMEM_LIMIT),
        cost_estimate=cost(1e6, 1e5),
    )(own, sib, own_other, sib_other, tok, tok_sib, vec, *wo_own, *wo_sib)


def feed_forward_kernel(*refs):
    n2, cot, vec = refs[:3]
    a_pieces, b_pieces = refs[3:7], refs[7:11]
    out, d_n2 = refs[11:13]
    w1, w2, hidden, d_gate, sem = refs[13:]
    chunks = HID // CHUNK
    copies = []
    for j in range(chunks):
        cols = slice(j * CHUNK, (j + 1) * CHUNK)
        group, part = j // 2, j % 2
        wide = slice(group * D, (group + 1) * D)
        some = []
        for step in range(4):
            x, y = turn_of("x", step), turn_of("y", step)
            some.append((a_pieces[step].at[:, :, :, cols], w1.at[:, x, :, :, cols]))
            some.append((b_pieces[step].at[part, :, :, wide], w2.at[j, :, y]))
        copies.append(
            [pltpu.make_async_copy(s, d, sem.at[j, n]) for n, (s, d) in enumerate(some)]
        )
    for some in copies:
        start_all(some)
    c = lax.axis_index("c")
    for j in range(chunks):
        wait_all(copies[j])
        g, part = j // 2, j % 2
        bias = vec[pl.ds(8 + 2 * c + g, 1), part * CHUNK : (part + 1) * CHUNK]
        cols = slice(j * CHUNK, (j + 1) * CHUNK)
        u = dot(n2[...], w1[..., cols].reshape(D, CHUNK)) + bias
        square = u * u
        t = jnp.tanh(u * (0.7978845608028654 + 0.7978845608028654 * 0.044715 * square))
        half = 0.5 * u
        more = 1.0 + t
        hidden[:, cols] = (half * more).astype(BF)
        slope = 0.5 * more + half * (1.0 - t * t) * (
            0.7978845608028654 + 3 * 0.7978845608028654 * 0.044715 * square
        )
        d_gate[:, cols] = (dot_last(cot[...], w2[j].reshape(CHUNK, D)) * slope).astype(BF)
    d_n2[...] = dot_last(d_gate[...], w1[...].reshape(D, HID)).astype(d_n2.dtype)
    out[...] = dot(hidden[...], w2[...].reshape(HID, D)).astype(out.dtype)


def feed_forward(n2, cot, vec, a_pieces, b_pieces):
    return pl.pallas_call(
        feed_forward_kernel,
        grid=(1,),
        out_shape=[jax.ShapeDtypeStruct((HALF, D), BF)] * 2,
        in_specs=[
            pl.BlockSpec((HALF, D), lambda i: (0, 0)),
            pl.BlockSpec((HALF, D), lambda i: (1, 0)),
            pl.BlockSpec((16, D), lambda i: (0, 0)),
        ]
        + [ANY] * 8,
        out_specs=[pl.BlockSpec((HALF, D), lambda i: (0, 0))] * 2,
        scratch_shapes=[
            pltpu.VMEM((2, 4, 4, 32, HID), BF),
            pltpu.VMEM((4, 4, 4, 32, D), BF),
            pltpu.VMEM((HALF, HID), BF),
            pltpu.VMEM((HALF, HID), BF),
            pltpu.SemaphoreType.DMA((4, 8)),
        ],
        compiler_params=pltpu.CompilerParams(vmem_limit_bytes=VMEM_LIMIT),
        cost_estimate=cost(8 * HALF * D * HID, 16e6, HALF * HID),
    )(n2, cot, vec, *a_pieces, *b_pieces)


def before_attention_kernel(*refs):
    residual, cot, d_own, d_recv, vec = refs[:5]
    wo_own, wo_sib = refs[5:7], refs[7:9]
    d_residual, d_mixed_own, d_mixed_sib = refs[9:]
    normed, inverse = normalise(residual[...])
    d_n2 = d_own[...].astype(F32) + d_recv[...].astype(F32)
    d_rows = cot[...].astype(F32) + norm_back(d_n2, normed, inverse, vec[1:2])
    d_residual[...] = d_rows
    d_attended = d_rows.astype(BF)
    left, right = d_attended[:, :HALF], d_attended[:, HALF:]
    first = lax.axis_index("c") == 0
    mine, others = jnp.where(first, left, right), jnp.where(first, right, left)
    low = (dot_last(wo_own[0][...], mine) + dot_last(wo_sib[0][...], others)).astype(BF)
    high = (dot_last(wo_own[1][...], mine) + dot_last(wo_sib[1][...], others)).astype(BF)
    d_mixed_own[...] = jnp.where(first, low, high)
    d_mixed_sib[...] = jnp.where(first, high, low)


def before_attention(residual, cot, d_own, d_recv, vec, wo_own, wo_sib):
    shape = jax.ShapeDtypeStruct
    rows = pl.BlockSpec((PART, D), lambda i: (i, 0))
    later = pl.BlockSpec((PART, D), lambda i: (i + HALF // PART, 0))
    across = pl.BlockSpec((HALF, PART), lambda i: (0, i))
    weight = pl.BlockSpec((HALF, HALF), lambda i: (0, 0))
    return pl.pallas_call(
        before_attention_kernel,
        grid=(HALF // PART,),
        out_shape=[shape((HALF, D), F32), shape((HALF, HALF), BF), shape((HALF, HALF), BF)],
        in_specs=[rows, later, rows, rows, pl.BlockSpec((16, D), lambda i: (0, 0))] + [weight] * 4,
        out_specs=[rows, across, across],
        compiler_params=pltpu.CompilerParams(vmem_limit_bytes=VMEM_LIMIT),
        cost_estimate=cost(2 * HALF * D * D, 12e6),
    )(residual, cot, d_own, d_recv, vec, *wo_own, *wo_sib)


def copy_kernel(rows, out):
    out[...] = rows[...]


def copied(rows):
    return pl.pallas_call(
        copy_kernel,
        out_shape=jax.ShapeDtypeStruct(rows.shape, rows.dtype),
        in_specs=[VMEM],
        out_specs=VMEM,
        cost_estimate=cost(0, 2e6),
    )(rows)


def local(
    tokens,
    norm_gains,
    norm_shifts,
    query_value_offsets_bias,
    output_biases,
    expand_bias,
    joint_weight,
    output_weight,
    expand_weight,
    shrink_weight,
    query_down,
    query_raise_factor,
    value_down,
    value_raise_factor,
    cotangent,
):
    own, sibling = pack(
        joint_weight,
        norm_gains,
        norm_shifts,
        query_value_offsets_bias,
        output_biases,
        expand_bias,
        output_weight,
        expand_weight,
        shrink_weight,
    )
    a, b = assemble_z(ring(chip_rows(own, sibling), ZRING), (B_AT, B_FIRST + HID))
    rows = jnp.concatenate([tokens, cotangent], axis=0)
    a, b, rows = together(a, b, rows)
    a_near, b_near, rows = together(near(a, "y"), near(b, "x"), rows)
    rows = lax.ppermute(rows, PAIR, SWAP)
    a_far, b_far = ahead(a_near[0], "y"), ahead(b_near[0], "x")
    a_pieces = (a, a_near[0], a_far, a_near[1])
    b_pieces = (b, b_near[0], b_far, b_near[1])
    joint_a, joint_b = assemble_second(a_pieces, b_pieces, (0, 0), (A_FIRST, B_FIRST))
    a, b = assemble_second(a_pieces, b_pieces, (A_FIRST, B_FIRST), (HID, HID))
    a_near, b_near = near(joint_a, "x"), near(joint_b, "y")
    a_near, b_near, rows, a, b = together(a_near, b_near, rows, a, b)
    rows_sib = from_sibling(rows)
    a_far, b_far = ahead(a_near[0], "x"), ahead(b_near[0], "y")
    joint_a = (joint_a, a_near[0], a_far, a_near[1])
    joint_b = (joint_b, b_near[0], b_far, b_near[1])

    a_ahead, b_ahead = ahead(a, "x"), ahead(b, "y")
    *joint, a, b = together(*joint_a, *joint_b, a, b)
    joint_a, joint_b = joint[:4], joint[4:]

    c = lax.axis_index("c")
    down = jnp.pad(jnp.concatenate([query_down.T, value_down.T], axis=0), ((0, 120), (0, 0)))
    raise_q = lax.dynamic_slice_in_dim(query_raise_factor, c * HALF, HALF, axis=1)
    raise_v = lax.dynamic_slice_in_dim(value_raise_factor, c * HALF, HALF, axis=1)
    raised = ADAPTER_SCALE * jnp.concatenate(
        [jnp.pad(raise_q, ((0, 124), (0, 0))), jnp.pad(raise_v, ((4, 120), (0, 0)))], axis=1
    )
    raised = raised.astype(BF)

    q_t, k, k_t, v, v_t, low_t, n1, vec, joint, *wo_own = project(
        rows, rows_sib, joint_a, joint_b, down, raised
    )
    joint = joint.reshape(D, 3 * HALF)
    a_near, b_near = (a_ahead, back(a, "x")), (b_ahead, back(b, "y"))
    wo_own = [part.reshape(HALF, HALF) for part in wo_own]
    own, sib, out, exps, inverse = attend(q_t, k, k_t, v_t)
    own, sib, a_near, b_near, wo_own = together(own, sib, a_near, b_near, wo_own)
    own_other, sib_other = from_sibling(sib), from_sibling(own)
    wo_sib = [from_sibling(part) for part in wo_own]
    a_far, b_far = ahead(a_near[0], "x"), ahead(b_near[0], "y")
    a_pieces = (a, a_near[0], a_far, a_near[1])
    b_pieces = (b, b_near[0], b_far, b_near[1])
    residual, n2, n2_sib = after_attention(
        own, sib, own_other, sib_other, rows, rows_sib, vec, wo_own, wo_sib
    )
    out_own, d_own = feed_forward(n2, rows, vec, a_pieces, b_pieces)
    out_sib, d_sib = feed_forward(n2_sib, rows_sib, vec, a_pieces, b_pieces)
    d_recv = from_sibling(d_sib)
    out_recv = from_sibling(out_sib)
    d_residual, d_mixed_own, d_mixed_sib = before_attention(
        residual, rows, d_own, d_recv, vec, wo_own, wo_sib
    )
    block_rows = (residual + out_own.astype(F32) + out_recv.astype(F32) + vec[7]).astype(BF)
    d_mixed_other = from_sibling(d_mixed_sib)
    q_t, block_rows = together(q_t, block_rows)
    block_output = lax.ppermute(block_rows, PAIR, SWAP)
    sums, dq_t, dk_t, dv_t, d_low_t = attend_back(
        q_t, k_t, v, d_mixed_own, d_mixed_other, out, exps, inverse, low_t, n1, raised
    )
    dq_t, sums, block_output = together(dq_t, sums, block_output)
    sums_sib = from_sibling(sums)
    heads = (dk_t, dv_t, d_low_t, down, joint)
    part_sib = sibling_part(dq_t, *heads)
    part_sib, sums, sums_sib, dq_t = together(part_sib, sums, sums_sib, dq_t)
    part_recv = from_sibling(part_sib)
    sums = ring(sums + sums_sib, ZRING)
    grad = input_rows(dq_t, *heads, rows, d_residual, part_recv, vec)
    grad, sums = together(grad, sums)
    sums = ring(ring_sum(sums), "x")
    grad = lax.ppermute(grad, PAIR, SWAP)
    sums, block_output = together(ring_sum(sums), block_output)
    sums = ring(sums, "y")
    block_output, input_grad, sums = together(copied(block_output), grad.astype(F32), sums)
    sums = ring_sum(sums) / 64.0
    return (
        block_output,
        input_grad,
        sums[0:4].T,
        sums[8:12],
        sums[4:8].T,
        sums[12:16],
    )


def solution(mesh):
    fine = Mesh(mesh.devices.reshape(2, 4, 4, 2, 2), AXES)
    rows, columns = P(AXES, None), P(None, AXES)
    placed = (
        (rows,) + (columns,) * 4 + (P(AXES),) + (rows,) * 4 + (P(),) * 4 + (rows,)
    )
    return jax.shard_map(
        local,
        mesh=fine,
        in_specs=placed,
        out_specs=(rows, rows, P(), P(), P(), P()),
        check_vma=False,
    )
```

```python
import math

import jax
import jax.numpy as jnp
from jax import lax
from jax.experimental import pallas as pl
from jax.experimental.pallas import tpu as pltpu
from jax.sharding import Mesh, PartitionSpec as P

AXES = ("zl", "x", "y", "c", "zh")
PAIR = ("c", "zh")
ZRING = ("zl", "zh")
Z_PLACE = (0, 2, 1, 3)
SWAP = [(0, 0), (1, 2), (2, 1), (3, 3)]
FLIP = [(0, 1), (1, 0)]
FROM_NEXT = [(i, (i - 1) % 4) for i in range(4)]
FROM_PREV = [(i, (i + 1) % 4) for i in range(4)]
FROM_OPPOSITE = [(i, (i + 2) % 4) for i in range(4)]

EPS = 1e-05
ADAPTER_SCALE = 8.0
D = 1024
HALF = 512
HID = 2048
CHUNK = 512
A_FIRST = 1152
B_FIRST = 1024
B_AT = A_FIRST + HID
VMEM_LIMIT = 24 * 2**20
BF = jnp.bfloat16
F32 = jnp.float32

ANY = pl.BlockSpec(memory_space=pl.ANY)
VMEM = pl.BlockSpec(memory_space=pltpu.VMEM)


def permute(value, axis, pairs):
    if axis == ZRING:
        pairs = [(Z_PLACE[i], Z_PLACE[j]) for i, j in pairs]
    return lax.ppermute(value, axis, pairs)


def from_sibling(value):
    return lax.ppermute(value, "c", FLIP)


def ring(value, axis):
    return (
        value,
        permute(value, axis, FROM_NEXT),
        permute(value, axis, FROM_OPPOSITE),
        permute(value, axis, FROM_PREV),
    )


def parity_pairs(axis, back):
    pairs = []
    for i in range(4):
        for c in range(2):
            j = (i + (1 if (c == 0) != back else -1)) % 4
            if axis == ZRING:
                i_at, j_at = (4 * (i % 2) + 2 * c + i // 2, 4 * (j % 2) + 2 * c + j // 2)
            else:
                i_at, j_at = 2 * i + c, 2 * j + c
            pairs.append((i_at, j_at))
    return pairs


def ahead(value, axis):
    names = ("zl", "c", "zh") if axis == ZRING else (axis, "c")
    return lax.ppermute(value, names, parity_pairs(axis, False))


def back(value, axis):
    names = ("zl", "c", "zh") if axis == ZRING else (axis, "c")
    return lax.ppermute(value, names, parity_pairs(axis, True))


def near(value, axis):
    return ahead(value, axis), back(value, axis)


def ring_sum(pieces):
    own, after, opposite, before = pieces
    return (own + opposite) + (after + before)


def places():
    z = lax.axis_index("zh") * 2 + lax.axis_index("zl")
    return {"x": lax.axis_index("x"), "y": lax.axis_index("y"), "z": z}


def place_of(axis, step):
    spot = lax.rem(places()[axis] + step, 4)
    if axis == "z":
        return lax.rem(spot, 2), lax.div(spot, 2)
    return (spot,)


def turn_of(axis, step):
    way = 1 + 2 * lax.axis_index("c") if step % 2 else 1
    return lax.rem(places()[axis] + (4 - step) * way, 4)


def cost(flops, nbytes, transcendentals=0):
    return pl.CostEstimate(
        flops=int(flops), bytes_accessed=int(nbytes), transcendentals=int(transcendentals)
    )


def pack_first_kernel(
    joint, gains, shifts, offsets, biases, expand_bias, own, sibling, rows
):
    c = lax.axis_index("c")
    rows[...] = jnp.zeros_like(rows)
    for at, pair in enumerate((gains, shifts, offsets, biases)):
        rows[2 * at : 2 * at + 2, :8] = pair[...].astype(F32)
    rows[8:9, :32] = expand_bias[...].astype(F32)
    bias = rows[8:16]
    for part in range(1, 4):
        rows[8 + part : 9 + part] = pltpu.roll(bias, 128 - 8 * part, axis=1)[0:1]
    vectors = jnp.transpose(rows[...])[:8].astype(BF)
    for half, out in ((c, own), (1 - c, sibling)):
        q, k, v = [joint[:, pl.ds(pl.multiple_of(n * D + half * HALF, 128), HALF)] for n in range(3)]
        out[:, 0:512] = q
        out[:, 512:768] = k[:, 0:256]
        out[:, 768:896] = vectors
        out[:, B_AT : B_AT + 256] = k[:, 256:512]
        out[:, B_AT + 256 : B_AT + 768] = v


def pack_rest_kernel(wo, w1, w2, own, sibling, shuffled):
    c = lax.axis_index("c")
    rows = jnp.concatenate(
        [w1[:, s * 512 : (s + 1) * 512].astype(F32) for s in range(8)], axis=0
    ).astype(BF)
    lane = lax.broadcasted_iota(jnp.int32, (512, 512), 0)
    out = lax.broadcasted_iota(jnp.int32, (512, 512), 1)
    match = (lane >> 5) == ((out & 127) >> 3)
    match = match & (((lane & 31) >> 3) == (out >> 7)) & ((lane & 7) == (out & 7))
    mixed = jnp.dot(rows, jnp.where(match, 1.0, 0.0).astype(BF), preferred_element_type=F32)
    for s in range(8):
        for part in range(4):
            shuffled[part, :, s * 128 : (s + 1) * 128] = mixed[
                s * 8 : (s + 1) * 8, part * 128 : (part + 1) * 128
            ]
    for half, rest in ((c, own), (1 - c, sibling)):
        for g in range(2):
            at = A_FIRST + g * D
            rest[:, at : at + D] = shuffled[2 * half + g].astype(BF)
            at = B_AT + B_FIRST + g * D
            rest[:, at : at + D] = w2[2 * half + g]
        quarter = pl.multiple_of(half * HALF, 128)
        rest[:, 896:A_FIRST] = wo[:, pl.ds(quarter, 256)]
        rest[:, B_AT + 768 : B_AT + B_FIRST] = wo[:, pl.ds(quarter + 256, 256)]


def pack_kernel(*refs):
    first, rest = refs[:6], refs[6:9]
    own, sibling = refs[9:11]
    rows, shuffled = refs[11:]
    pack_first_kernel(*first, own, sibling, rows)
    pack_rest_kernel(*rest, own, sibling, shuffled)


def pack(joint, gains, shifts, offsets, biases, expand_bias, wo, w1, w2):
    return pl.pallas_call(
        pack_kernel,
        out_shape=[jax.ShapeDtypeStruct((8, B_AT + B_FIRST + HID), BF)] * 2,
        in_specs=[VMEM] * 9,
        out_specs=[VMEM] * 2,
        scratch_shapes=[pltpu.VMEM((128, 128), F32), pltpu.VMEM((4, 8, D), F32)],
        cost_estimate=cost(2 * 64 * 512 * 512, 700_000),
    )(joint, gains, shifts, offsets, biases, expand_bias.reshape(1, 32), wo, w1, w2.reshape(4, 8, D))


def chip_rows(own, sibling):
    return jnp.concatenate([own, from_sibling(sibling)], axis=0)


def assemble_z(pieces, widths):
    total = sum(widths)

    def kernel(*refs):
        outs, rows = refs[4:-1], refs[-1]
        c = lax.axis_index("c")
        for step in range(4):
            zl, zh = place_of("z", step)
            piece = refs[step][...].astype(F32)
            rows[zl, 2 * c + zh] = piece[0:8]
            rows[zl, 2 * (1 - c) + zh] = piece[8:16]
        for zl in range(2):
            at = 0
            for out, width in zip(outs, widths, strict=True):
                out[zl] = rows[zl, :, :, at : at + width].reshape(32, width).astype(BF)
                at += width

    return pl.pallas_call(
        kernel,
        out_shape=[pltpu.VMEM((2, 32, width), BF) for width in widths],
        in_specs=[VMEM] * 4,
        out_specs=[VMEM] * len(widths),
        scratch_shapes=[pltpu.VMEM((2, 4, 8, total), F32)],
        cost_estimate=cost(0, 4 * 64 * total),
    )(*pieces)


def assemble_second(a_pieces, b_pieces, starts, widths):
    def kernel(*refs):
        outs = refs[8:]
        for n, axis in enumerate(("y", "x")):
            cols = slice(starts[n], starts[n] + widths[n])
            for step in range(4):
                spot = turn_of(axis, step)
                for zl in range(2):
                    outs[n][zl, spot] = refs[4 * n + step][zl, :, cols]

    return pl.pallas_call(
        kernel,
        out_shape=[jax.ShapeDtypeStruct((2, 4, 32, width), BF) for width in widths],
        in_specs=[VMEM] * 8,
        out_specs=[VMEM] * 2,
        compiler_params=pltpu.CompilerParams(vmem_limit_bytes=VMEM_LIMIT),
        cost_estimate=cost(0, 4 * 256 * sum(widths)),
    )(*a_pieces, *b_pieces)


def together(*arrays):
    return lax.optimization_barrier(arrays)


def dot(left, right):
    return jnp.dot(left, right, preferred_element_type=F32)


def dot_last(left, right):
    return lax.dot_general(left, right, (((1,), (1,)), ((), ())), preferred_element_type=F32)


def dot_first(left, right):
    return lax.dot_general(left, right, (((0,), (0,)), ((), ())), preferred_element_type=F32)


def normalise(rows):
    centered = rows - jnp.mean(rows, axis=-1, keepdims=True)
    inverse = lax.rsqrt(jnp.mean(centered * centered, axis=-1, keepdims=True) + EPS)
    return centered * inverse, inverse


def norm_back(upstream, normed, inverse, gain):
    scaled = upstream * gain
    return inverse * (
        scaled
        - jnp.mean(scaled, axis=-1, keepdims=True)
        - normed * jnp.mean(scaled * normed, axis=-1, keepdims=True)
    )


def in_hbm(*arrays):
    return [pltpu.with_memory_space_constraint(a, pltpu.HBM) for a in arrays]


def start_all(copies):
    for copy in copies:
        copy.start()


def wait_all(copies):
    for copy in copies:
        copy.wait()


def own_half():
    c = lax.axis_index("c")
    own = pl.ds(pl.multiple_of(c * HALF, HALF), HALF)
    other = pl.ds(pl.multiple_of((1 - c) * HALF, HALF), HALF)
    return own, other


ROWS = 256


def joint_copies(a_pieces, b_pieces, joint, sem):
    copies = []
    for step in range(4):
        x, y = turn_of("x", step), turn_of("y", step)
        a, b = a_pieces[step].at[:, :, :, 0:768], b_pieces[step].at[:, :, :, 0:768]
        copies += [
            pltpu.make_async_copy(a, joint.at[:, x, :, :, 0:768], sem.at[step]),
            pltpu.make_async_copy(b, joint.at[:, :, y, :, 768:1536], sem.at[4 + step]),
        ]
    return copies


def project_kernel(*refs):
    tok_own, tok_sib = refs[:2]
    a_pieces, b_pieces = refs[2:6], refs[6:10]
    down, raised = refs[10:12]
    q_t, k, k_t, v, v_t, low_t, n1, vec_out, joint_out, *wo = refs[12:23]
    tok, joint, vec, sem = refs[23:]
    own, other = own_half()
    i = pl.program_id(0)
    tokens = [
        pltpu.make_async_copy(tok_own.at[0:HALF], tok.at[own], sem.at[0]),
        pltpu.make_async_copy(tok_sib.at[0:HALF], tok.at[other], sem.at[1]),
    ]
    vectors = [
        pltpu.make_async_copy(
            a_pieces[step].at[:, :, :, 768:896], vec.at[:, turn_of("x", step)], sem.at[2 + step]
        )
        for step in range(4)
    ]
    weights = joint_copies(a_pieces, b_pieces, joint, sem.at[pl.ds(6, 8)])
    outputs = []
    for step in range(4):
        x, y = turn_of("x", step), turn_of("y", step)
        for zl in range(2):
            a, b = a_pieces[step].at[zl, :, :, 896:], b_pieces[step].at[zl, :, :, 768:]
            outputs += [
                pltpu.make_async_copy(a, wo[zl].at[x, :, :, 0:256], sem.at[14 + 4 * step + zl]),
                pltpu.make_async_copy(b, wo[zl].at[:, y, :, 256:512], sem.at[16 + 4 * step + zl]),
            ]
    save = pltpu.make_async_copy(joint, joint_out, sem.at[30])

    @pl.when(i == 0)
    def _():
        start_all(vectors)
        start_all(tokens)
        start_all(weights)
        start_all(outputs)
        wait_all(vectors)
        vec_out[...] = jnp.transpose(vec[...].reshape(D, 128).astype(F32))[:16]
        wait_all(tokens)

    rows = pl.ds(pl.multiple_of(i * ROWS, ROWS), ROWS)
    normed, _ = normalise(tok[rows].astype(F32))
    normed = (normed * vec_out[0:1] + vec_out[2:3]).astype(BF)
    n1[...] = normed
    reduced = dot_last(normed, down[...]).astype(BF)
    low_t[...] = jnp.transpose(reduced)[:16]
    added = dot(reduced, raised[...])

    @pl.when(i == 0)
    def _():
        wait_all(weights)
        save.start()

    both = dot(normed, joint[...].reshape(D, 3 * HALF))
    q = (both[:, :512] + vec_out[4:5, own] + added[:, :512]).astype(BF) * 0.125
    q_t[...] = jnp.transpose(q.astype(BF))
    key = both[:, 512:1024].astype(BF)
    k[...] = key
    k_t[...] = jnp.transpose(key)
    value = (both[:, 1024:] + vec_out[5:6, own] + added[:, 512:]).astype(BF)
    v[...] = value
    v_t[...] = jnp.transpose(value)

    @pl.when(i == D // ROWS - 1)
    def _():
        wait_all(outputs)
        save.wait()


def project(tok_own, tok_sib, a_pieces, b_pieces, down, raised):
    shape = jax.ShapeDtypeStruct
    down_rows = pl.BlockSpec((ROWS, HALF), lambda i: (i, 0))
    across = pl.BlockSpec((HALF, ROWS), lambda i: (0, i))
    wide, tall = shape((HALF, D), BF), shape((D, HALF), BF)
    return pl.pallas_call(
        project_kernel,
        grid=(D // ROWS,),
        out_shape=[wide, tall, wide, tall, wide, shape((16, D), BF), pltpu.HBM((D, D), BF), shape((16, D), F32), pltpu.HBM((2, 4, 4, 32, 3 * HALF), BF)] + [shape((4, 4, 32, HALF), BF)] * 2,
        in_specs=[ANY] * 10 + [pl.BlockSpec((128, D), lambda i: (0, 0))] * 2,
        out_specs=[
            across,
            down_rows,
            across,
            down_rows,
            across,
            pl.BlockSpec((16, ROWS), lambda i: (0, i)),
            pl.BlockSpec((ROWS, D), lambda i: (i, 0)),
            pl.BlockSpec((16, D), lambda i: (0, 0)),
            ANY,
        ]
        + [pl.BlockSpec((4, 4, 32, HALF), lambda i: (0, 0, 0, 0))] * 2,
        scratch_shapes=[
            pltpu.VMEM((D, D), BF),
            pltpu.VMEM((2, 4, 4, 32, 3 * HALF), BF),
            pltpu.VMEM((2, 4, 4, 32, 128), BF),
            pltpu.SemaphoreType.DMA((31,)),
        ],
        compiler_params=pltpu.CompilerParams(vmem_limit_bytes=VMEM_LIMIT),
        cost_estimate=cost(2 * D * D * 1536, 16e6),
    )(*in_hbm(tok_own, tok_sib, *a_pieces, *b_pieces), down, raised)


def only_head(head, pair):
    zeros = jnp.zeros((64, pair.shape[1]), pair.dtype)
    part = pair[64 * head : 64 * head + 64]
    return jnp.concatenate([zeros, part] if head else [part, zeros], axis=0)


def attend_heads(q_t, k, k_t, v_t, out, exps, inverse, exact):
    first, second = slice(0, HALF), slice(HALF, D)
    low, high = slice(0, 256), slice(256, HALF)
    causal = lax.broadcasted_iota(jnp.int32, (256, HALF), 0) <= lax.broadcasted_iota(
        jnp.int32, (256, HALF), 1
    )
    most = jnp.full((1, 1), -1e30, F32)

    def by_column(reduce, join, top, bottom):
        over = reduce(top, axis=0, keepdims=True)
        under = reduce(bottom, axis=0, keepdims=True)
        return jnp.concatenate([over[:, low], join(over[:, high], under)], axis=1)

    for head in range(2):
        dims = slice(64 * head, 64 * head + 64)
        q_head = only_head(head, q_t[...])
        level = jnp.sum(q_t[dims].astype(F32) * k_t[dims].astype(F32), axis=0, keepdims=True)
        level_one, level_two = level[:, first], level[:, second]
        blocks = []
        for at in (0, HALF):
            top = dot(k[at : at + 256], q_head[:, at : at + HALF])
            bottom = dot(k[at + 256 : at + HALF], q_head[:, at + 256 : at + HALF])
            blocks.append(
                (jnp.where(causal, top, -1e30), jnp.where(causal[:, low], bottom, -1e30))
            )
        one, three = blocks
        two = dot(k[first], q_head[:, second])
        if exact:
            level_one = by_column(jnp.max, jnp.maximum, *one)
            level_two = by_column(jnp.max, jnp.maximum, *three)
            level_two = jnp.maximum(level_two, jnp.max(two, axis=0, keepdims=True))
        parts = [
            (0, low, slice(0, HALF), one[0] - level_one),
            (0, high, high, one[1] - level_one[:, high]),
            (1, slice(0, HALF), slice(0, HALF), two - level_two),
            (2, low, slice(0, HALF), three[0] - level_two),
            (2, high, high, three[1] - level_two[:, high]),
        ]
        rounded = []
        for n, rows, cols, part in parts:
            peak = jnp.max(jnp.max(part, axis=0, keepdims=True), axis=1, keepdims=True)
            most = jnp.maximum(most, peak)
            part = jnp.exp(part).astype(BF)
            exps[head, n, rows, cols] = part
            rounded.append(part.astype(F32))
        scale_one = 1.0 / by_column(jnp.sum, jnp.add, *rounded[:2])
        total = by_column(jnp.sum, jnp.add, *rounded[3:])
        scale_two = 1.0 / (total + jnp.sum(rounded[2], axis=0, keepdims=True))
        inverse[0, head : head + 1, first] = scale_one
        inverse[0, head : head + 1, second] = scale_two
        value = v_t[dims]
        out[dims, 0:256] = dot(value[:, 0:256], exps[head, 0, low, low]) * scale_one[:, low]
        out[dims, 256:512] = dot(value[:, first], exps[head, 0, :, high]) * scale_one[:, high]
        total = dot(value[:, first], exps[head, 1])
        left = total[:, low] + dot(value[:, 512:768], exps[head, 2, low, low])
        right = total[:, high] + dot(value[:, second], exps[head, 2, :, high])
        out[dims, 512:768] = left * scale_two[:, low]
        out[dims, 768:1024] = right * scale_two[:, high]
    return jnp.max(most)


def attend_kernel(q_t, k, k_t, v_t, mixed_own, mixed_sib, out, exps, inverse):
    args = (q_t, k, k_t, v_t, out, exps, inverse)
    most = attend_heads(*args, False)

    @pl.when(most > 60.0)
    def _():
        attend_heads(*args, True)

    own, other = own_half()
    mixed_own[...] = out[:, own].astype(BF)
    mixed_sib[...] = out[:, other].astype(BF)


def attend(q_t, k, k_t, v_t):
    shape = jax.ShapeDtypeStruct
    halves = pl.BlockSpec((128, HALF), lambda j: (j, 0))
    wide = pl.BlockSpec((128, D), lambda j: (j, 0))
    return pl.pallas_call(
        attend_kernel,
        grid=(4,),
        out_shape=[
            shape((HALF, HALF), BF),
            shape((HALF, HALF), BF),
            shape((HALF, D), F32),
            pltpu.HBM((8, 3, HALF, HALF), BF),
            shape((4, 8, D), F32),
        ],
        in_specs=[wide, pl.BlockSpec((D, 128), lambda j: (0, j)), wide, wide],
        out_specs=[
            halves,
            halves,
            wide,
            pl.BlockSpec((2, 3, HALF, HALF), lambda j: (j, 0, 0, 0)),
            pl.BlockSpec((1, 8, D), lambda j: (j, 0, 0)),
        ],
        compiler_params=pltpu.CompilerParams(vmem_limit_bytes=VMEM_LIMIT),
        cost_estimate=cost(8e9, 20e6, 8 * D * D),
    )(q_t, k, k_t, v_t)


def attend_back_kernel(*refs):
    q_t, k_t, v, d_own, d_sib, out, exps, inverse, low_t, n1_in, raised = refs[:11]
    sums, dq_t, dk_t, dv_t, d_low_out = refs[11:16]
    d_scores, d_low, n1, sem = refs[16:]
    copy = pltpu.make_async_copy(n1_in, n1, sem)

    c = lax.axis_index("c")
    own, other = own_half()
    step = pl.program_id(0)

    @pl.when(step == 0)
    def _():
        copy.start()

    low, high = jnp.where(c == 0, d_own[...], d_sib[...]), jnp.where(c == 0, d_sib[...], d_own[...])
    d_out = jnp.concatenate([low, high], axis=1).astype(F32)
    first, second = slice(0, HALF), slice(HALF, D)
    for head in range(2):
        dims = slice(64 * head, 64 * head + 64)
        scale = inverse[0, head : head + 1]
        scaled = (d_out * scale).astype(BF)
        mean = jnp.sum(scaled[dims].astype(F32) * out[dims], axis=0, keepdims=True)
        d_head = only_head(head, scaled)
        low, high = slice(0, 256), slice(256, HALF)
        for n, keys, cols in ((0, 0, 0), (1, 0, HALF), (2, HALF, HALF)):
            for rows, part in ((low, slice(0, HALF)), (high, slice(0 if n == 1 else 256, HALF))):
                at = slice(cols + part.start, cols + part.stop)
                d_probs = dot(v[keys + rows.start : keys + rows.stop], d_head[:, at])
                ds = exps[head, n, rows, part].astype(F32) * (d_probs - mean[:, at])
                d_scores[n, rows, part] = ds.astype(BF)
        key, query, d_value = k_t[dims], q_t[dims], scaled[dims]
        dq_t[dims, 0:256] = (dot(key[:, 0:256], d_scores[0, low, low]) * 0.125).astype(BF)
        dq_t[dims, 256:512] = (dot(key[:, 0:512], d_scores[0, :, high]) * 0.125).astype(BF)
        total = dot(key[:, first], d_scores[1])
        one = total[:, low] + dot(key[:, 512:768], d_scores[2, low, low])
        two = total[:, high] + dot(key[:, second], d_scores[2, :, high])
        dq_t[dims, 512:768] = (one * 0.125).astype(BF)
        dq_t[dims, 768:1024] = (two * 0.125).astype(BF)
        for grad, left, right in (
            (dk_t, query, d_scores),
            (dv_t, d_value, exps.at[head]),
        ):
            total = dot_last(left[:, second], right[1])
            one = total[:, low] + dot_last(left[:, first], right[0, low])
            two = total[:, high] + dot_last(left[:, 256:512], right[0, high, high])
            grad[dims, 0:256] = one.astype(BF)
            grad[dims, 256:512] = two.astype(BF)
            grad[dims, 512:768] = dot_last(left[:, second], right[2, low]).astype(BF)
            grad[dims, 768:1024] = dot_last(left[:, 768:1024], right[2, high, high]).astype(BF)
    cols = pl.ds(pl.multiple_of(step * 128, 128), 128)
    value_cols = pl.ds(pl.multiple_of(HALF + step * 128, 128), 128)
    part = dot(raised[:16, cols], dq_t[...]) + dot(raised[:16, value_cols], dv_t[...])
    at = pl.ds(pl.multiple_of(c * HALF + step * 128, 128), 128)
    top = lax.broadcasted_iota(jnp.int32, (8, 128), 0) < 4
    from_q = dot_last(low_t[...], dq_t[...])[:8] * ADAPTER_SCALE
    from_v = dot_last(low_t[...], dv_t[...])[:8] * ADAPTER_SCALE

    @pl.when(step == 0)
    def _():
        d_low[...] = part
        sums[8:16] = jnp.zeros((8, D), F32)

    @pl.when(step > 0)
    def _():
        d_low[...] += part

    sums[8:16, at] = jnp.where(top, from_q, from_v)

    @pl.when(step == 3)
    def _():
        copy.wait()
        low = d_low[...].astype(BF)
        d_low_out[...] = low
        sums[0:8] = dot(low, n1[...])[:8]


def attend_back(q_t, k_t, v, d_own, d_sib, out, exps, inverse, low_t, n1, raised):
    shape = jax.ShapeDtypeStruct
    wide = pl.BlockSpec((128, D), lambda j: (j, 0))
    halves = pl.BlockSpec((128, HALF), lambda j: (j, 0))
    whole = pl.BlockSpec((16, D), lambda j: (0, 0))
    return pl.pallas_call(
        attend_back_kernel,
        grid=(4,),
        out_shape=[shape((16, D), F32)] + [shape((HALF, D), BF)] * 3 + [shape((16, D), BF)],
        in_specs=[
            wide,
            wide,
            pl.BlockSpec((D, 128), lambda j: (0, j)),
            halves,
            halves,
            wide,
            pl.BlockSpec((2, 3, HALF, HALF), lambda j: (j, 0, 0, 0)),
            pl.BlockSpec((1, 8, D), lambda j: (j, 0, 0)),
            whole,
            ANY,
            pl.BlockSpec((128, D), lambda j: (0, 0)),
        ],
        out_specs=[whole, wide, wide, wide, whole],
        scratch_shapes=[
            pltpu.VMEM((3, HALF, HALF), BF),
            pltpu.VMEM((16, D), F32),
            pltpu.VMEM((D, D), BF),
            pltpu.SemaphoreType.DMA,
        ],
        compiler_params=pltpu.CompilerParams(vmem_limit_bytes=VMEM_LIMIT),
        cost_estimate=cost(16e9, 30e6),
    )(q_t, k_t, v, d_own, d_sib, out, *in_hbm(exps), inverse, low_t, *in_hbm(n1), raised)


def input_part(grads, d_low, down, joint, mine):
    own, other = own_half()
    rows = own if mine else other
    grad = jnp.concatenate([jnp.transpose(grad[:, rows]) for grad in grads], axis=1)
    total = dot(jnp.transpose(d_low[:, rows]), down[:16])
    return total + dot_last(grad, joint[...])


def sibling_part_kernel(dq_t, dk_t, dv_t, d_low, down, joint, out):
    out[...] = input_part((dq_t, dk_t, dv_t), d_low, down, joint, False).astype(BF)


def sibling_part(dq_t, dk_t, dv_t, d_low_t, down, joint):
    return pl.pallas_call(
        sibling_part_kernel,
        out_shape=jax.ShapeDtypeStruct((HALF, D), BF),
        in_specs=[VMEM] * 6,
        out_specs=VMEM,
        compiler_params=pltpu.CompilerParams(vmem_limit_bytes=VMEM_LIMIT),
        cost_estimate=cost(2 * HALF * D * 1664, 8e6),
    )(dq_t, dk_t, dv_t, d_low_t, down, joint)


def input_kernel(dq_t, dk_t, dv_t, d_low, down, joint, tok, d_residual, recv, vec, out):
    part = input_part((dq_t, dk_t, dv_t), d_low, down, joint, True)
    normed, inverse = normalise(tok[...].astype(F32))
    d_n1 = part + recv[...].astype(F32)
    out[...] = (d_residual[...] + norm_back(d_n1, normed, inverse, vec[0:1])).astype(BF)


def input_rows(dq_t, dk_t, dv_t, d_low_t, down, joint, tok, d_residual, recv, vec):
    def whole(rows):
        return pl.BlockSpec((rows, D), lambda i: (0, 0))

    weight = pl.BlockSpec((D, 3 * HALF), lambda i: (0, 0))
    return pl.pallas_call(
        input_kernel,
        grid=(1,),
        out_shape=jax.ShapeDtypeStruct((HALF, D), BF),
        in_specs=[whole(HALF)] * 3 + [whole(16), whole(128), weight] + [whole(HALF)] * 3 + [whole(16)],
        out_specs=whole(HALF),
        compiler_params=pltpu.CompilerParams(vmem_limit_bytes=VMEM_LIMIT),
        cost_estimate=cost(2 * HALF * D * 1664, 8e6),
    )(dq_t, dk_t, dv_t, d_low_t, down, joint, tok, d_residual, recv, vec)


PART = 256


def in_order(own, other, axis):
    first = lax.axis_index("c") == 0
    return jnp.concatenate(
        [jnp.where(first, own, other), jnp.where(first, other, own)], axis=axis
    )


def output_product(mixed, wo):
    return dot_first(mixed[:HALF], wo[0][...]) + dot_first(mixed[HALF:], wo[1][...])


def after_attention_kernel(*refs):
    own, sib, own_other, sib_other, tok, tok_sib, vec = refs[:7]
    wo_own, wo_sib = refs[7:9], refs[9:11]
    residual, n2, n2_sib = refs[11:]
    mine = pl.program_id(0) < HALF // PART
    mixed = in_order(
        jnp.where(mine, own[...], sib[...]), jnp.where(mine, own_other[...], sib_other[...]), 0
    )
    attended = in_order(output_product(mixed, wo_own), output_product(mixed, wo_sib), 1)
    rows = jnp.where(mine, tok[...], tok_sib[...]).astype(F32) + attended + vec[6:7]
    normed, _ = normalise(rows)
    normed = (normed * vec[1:2] + vec[3:4]).astype(BF)

    @pl.when(mine)
    def _():
        residual[...] = rows
        n2[...] = normed

    @pl.when(jnp.logical_not(mine))
    def _():
        n2_sib[...] = normed


def after_attention(own, sib, own_other, sib_other, tok, tok_sib, vec, wo_own, wo_sib):
    shape = jax.ShapeDtypeStruct
    parts = HALF // PART

    def mine(i):
        return jnp.minimum(i, parts - 1)

    def other(i):
        return jnp.maximum(i - parts, 0)

    weight = pl.BlockSpec((HALF, HALF), lambda i: (0, 0))
    rows = pl.BlockSpec((PART, D), lambda i: (mine(i), 0))
    rows_sib = pl.BlockSpec((PART, D), lambda i: (other(i), 0))
    columns = pl.BlockSpec((HALF, PART), lambda i: (0, mine(i)))
    columns_sib = pl.BlockSpec((HALF, PART), lambda i: (0, other(i)))
    return pl.pallas_call(
        after_attention_kernel,
        grid=(2 * parts,),
        out_shape=[shape((HALF, D), F32), shape((HALF, D), BF), shape((HALF, D), BF)],
        in_specs=[
            columns,
            columns_sib,
            columns,
            columns_sib,
            rows,
            rows_sib,
            pl.BlockSpec((16, D), lambda i: (0, 0)),
        ]
        + [weight] * 4,
        out_specs=[rows, rows, rows_sib],
        compiler_params=pltpu.CompilerParams(vmem_limit_bytes=VMEM_LIMIT),
        cost_estimate=cost(1e6, 1e5),
    )(own, sib, own_other, sib_other, tok, tok_sib, vec, *wo_own, *wo_sib)


def feed_forward_kernel(*refs):
    n2, cot, vec = refs[:3]
    a_pieces, b_pieces = refs[3:7], refs[7:11]
    out, d_n2 = refs[11:13]
    w1, w2, hidden, d_gate, sem = refs[13:]
    chunks = HID // CHUNK
    copies = []
    for j in range(chunks):
        cols = slice(j * CHUNK, (j + 1) * CHUNK)
        group, part = j // 2, j % 2
        wide = slice(group * D, (group + 1) * D)
        some = []
        for step in range(4):
            x, y = turn_of("x", step), turn_of("y", step)
            some.append((a_pieces[step].at[:, :, :, cols], w1.at[:, x, :, :, cols]))
            some.append((b_pieces[step].at[part, :, :, wide], w2.at[j, :, y]))
        copies.append(
            [pltpu.make_async_copy(s, d, sem.at[j, n]) for n, (s, d) in enumerate(some)]
        )
    for some in copies:
        start_all(some)
    c = lax.axis_index("c")
    for j in range(chunks):
        wait_all(copies[j])
        g, part = j // 2, j % 2
        bias = vec[pl.ds(8 + 2 * c + g, 1), part * CHUNK : (part + 1) * CHUNK]
        cols = slice(j * CHUNK, (j + 1) * CHUNK)
        u = dot(n2[...], w1[..., cols].reshape(D, CHUNK)) + bias
        square = u * u
        t = jnp.tanh(u * (0.7978845608028654 + 0.7978845608028654 * 0.044715 * square))
        half = 0.5 * u
        more = 1.0 + t
        hidden[:, cols] = (half * more).astype(BF)
        slope = 0.5 * more + half * (1.0 - t * t) * (
            0.7978845608028654 + 3 * 0.7978845608028654 * 0.044715 * square
        )
        d_gate[:, cols] = (dot_last(cot[...], w2[j].reshape(CHUNK, D)) * slope).astype(BF)
    d_n2[...] = dot_last(d_gate[...], w1[...].reshape(D, HID)).astype(d_n2.dtype)
    out[...] = dot(hidden[...], w2[...].reshape(HID, D)).astype(out.dtype)


def feed_forward(n2, cot, vec, a_pieces, b_pieces):
    return pl.pallas_call(
        feed_forward_kernel,
        grid=(1,),
        out_shape=[jax.ShapeDtypeStruct((HALF, D), BF)] * 2,
        in_specs=[
            pl.BlockSpec((HALF, D), lambda i: (0, 0)),
            pl.BlockSpec((HALF, D), lambda i: (1, 0)),
            pl.BlockSpec((16, D), lambda i: (0, 0)),
        ]
        + [ANY] * 8,
        out_specs=[pl.BlockSpec((HALF, D), lambda i: (0, 0))] * 2,
        scratch_shapes=[
            pltpu.VMEM((2, 4, 4, 32, HID), BF),
            pltpu.VMEM((4, 4, 4, 32, D), BF),
            pltpu.VMEM((HALF, HID), BF),
            pltpu.VMEM((HALF, HID), BF),
            pltpu.SemaphoreType.DMA((4, 8)),
        ],
        compiler_params=pltpu.CompilerParams(vmem_limit_bytes=VMEM_LIMIT),
        cost_estimate=cost(8 * HALF * D * HID, 16e6, HALF * HID),
    )(n2, cot, vec, *a_pieces, *b_pieces)


def before_attention_kernel(*refs):
    residual, cot, d_own, d_recv, vec = refs[:5]
    wo_own, wo_sib = refs[5:7], refs[7:9]
    d_residual, d_mixed_own, d_mixed_sib = refs[9:]
    normed, inverse = normalise(residual[...])
    d_n2 = d_own[...].astype(F32) + d_recv[...].astype(F32)
    d_rows = cot[...].astype(F32) + norm_back(d_n2, normed, inverse, vec[1:2])
    d_residual[...] = d_rows
    d_attended = d_rows.astype(BF)
    left, right = d_attended[:, :HALF], d_attended[:, HALF:]
    first = lax.axis_index("c") == 0
    mine, others = jnp.where(first, left, right), jnp.where(first, right, left)
    low = (dot_last(wo_own[0][...], mine) + dot_last(wo_sib[0][...], others)).astype(BF)
    high = (dot_last(wo_own[1][...], mine) + dot_last(wo_sib[1][...], others)).astype(BF)
    d_mixed_own[...] = jnp.where(first, low, high)
    d_mixed_sib[...] = jnp.where(first, high, low)


def before_attention(residual, cot, d_own, d_recv, vec, wo_own, wo_sib):
    shape = jax.ShapeDtypeStruct
    rows = pl.BlockSpec((PART, D), lambda i: (i, 0))
    later = pl.BlockSpec((PART, D), lambda i: (i + HALF // PART, 0))
    across = pl.BlockSpec((HALF, PART), lambda i: (0, i))
    weight = pl.BlockSpec((HALF, HALF), lambda i: (0, 0))
    return pl.pallas_call(
        before_attention_kernel,
        grid=(HALF // PART,),
        out_shape=[shape((HALF, D), F32), shape((HALF, HALF), BF), shape((HALF, HALF), BF)],
        in_specs=[rows, later, rows, rows, pl.BlockSpec((16, D), lambda i: (0, 0))] + [weight] * 4,
        out_specs=[rows, across, across],
        compiler_params=pltpu.CompilerParams(vmem_limit_bytes=VMEM_LIMIT),
        cost_estimate=cost(2 * HALF * D * D, 12e6),
    )(residual, cot, d_own, d_recv, vec, *wo_own, *wo_sib)


def copy_kernel(rows, out):
    out[...] = rows[...]


def copied(rows):
    return pl.pallas_call(
        copy_kernel,
        out_shape=jax.ShapeDtypeStruct(rows.shape, rows.dtype),
        in_specs=[VMEM],
        out_specs=VMEM,
        cost_estimate=cost(0, 2e6),
    )(rows)


def local(
    tokens,
    norm_gains,
    norm_shifts,
    query_value_offsets_bias,
    output_biases,
    expand_bias,
    joint_weight,
    output_weight,
    expand_weight,
    shrink_weight,
    query_down,
    query_raise_factor,
    value_down,
    value_raise_factor,
    cotangent,
):
    own, sibling = pack(
        joint_weight,
        norm_gains,
        norm_shifts,
        query_value_offsets_bias,
        output_biases,
        expand_bias,
        output_weight,
        expand_weight,
        shrink_weight,
    )
    a, b = assemble_z(ring(chip_rows(own, sibling), ZRING), (B_AT, B_FIRST + HID))
    rows = jnp.concatenate([tokens, cotangent], axis=0)
    a, b, rows = together(a, b, rows)
    a_near, b_near, rows = together(near(a, "y"), near(b, "x"), rows)
    rows = lax.ppermute(rows, PAIR, SWAP)
    a_far, b_far = ahead(a_near[0], "y"), ahead(b_near[0], "x")
    a_pieces = (a, a_near[0], a_far, a_near[1])
    b_pieces = (b, b_near[0], b_far, b_near[1])
    joint_a, joint_b = assemble_second(a_pieces, b_pieces, (0, 0), (A_FIRST, B_FIRST))
    a, b = assemble_second(a_pieces, b_pieces, (A_FIRST, B_FIRST), (HID, HID))
    a_near, b_near = near(joint_a, "x"), near(joint_b, "y")
    a_near, b_near, rows, a, b = together(a_near, b_near, rows, a, b)
    rows_sib = from_sibling(rows)
    a_far, b_far = ahead(a_near[0], "x"), ahead(b_near[0], "y")
    joint_a = (joint_a, a_near[0], a_far, a_near[1])
    joint_b = (joint_b, b_near[0], b_far, b_near[1])

    a_ahead, b_ahead = ahead(a, "x"), ahead(b, "y")
    *joint, a, b = together(*joint_a, *joint_b, a, b)
    joint_a, joint_b = joint[:4], joint[4:]

    c = lax.axis_index("c")
    down = jnp.pad(jnp.concatenate([query_down.T, value_down.T], axis=0), ((0, 120), (0, 0)))
    raise_q = lax.dynamic_slice_in_dim(query_raise_factor, c * HALF, HALF, axis=1)
    raise_v = lax.dynamic_slice_in_dim(value_raise_factor, c * HALF, HALF, axis=1)
    raised = ADAPTER_SCALE * jnp.concatenate(
        [jnp.pad(raise_q, ((0, 124), (0, 0))), jnp.pad(raise_v, ((4, 120), (0, 0)))], axis=1
    )
    raised = raised.astype(BF)

    q_t, k, k_t, v, v_t, low_t, n1, vec, joint, *wo_own = project(
        rows, rows_sib, joint_a, joint_b, down, raised
    )
    joint = joint.reshape(D, 3 * HALF)
    a_near, b_near = (a_ahead, back(a, "x")), (b_ahead, back(b, "y"))
    wo_own = [part.reshape(HALF, HALF) for part in wo_own]
    own, sib, out, exps, inverse = attend(q_t, k, k_t, v_t)
    own, sib, a_near, b_near, wo_own = together(own, sib, a_near, b_near, wo_own)
    own_other, sib_other = from_sibling(sib), from_sibling(own)
    wo_sib = [from_sibling(part) for part in wo_own]
    a_far, b_far = ahead(a_near[0], "x"), ahead(b_near[0], "y")
    a_pieces = (a, a_near[0], a_far, a_near[1])
    b_pieces = (b, b_near[0], b_far, b_near[1])
    residual, n2, n2_sib = after_attention(
        own, sib, own_other, sib_other, rows, rows_sib, vec, wo_own, wo_sib
    )
    out_own, d_own = feed_forward(n2, rows, vec, a_pieces, b_pieces)
    out_sib, d_sib = feed_forward(n2_sib, rows_sib, vec, a_pieces, b_pieces)
    d_recv = from_sibling(d_sib)
    out_recv = from_sibling(out_sib)
    d_residual, d_mixed_own, d_mixed_sib = before_attention(
        residual, rows, d_own, d_recv, vec, wo_own, wo_sib
    )
    block_rows = (residual + out_own.astype(F32) + out_recv.astype(F32) + vec[7]).astype(BF)
    d_mixed_other = from_sibling(d_mixed_sib)
    q_t, block_rows = together(q_t, block_rows)
    block_output = lax.ppermute(block_rows, PAIR, SWAP)
    sums, dq_t, dk_t, dv_t, d_low_t = attend_back(
        q_t, k_t, v, d_mixed_own, d_mixed_other, out, exps, inverse, low_t, n1, raised
    )
    dq_t, sums, block_output = together(dq_t, sums, block_output)
    sums_sib = from_sibling(sums)
    heads = (dk_t, dv_t, d_low_t, down, joint)
    part_sib = sibling_part(dq_t, *heads)
    part_sib, sums, sums_sib, dq_t = together(part_sib, sums, sums_sib, dq_t)
    part_recv = from_sibling(part_sib)
    sums = ring(sums + sums_sib, ZRING)
    grad = input_rows(dq_t, *heads, rows, d_residual, part_recv, vec)
    grad, sums = together(grad, sums)
    sums = ring(ring_sum(sums), "x")
    grad = lax.ppermute(grad, PAIR, SWAP)
    sums, block_output = together(ring_sum(sums), block_output)
    sums = ring(sums, "y")
    block_output, input_grad, sums = together(copied(block_output), grad.astype(F32), sums)
    sums = ring_sum(sums) / 64.0
    return (
        block_output,
        input_grad,
        sums[0:4].T,
        sums[8:12],
        sums[4:8].T,
        sums[12:16],
    )


def solution(mesh):
    fine = Mesh(mesh.devices.reshape(2, 4, 4, 2, 2), AXES)
    rows, columns = P(AXES, None), P(None, AXES)
    placed = (
        (rows,) + (columns,) * 4 + (P(AXES),) + (rows,) * 4 + (P(),) * 4 + (rows,)
    )
    return jax.shard_map(
        local,
        mesh=fine,
        in_specs=placed,
        out_specs=(rows, rows, P(), P(), P(), P()),
        check_vma=False,
    )
```
